32 devices in a mesh: dates: 2 (over x), cols: 16 (over z, y, core).
Axes of the slice: x: 2, y: 2, z: 4, core: 2. Of those that a mesh axis runs over, the one named last changes fastest.
Arguments:
- complex_images: bfloat16 [296, 32, 2, 8192], P('dates', None, None, 'cols'), may hold values from -4 to 4
- pair_list: int32 [1480, 2], replicated, may hold values from 0 to 295, as said below
Outputs:
- refined_series: float32 [296, 16, 2, 2048], P(None, 'dates', None, 'cols')
The draws below stay inside these ranges and needn't reach their ends.
Inputs may be any that keep to these rules, and one draw needn't show every extreme that they name: `pair_list`: each row holds a reference date and a later secondary date at most 12 dates after it; some pair starts at date 0 and some ends at date 296 - 1.
All inputs are finite; a program needn't handle non-finite values.
Results may differ from the reference program's by a relative error of at most 0.0045.
Values may be sent and summed in bfloat16 or wider, within the bound.
No kernel may reach another device: no remote copies, remote signals or barrier semaphores. Data moves between devices by JAX's collectives and lax.ppermute only.
A program may use at most 128 MiB of HBM per device.

```python
import math
import jax
import jax.numpy as jnp
from jax import lax

NDATE = 296
NPAIR = 1480
ROWS = 32
LOOKR = 2
LOOKC = 4
GAP = 12
PAIR_BLOCK = 37
NCOLS = 8192
MLROWS = 16
MLCOLS = 2048


def draw_complex_images(key, part):
    key = jax.random.fold_in(key, 7)
    subkeys = jax.random.split(key, 6)
    row_coord = (2.0 * jnp.arange(ROWS, dtype=jnp.float32) + 1.0) / ROWS - 1.0
    col_coord = (2.0 * jnp.arange(NCOLS, dtype=jnp.float32) + 1.0) / NCOLS - 1.0
    slope_rows = jax.random.normal(subkeys[0], (NDATE, 1, 1), jnp.float32) * 1.5
    slope_cols = jax.random.normal(subkeys[1], (NDATE, 1, 1), jnp.float32) * 2.0
    offsets = jax.random.uniform(subkeys[2], (NDATE, 1, 1), jnp.float32, -math.pi, math.pi)
    scatter = jax.random.uniform(subkeys[3], (1, ROWS, NCOLS), jnp.float32, -math.pi, math.pi)
    noise = jax.random.normal(subkeys[4], (NDATE, ROWS, NCOLS), jnp.float32) * 0.5
    level = jax.random.uniform(subkeys[5], (1, ROWS, NCOLS), jnp.float32)
    amplitude = jnp.exp(level * 0.5 * math.log(10.0)) * jnp.sqrt((2.0 + col_coord[None, None, :]) / 3.0)
    phase = scatter + offsets + slope_rows * row_coord[None, :, None] + slope_cols * col_coord[None, None, :] + noise
    return jnp.stack([amplitude * jnp.cos(phase), amplitude * jnp.sin(phase)], axis=2).astype(jnp.bfloat16)


def draw_pair_list(key, part):
    key = jax.random.fold_in(key, 13)
    first_key, second_key = jax.random.split(key)
    reference_date = jax.random.randint(first_key, (NPAIR,), 0, NDATE - 1, jnp.int32)
    spacing = jax.random.randint(second_key, (NPAIR,), 1, GAP + 1, jnp.int32)
    secondary = jnp.minimum(reference_date + spacing, NDATE - 1)
    reference_date = reference_date.at[0].set(0)
    secondary = secondary.at[0].set(jnp.minimum(spacing[0], NDATE - 1))
    reference_date = reference_date.at[NPAIR - 1].set(NDATE - 2)
    secondary = secondary.at[NPAIR - 1].set(NDATE - 1)
    return jnp.stack([reference_date, secondary], axis=1).astype(jnp.int32)


def setup_inputs(seed: int = 0) -> dict:
    seeds = jax.random.split(jax.random.key(seed), 3)
    complex_images = draw_complex_images(jax.random.fold_in(seeds[2], 71), 0)
    pair_list = draw_pair_list(jax.random.fold_in(seeds[2], 71), 0)
    return {"complex_images": complex_images, "pair_list": pair_list}


ridge = 0.5
highest = lax.Precision.HIGHEST

def pseudo_inverse(pair_list, count):
    date_ids = jnp.arange(count, dtype=jnp.int32)
    design = (pair_list[:, 0:1] == date_ids[None, :]).astype(jnp.float32) - (pair_list[:, 1:2] == date_ids[None, :]).astype(jnp.float32)
    normal = jnp.dot(design.T, design, precision=highest) + ridge * jnp.eye(count, dtype=jnp.float32)
    factor = jnp.linalg.cholesky(normal)
    return jax.scipy.linalg.cho_solve((factor, True), design.T)

def interfere(first, second):
    first = first.astype(jnp.float32)
    second = second.astype(jnp.float32)
    real_part = first[:, :, 0] * second[:, :, 0] + first[:, :, 1] * second[:, :, 1]
    imag_part = first[:, :, 1] * second[:, :, 0] - first[:, :, 0] * second[:, :, 1]
    product = jnp.stack([real_part, imag_part], axis=2)
    grouped = product.reshape(product.shape[0], product.shape[1] // LOOKR, LOOKR, 2, product.shape[3] // LOOKC, LOOKC)
    return (jnp.sum(grouped, axis=(2, 5)) / float(LOOKR * LOOKC)).astype(jnp.bfloat16)

def multilook_pairs(tile_stack, pair_list, pair_block):
    groups = pair_list.reshape(-1, pair_block, 2)

    def one_group(group):
        return interfere(tile_stack[group[:, 0]], tile_stack[group[:, 1]])
    looked = lax.map(one_group, groups)
    return looked.reshape((pair_list.shape[0],) + looked.shape[2:])

def coordinates(start, count, total):
    return (2.0 * (start + jnp.arange(count, dtype=jnp.int32)).astype(jnp.float32) + 1.0) / float(total) - 1.0

def basis_planes(row_coord, col_coord):
    constant = jnp.ones((row_coord.shape[0], col_coord.shape[0]), jnp.float32)
    return jnp.stack([constant, row_coord[:, None] * constant, col_coord[None, :] * constant])

def weighted(interferograms, planes, pair_count):
    widened = interferograms.astype(jnp.float32)
    weights = jnp.sum(widened * widened, axis=(0, 2)) / float(pair_count)
    weighted_planes = planes * weights[None]
    normal = jnp.einsum('jrc,krc->jk', weighted_planes, planes, precision=highest)
    return (weighted_planes, normal)

def inverse3(matrix):

    def cyclic(row_at, col_at):
        return matrix[(row_at + 1) % 3, (col_at + 1) % 3] * matrix[(row_at + 2) % 3, (col_at + 2) % 3] - matrix[(row_at + 1) % 3, (col_at + 2) % 3] * matrix[(row_at + 2) % 3, (col_at + 1) % 3]
    cofacts = jnp.stack([jnp.stack([cyclic(row_at, col_at) for col_at in range(3)]) for row_at in range(3)])
    determinant = jnp.sum(matrix[0] * cofacts[0])
    return cofacts.T / determinant

def refine(series, ramp_rhs, normal, planes):
    ramp_coef = jnp.einsum('jk,dkh->djh', inverse3(normal), ramp_rhs, precision=highest)
    return series - jnp.einsum('djh,jrc->drhc', ramp_coef, planes, precision=highest)

def reference(complex_images, pair_list):
    rounded_pseudo = pseudo_inverse(pair_list, NDATE).astype(jnp.bfloat16)
    interferograms = multilook_pairs(complex_images, pair_list, PAIR_BLOCK)
    series = jnp.dot(rounded_pseudo.astype(jnp.float32), interferograms.reshape(NPAIR, -1).astype(jnp.float32), preferred_element_type=jnp.float32).reshape((NDATE,) + interferograms.shape[1:])
    planes = basis_planes(coordinates(0, MLROWS, MLROWS), coordinates(0, MLCOLS, MLCOLS))
    weighted_planes, normal = weighted(interferograms, planes, NPAIR)
    ramp_rhs = jnp.einsum('jrc,drhc->djh', weighted_planes, series, precision=highest)
    return refine(series, ramp_rhs, normal, planes)
```

```python
import jax
import jax.numpy as jnp
import numpy as np
from jax import lax
from jax.experimental import pallas as pl
from jax.experimental.pallas import tpu as pltpu
from jax.sharding import PartitionSpec as P

LOOKR = 2
LOOKC = 4
PAIR_BLOCK = 37
GAP = 12
RIDGE = 0.5
MAX_STEP = 40
UNROLL = 8
CHOOSE_UNROLL = 8
LANES = 128
SPLIT = 4
VMEM_LIMIT = 56 * 1024 * 1024
NN = (((1,), (0,)), ((), ()))
NT = (((1,), (1,)), ((), ()))


def look_matrix():
    row = np.arange(SPLIT * LANES)
    lane, sub = row % LANES, row // LANES
    target = (lane % LOOKC) * LANES + sub * (LANES // SPLIT) + lane // LOOKC
    return (target[:, None] == row[None, :]).astype(np.float32)


def split_bf16(value):
    high = value.astype(jnp.bfloat16)
    return high, (value - high.astype(jnp.float32)).astype(jnp.bfloat16)


def dot32(first, second, dims):
    return lax.dot_general(first, second, dims, preferred_element_type=jnp.float32)


def spread_looks(source, date, slot, step, looks, planes):
    raw = source[pl.ds(date, step)].reshape(step, 2, SPLIT, 16, LANES)
    left = jnp.concatenate(
        [raw[:, :, sub].reshape(step * 32, LANES) for sub in range(SPLIT)], axis=1
    )
    spread = dot32(left, looks[...], NN)
    for at in range(step):
        base = pl.multiple_of((slot + at) * 128, 128)
        for group in range(2):
            for rlook in range(LOOKR):
                top = (at * 2 + group) * 16 + rlook * 8
                for look in range(LOOKC):
                    planes[pl.ds(base + (rlook * LOOKC + look) * 16 + group * 8, 8), :] = spread[
                        top : top + 8, look * LANES : (look + 1) * LANES
                    ]


def pair_kernel(pair_count, with_halo, step, *refs):
    if with_halo:
        (bounds, listed, counts, images, halo, looks, series, weights, raw, raw_halo, planes, sems) = refs
    else:
        (bounds, pairs, images, looks, series, listed, counts, raw, planes, sems, sums) = refs
    dates = images.shape[0]
    steps = dates // step
    row_start, own_slot, halo_slot = bounds[0], bounds[1], bounds[2]
    copies = [
        pltpu.make_async_copy(
            images.at[pl.ds(at * step, step), pl.ds(row_start, 8)],
            raw.at[pl.ds(at * step, step)],
            sems.at[at],
        )
        for at in range(steps)
    ]
    if with_halo:
        copies.append(pltpu.make_async_copy(halo, raw_halo, sems.at[steps]))
    for copy in copies:
        copy.start()

    total = series if with_halo else sums
    spare = dates + GAP
    total[...] = jnp.zeros_like(total)
    planes[pl.ds(spare * 128, 128), :] = jnp.zeros((128, LANES), jnp.float32)

    if not with_halo:
        def choose(at, found):
            inside, across = found
            packed = pairs[at]
            listed[inside] = packed
            listed[pair_count + UNROLL + across] = packed
            return (inside + ((packed >> 20) & 1), across + (packed >> 21))

        found = lax.fori_loop(
            0, pair_count, choose, (jnp.int32(0), jnp.int32(0)), unroll=CHOOSE_UNROLL
        )
        for part in range(2):
            counts[part] = found[part]
            for at in range(UNROLL):
                listed[part * (pair_count + UNROLL) + found[part] + at] = jnp.int32(spare * 1025)

    def spread_step(at, carry):
        spread_looks(raw, at * step, own_slot + at * step, step, looks, planes)
        return carry

    for at in range(steps):
        copies[at].wait()
        spread_step(at, 0)
    if with_halo:
        copies[steps].wait()
        spread_looks(raw_halo, 0, halo_slot, GAP, looks, planes)

    def one_pair(packed, power):
        first = packed & 1023
        second = (packed >> 10) & 1023
        a_row = pl.multiple_of(first * 128, 128)
        b_row = pl.multiple_of(second * 128, 128)
        terms_re, terms_im = [], []
        for look in range(LOOKR * LOOKC):
            a_re = planes[pl.ds(a_row + look * 16, 8, stride=2), :]
            a_im = planes[pl.ds(a_row + look * 16 + 1, 8, stride=2), :]
            b_re = planes[pl.ds(b_row + look * 16, 8, stride=2), :]
            b_im = planes[pl.ds(b_row + look * 16 + 1, 8, stride=2), :]
            terms_re.append(a_re * b_re + a_im * b_im)
            terms_im.append(a_im * b_re - a_re * b_im)
        while len(terms_re) > 1:
            terms_re = [terms_re[k] + terms_re[k + 1] for k in range(0, len(terms_re), 2)]
            terms_im = [terms_im[k] + terms_im[k + 1] for k in range(0, len(terms_im), 2)]
        real = terms_re[0].astype(jnp.bfloat16).astype(jnp.float32)
        imag = terms_im[0].astype(jnp.bfloat16).astype(jnp.float32)
        a_at = pl.multiple_of(first * 16, 16)
        b_at = pl.multiple_of(second * 16, 16)
        total[pl.ds(a_at, 8), :] += real
        total[pl.ds(a_at + 8, 8), :] += imag
        total[pl.ds(b_at, 8), :] -= real
        total[pl.ds(b_at + 8, 8), :] -= imag
        return power + (real * real + imag * imag)

    power = jnp.zeros((8, LANES), jnp.float32)
    for part in range(2 if with_halo else 1):

        def some_pairs(at, power, part=part):
            for k in range(UNROLL):
                power = one_pair(listed[part * (pair_count + UNROLL) + at * UNROLL + k], power)
            return power

        power = lax.fori_loop(0, (counts[part] + UNROLL - 1) // UNROLL, some_pairs, power)
    scale = 1.0 / float(LOOKR * LOOKC)
    if with_halo:
        weights[...] = power * (scale * scale / float(pair_count))
    else:
        def narrow(date, carry):
            value = sums[pl.ds(pl.multiple_of((own_slot + date) * 16, 16), 16), :] * scale + carry
            rounded = value.astype(jnp.bfloat16)
            series[pl.ds(pl.multiple_of(date * 16, 16), 16), :] = rounded
            return value - rounded.astype(jnp.float32)

        lax.fori_loop(0, dates, narrow, jnp.zeros((16, LANES), jnp.float32), unroll=4)
        high, low = split_bf16(power * (scale * scale / float(pair_count)))
        series[pl.ds(dates * 16, 16), :] = jnp.concatenate(
            [high.astype(jnp.float32), low.astype(jnp.float32)], axis=0
        ).astype(jnp.bfloat16)


def in_vmem():
    return pl.BlockSpec(memory_space=pltpu.VMEM)


def in_smem():
    return pl.BlockSpec(memory_space=pltpu.SMEM)


def in_hbm():
    return pl.BlockSpec(memory_space=pl.ANY)


def call_pairs(bounds, pairs, images, looks, given=None):
    dates = images.shape[0]
    pair_count = pairs.shape[0]
    step = max(k for k in range(1, MAX_STEP + 1) if dates % k == 0)
    slots = dates + GAP + 1
    scratch = [
        pltpu.VMEM((dates, 8, 16, LANES), jnp.bfloat16),
        pltpu.VMEM((slots * 128, LANES), jnp.float32),
        pltpu.SemaphoreType.DMA((dates // step + 1,)),
    ]
    sums = jax.ShapeDtypeStruct((slots * 16, LANES), jnp.float32)
    if given is not None:
        halo, listed, counts = given
        out_shape = (sums, jax.ShapeDtypeStruct((8, LANES), jnp.float32))
        scratch.insert(1, pltpu.VMEM((GAP, 8, 16, LANES), jnp.bfloat16))
        in_specs = [in_smem()] * 3 + [in_hbm(), in_hbm(), in_vmem()]
        out_specs = (in_vmem(), in_vmem())
        args = (bounds, listed, counts, images, halo, looks)
    else:
        out_shape = (
            jax.ShapeDtypeStruct(((dates + 1) * 16, LANES), jnp.bfloat16),
            jax.ShapeDtypeStruct((2 * (pair_count + UNROLL),), jnp.int32),
            jax.ShapeDtypeStruct((2,), jnp.int32),
        )
        scratch.append(pltpu.VMEM(sums.shape, sums.dtype))
        in_specs = [in_smem(), in_smem(), in_hbm(), in_vmem()]
        out_specs = (in_vmem(), in_smem(), in_smem())
        args = (bounds, pairs, images, looks)
    return pl.pallas_call(
        lambda *refs: pair_kernel(pair_count, given is not None, step, *refs),
        out_shape=out_shape,
        in_specs=in_specs,
        out_specs=out_specs,
        scratch_shapes=scratch,
        compiler_params=pltpu.CompilerParams(vmem_limit_bytes=VMEM_LIMIT),
        cost_estimate=pl.CostEstimate(
            flops=pair_count * 70 * 1024, bytes_accessed=dates * 8 * 16 * 256, transcendentals=0
        ),
        name="pairs_other" if given is None else "pairs_own",
    )(*args)


def half_basis(row_start, col_start, row_total, col_total):
    sub = lax.broadcasted_iota(jnp.int32, (8, LANES), 0)
    lane = lax.broadcasted_iota(jnp.int32, (8, LANES), 1)
    width = LANES // SPLIT
    row = row_start + (sub // SPLIT) * SPLIT + lane // width
    col = col_start + (sub % SPLIT) * width + lane % width
    return centred(row, row_total), centred(col, col_total)


def centred(place, total):
    return (2.0 * place.astype(jnp.float32) + 1.0) / float(total) - 1.0


def combine_kernel(dates, row_total, col_total, *refs):
    (bounds, own, own_weights, other, high, low, moments, full, weighted_rows) = refs
    count = dates * 2
    span = dates + GAP
    scale = 1.0 / float(LOOKR * LOOKC)

    def rows(start, size):
        return pl.ds(pl.multiple_of(start * 16, 16), size * 16)

    full[rows(bounds[0], span), :] = own[pl.ds(0, span * 16), :] * scale
    rest = dates - GAP
    full[rows(bounds[1], rest), :] = other[rows(bounds[2], rest), :].astype(jnp.float32)
    full[rows(bounds[3], GAP), :] += other[rows(bounds[4], GAP), :].astype(jnp.float32)
    y_plane, x_plane = half_basis(bounds[5], bounds[6], row_total, col_total)
    basis = (jnp.ones((8, LANES), jnp.float32), y_plane, x_plane)
    padded = full.shape[0] // 16
    full[pl.ds(count * 16, (padded - count) * 16), :] = jnp.zeros(
        ((padded - count) * 16, LANES), jnp.float32
    )
    for at in range(3):
        full[pl.ds((count + at) * 16, 8), :] = basis[at]
    sent = other[pl.ds(dates * 16, 16), :].astype(jnp.float32)
    weights = own_weights[...] + (sent[:8] + sent[8:])
    weighted_rows[...] = jnp.zeros_like(weighted_rows)
    for at in range(3):
        plane = weights * basis[at]
        for part in range(2):
            for sub in range(8):
                weighted_rows[part * 3 + at : part * 3 + at + 1, pl.ds((part * 8 + sub) * LANES, LANES)] = (
                    plane[sub : sub + 1]
                )
    for at in range(16):
        value = full[pl.ds(at, padded, stride=16), :]
        upper, lower = split_bf16(value)
        high[:, at * LANES : (at + 1) * LANES] = upper
        low[:, at * LANES : (at + 1) * LANES] = lower
    upper, lower = split_bf16(weighted_rows[...])
    moments[...] = (
        dot32(upper, high[...], NT) + dot32(lower, high[...], NT) + dot32(upper, low[...], NT)
    )


def call_combine(bounds, own, own_weights, other, dates, row_total, col_total):
    padded = pad_dates(dates * 2)
    wide = jax.ShapeDtypeStruct((padded, 16 * LANES), jnp.bfloat16)
    return pl.pallas_call(
        lambda *refs: combine_kernel(dates, row_total, col_total, *refs),
        out_shape=(wide, wide, jax.ShapeDtypeStruct((8, padded), jnp.float32)),
        in_specs=[in_smem()] + [in_vmem()] * 3,
        out_specs=(in_vmem(),) * 3,
        scratch_shapes=[
            pltpu.VMEM((padded * 16, LANES), jnp.float32),
            pltpu.VMEM((8, 16 * LANES), jnp.float32),
        ],
        compiler_params=pltpu.CompilerParams(vmem_limit_bytes=VMEM_LIMIT),
        cost_estimate=pl.CostEstimate(flops=padded * 8 * 12288, bytes_accessed=8 << 20, transcendentals=0),
        name="combine",
    )(bounds, own, own_weights, other)


def pad_dates(count):
    return (count + 3 + 15) // 16 * 16


def inverse_kernel(pairs, high, low, state, normal_high, normal_low):
    padded = high.shape[0]
    date = lax.broadcasted_iota(jnp.int32, (padded, pairs.shape[1]), 0)
    design = (
        jnp.where(date == pairs[0:1, :], 1.0, 0.0) - jnp.where(date == pairs[1:2, :], 1.0, 0.0)
    ).astype(jnp.bfloat16)
    eye = jnp.where(
        lax.broadcasted_iota(jnp.int32, (padded, padded), 0)
        == lax.broadcasted_iota(jnp.int32, (padded, padded), 1),
        1.0,
        0.0,
    )
    normal = dot32(design, design, NT) + RIDGE * eye
    normal_high[...], normal_low[...] = split_bf16(normal)
    largest = jnp.max(jnp.sum(jnp.abs(normal), axis=1))
    state[...] = eye * (2.0 / (largest + RIDGE))
    error = (largest - RIDGE) / (largest + RIDGE)

    def product(first, second):
        return (
            dot32(first[0], second[0], NN) + dot32(first[0], second[1], NN) + dot32(first[1], second[0], NN)
        )

    def step(error):
        scale = 2.0 / (2.0 - error * error)
        now = split_bf16(state[...])
        residual = split_bf16(eye - product((normal_high[...], normal_low[...]), now))
        state[...] = scale * (state[...] + product(now, residual))
        return scale - 1.0

    lax.while_loop(lambda error: error > 1e-6, step, error)
    step(jnp.float32(0.0))
    high[...], low[...] = split_bf16(state[...])


def call_inverse(pair_rows, count):
    padded = pad_dates(count)
    square = jax.ShapeDtypeStruct((padded, padded), jnp.bfloat16)
    return pl.pallas_call(
        inverse_kernel,
        out_shape=(square, square),
        in_specs=[in_vmem()],
        out_specs=(in_vmem(),) * 2,
        scratch_shapes=[
            pltpu.VMEM((padded, padded), jnp.float32),
            pltpu.VMEM((padded, padded), jnp.bfloat16),
            pltpu.VMEM((padded, padded), jnp.bfloat16),
        ],
        compiler_params=pltpu.CompilerParams(vmem_limit_bytes=VMEM_LIMIT),
        cost_estimate=pl.CostEstimate(flops=100 * padded**3, bytes_accessed=8 << 20, transcendentals=0),
        name="inverse",
    )(pair_rows)


def solve_kernel(inverse_high, inverse_low, high, low, series):
    padded = high.shape[0]
    lane = lax.broadcasted_iota(jnp.int32, (padded, LANES), 1)
    width = LANES // SPLIT
    for group in range(4):
        cols = pl.ds(group * SPLIT * LANES, SPLIT * LANES)
        solved = (
            dot32(inverse_high[...], high[:, cols], NN)
            + dot32(inverse_high[...], low[:, cols], NN)
            + dot32(inverse_low[...], high[:, cols], NN)
        )
        blocks = [solved[:, k * LANES : (k + 1) * LANES] for k in range(SPLIT)]
        for bit in (1, 2):
            shift = bit * width
            even = (lane // shift) % 2 == 0
            swapped = list(blocks)
            for k in range(SPLIT):
                if k & bit == 0:
                    first, second = blocks[k], blocks[k | bit]
                    swapped[k] = jnp.where(even, first, pltpu.roll(second, shift, 1))
                    swapped[k | bit] = jnp.where(even, pltpu.roll(first, LANES - shift, 1), second)
            blocks = swapped
        part, half = group // 2, group % 2
        for k in range(SPLIT):
            series[(half * SPLIT + k) * 2 + part] = blocks[k]


def call_solve(inverse, values):
    padded = values[0].shape[0]
    return pl.pallas_call(
        solve_kernel,
        out_shape=jax.ShapeDtypeStruct((16, padded, LANES), jnp.float32),
        in_specs=[in_vmem()] * 4,
        out_specs=in_vmem(),
        compiler_params=pltpu.CompilerParams(vmem_limit_bytes=VMEM_LIMIT),
        cost_estimate=pl.CostEstimate(
            flops=6 * padded * padded * 16 * LANES, bytes_accessed=6 << 20, transcendentals=0
        ),
        name="solve",
    )(*inverse, *values)


def refine_kernel(count, row_total, col_total, *refs):
    (bounds, series, moments, inverse_high, inverse_low, refined) = refs
    padded = series.shape[1]
    normal = [
        [moments[at : at + 1, count + k : count + k + 1] for k in range(3)] for at in range(3)
    ]

    def cyclic(row_at, col_at):
        a, b = (row_at + 1) % 3, (row_at + 2) % 3
        c, d = (col_at + 1) % 3, (col_at + 2) % 3
        return normal[a][c] * normal[b][d] - normal[a][d] * normal[b][c]

    cofacts = [[cyclic(row_at, col_at) for col_at in range(3)] for row_at in range(3)]
    determinant = sum(normal[0][k] * cofacts[0][k] for k in range(3))
    rows = []
    for part in range(2):
        for at in range(3):
            rows.append(
                sum(
                    (cofacts[k][at] / determinant) * moments[part * 3 + k : part * 3 + k + 1, :]
                    for k in range(3)
                )
            )
    rows.append(jnp.zeros((2, padded), jnp.float32))
    upper, lower = split_bf16(jnp.concatenate(rows, axis=0))
    ramps = (
        dot32(inverse_high[...], upper, NT)
        + dot32(inverse_high[...], lower, NT)
        + dot32(inverse_low[...], upper, NT)
    )[:count]
    lane = lax.broadcasted_iota(jnp.int32, (1, LANES), 1)
    x_row = centred(bounds[1] + lane, col_total)
    for part in range(2):
        level, along_y, along_x = (
            jnp.broadcast_to(ramps[:, part * 3 + at : part * 3 + at + 1], (count, LANES))
            for at in range(3)
        )
        level = level + along_x * x_row
        for row in range(8):
            y = centred(bounds[0] + row, row_total)
            refined[pl.ds(row * 2 + part, count, stride=16), :] = series[row * 2 + part, :count] - (
                level + along_y * y
            )


def call_refine(bounds, series, moments, inverse, count, row_total, col_total):
    return pl.pallas_call(
        lambda *refs: refine_kernel(count, row_total, col_total, *refs),
        out_shape=jax.ShapeDtypeStruct((count * 16, LANES), jnp.float32),
        in_specs=[in_smem()] + [in_vmem()] * 4,
        out_specs=in_vmem(),
        compiler_params=pltpu.CompilerParams(vmem_limit_bytes=VMEM_LIMIT),
        cost_estimate=pl.CostEstimate(flops=count * 16 * LANES * 6, bytes_accessed=5 << 20, transcendentals=0),
        name="refine",
    )(bounds, series, moments, *inverse)


def sum_devices(value):
    cols = lax.axis_size("cols")
    if cols & (cols - 1):
        return lax.psum(value, ("dates", "cols"))
    bit = 1
    while bit < cols:
        value = value + lax.ppermute(value, "cols", [(at, at ^ bit) for at in range(cols)])
        bit *= 2
        if bit == 2:
            value = value + swap_dates(value)
    return value


def swap_dates(value):
    return lax.ppermute(value, "dates", [(0, 1), (1, 0)])


def two_halves(complex_images, pair_list):
    dates, rows, _, cols = complex_images.shape
    me = lax.axis_index("dates")
    half = rows // LOOKR // 2
    row_total, col_total = half * 2, cols // LOOKC * lax.axis_size("cols")
    images = complex_images.reshape(dates, rows, 2, SPLIT, cols // SPLIT)
    images = images.transpose(0, 1, 3, 2, 4).reshape(dates, rows // LOOKR, 16, LANES)
    first, second = pair_list[:, 0], pair_list[:, 1]
    low, base = dates * me, (dates - GAP) * me
    first_own = (first >= low) & (first < low + dates)
    second_own = (second >= low) & (second < low + dates)
    inside = (first_own & second_own).astype(jnp.int32)
    across = (first_own ^ second_own).astype(jnp.int32)
    packed = (first - base) | ((second - base) << 10)
    packed = jnp.where(first_own | second_own, packed | (inside << 20) | (across << 21), 0)

    edge = lax.dynamic_slice(
        images, ((dates - GAP) * (1 - me), half * (1 - me), 0, 0), (GAP, half, 16, LANES)
    )
    halo = swap_dates(edge)
    looks = jnp.asarray(look_matrix(), jnp.bfloat16)
    own_slot, halo_slot = GAP * me, dates * (1 - me)
    other, listed, counts = call_pairs(
        jnp.stack([half * (1 - me), own_slot, halo_slot]), packed, images, looks
    )
    other = swap_dates(other)
    own, own_weights = call_pairs(
        jnp.stack([half * me, own_slot, halo_slot]), packed, images, looks, (halo, listed, counts)
    )
    row_start, col_start = half * me, LANES * lax.axis_index("cols")
    high, lowpart, moments = call_combine(
        jnp.stack(
            [
                base,
                (dates + GAP) * (1 - me),
                GAP * (1 - me),
                dates - GAP * me,
                (dates - GAP) * me,
                row_start,
                col_start,
            ]
        ),
        own,
        own_weights,
        other,
        dates,
        row_total,
        col_total,
    )
    inverse = call_inverse(pair_list.T, dates * 2)
    moments = sum_devices(moments)
    series = call_solve(inverse, (high, lowpart))
    refined = call_refine(
        jnp.stack([row_start, col_start]), series, moments, inverse, dates * 2, row_total, col_total
    )
    return refined.reshape(dates * 2, half, 2, LANES)


highest = lax.Precision.HIGHEST


def pseudo_inverse(pair_list, count):
    date_ids = jnp.arange(count, dtype=jnp.int32)
    design = (pair_list[:, 0:1] == date_ids[None, :]).astype(jnp.float32) - (
        pair_list[:, 1:2] == date_ids[None, :]
    ).astype(jnp.float32)
    normal = jnp.dot(design.T, design, precision=highest) + RIDGE * jnp.eye(
        count, dtype=jnp.float32
    )
    factor = jnp.linalg.cholesky(normal)
    return jax.scipy.linalg.cho_solve((factor, True), design.T)


def pool_looks(plane):
    count, rows, cols = plane.shape
    rows_pooled = jnp.sum(plane.reshape(count, rows // LOOKR, LOOKR, cols), axis=2)
    return jnp.sum(rows_pooled.reshape(count, rows // LOOKR, cols // LOOKC, LOOKC), axis=3)


def multilook_pairs(tile_stack, pair_list, pair_block):
    real_planes = tile_stack[:, :, 0, :]
    imag_planes = tile_stack[:, :, 1, :]
    groups = pair_list.reshape(-1, pair_block, 2)
    scale = 1.0 / float(LOOKR * LOOKC)

    def one_group(group):
        first_real = jnp.take(real_planes, group[:, 0], axis=0).astype(jnp.float32)
        first_imag = jnp.take(imag_planes, group[:, 0], axis=0).astype(jnp.float32)
        second_real = jnp.take(real_planes, group[:, 1], axis=0).astype(jnp.float32)
        second_imag = jnp.take(imag_planes, group[:, 1], axis=0).astype(jnp.float32)
        real_part = pool_looks(first_real * second_real + first_imag * second_imag)
        imag_part = pool_looks(first_imag * second_real - first_real * second_imag)
        return (jnp.stack([real_part, imag_part], axis=2) * scale).astype(jnp.bfloat16)

    looked = lax.map(one_group, groups)
    return looked.reshape((pair_list.shape[0],) + looked.shape[2:])


def coordinates(start, count, total):
    return (2.0 * (start + jnp.arange(count, dtype=jnp.int32)).astype(jnp.float32) + 1.0) / float(
        total
    ) - 1.0


def basis_planes(row_coord, col_coord):
    constant = jnp.ones((row_coord.shape[0], col_coord.shape[0]), jnp.float32)
    return jnp.stack([constant, row_coord[:, None] * constant, col_coord[None, :] * constant])


def weighted(widened, planes, pair_count):
    weights = jnp.sum(widened * widened, axis=(0, 2)) / float(pair_count)
    weighted_planes = planes * weights[None]
    normal = jnp.einsum("jrc,krc->jk", weighted_planes, planes, precision=highest)
    return (weighted_planes, normal)


def inverse3(matrix):

    def cyclic(row_at, col_at):
        return (
            matrix[(row_at + 1) % 3, (col_at + 1) % 3] * matrix[(row_at + 2) % 3, (col_at + 2) % 3]
            - matrix[(row_at + 1) % 3, (col_at + 2) % 3]
            * matrix[(row_at + 2) % 3, (col_at + 1) % 3]
        )

    cofacts = jnp.stack(
        [jnp.stack([cyclic(row_at, col_at) for col_at in range(3)]) for row_at in range(3)]
    )
    determinant = jnp.sum(matrix[0] * cofacts[0])
    return cofacts.T / determinant


def refine(series, ramp_rhs, normal, planes):
    ramp_coef = jnp.einsum("jk,dkh->djh", inverse3(normal), ramp_rhs, precision=highest)
    return series - jnp.einsum("djh,jrc->drhc", ramp_coef, planes, precision=highest)


def any_dates(complex_images, pair_list):
    date_count = lax.axis_size("dates")
    date_index = lax.axis_index("dates")
    col_index = lax.axis_index("cols")
    pair_count = pair_list.shape[0]
    date_total = complex_images.shape[0] * date_count
    rounded_pseudo = pseudo_inverse(pair_list, date_total).astype(jnp.bfloat16)
    regrouped = lax.all_to_all(complex_images, "dates", split_axis=1, concat_axis=0, tiled=True)
    interferograms = multilook_pairs(regrouped, pair_list, PAIR_BLOCK * date_count)
    ml_rows = interferograms.shape[1]
    ml_cols = interferograms.shape[3]
    planes = basis_planes(
        coordinates(date_index * ml_rows, ml_rows, ml_rows * date_count),
        coordinates(col_index * ml_cols, ml_cols, ml_cols * lax.axis_size("cols")),
    )
    widened = interferograms.astype(jnp.float32)
    weighted_planes, normal_part = weighted(widened, planes, pair_count)
    flat_pairs = interferograms.reshape(pair_count, -1)
    series = jnp.dot(rounded_pseudo, flat_pairs, preferred_element_type=jnp.float32).reshape(
        (date_total,) + interferograms.shape[1:]
    )
    rhs_part = jnp.einsum("jrc,drhc->djh", weighted_planes, series, precision=highest)
    normal, ramp_rhs = lax.psum((normal_part, rhs_part), ("dates", "cols"))
    return refine(series, ramp_rhs, normal, planes)


def solution(mesh):
    def body(complex_images, pair_list):
        dates, rows, _, cols = complex_images.shape
        if mesh.shape["dates"] == 2 and cols == LANES * LOOKC and rows == 32 and dates >= GAP:
            return two_halves(complex_images, pair_list)
        return any_dates(complex_images, pair_list)

    return jax.shard_map(
        body,
        mesh=mesh,
        in_specs=(P("dates", None, None, "cols"), P()),
        out_specs=P(None, "dates", None, "cols"),
        check_vma=False,
    )
```

```python
import jax
import jax.numpy as jnp
import numpy as np
from jax import lax
from jax.experimental import pallas as pl
from jax.experimental.pallas import tpu as pltpu
from jax.sharding import PartitionSpec as P

LOOKR = 2
LOOKC = 4
PAIR_BLOCK = 37
GAP = 12
RIDGE = 0.5
MAX_STEP = 40
UNROLL = 8
LANES = 128
SPLIT = 4
VMEM_LIMIT = 56 * 1024 * 1024
NN = (((1,), (0,)), ((), ()))
NT = (((1,), (1,)), ((), ()))


def look_matrix():
    row = np.arange(SPLIT * LANES)
    lane, sub = row % LANES, row // LANES
    target = (lane % LOOKC) * LANES + sub * (LANES // SPLIT) + lane // LOOKC
    return (target[:, None] == row[None, :]).astype(np.float32)


def split_bf16(value):
    high = value.astype(jnp.bfloat16)
    return high, (value - high.astype(jnp.float32)).astype(jnp.bfloat16)


def dot32(first, second, dims):
    return lax.dot_general(first, second, dims, preferred_element_type=jnp.float32)


def spread_looks(source, date, slot, step, looks, planes, choose=None, start=0, share=0, found=None):
    raw = source[pl.ds(date, step)].reshape(step, 2, SPLIT, 16, LANES)
    left = jnp.concatenate(
        [raw[:, :, sub].reshape(step * 32, LANES) for sub in range(SPLIT)], axis=1
    )
    spread = dot32(left, looks[...], NN)
    for at in range(step):
        base = pl.multiple_of((slot + at) * 128, 128)
        for group in range(2):
            for rlook in range(LOOKR):
                top = (at * 2 + group) * 16 + rlook * 8
                for look in range(LOOKC):
                    planes[pl.ds(base + (rlook * LOOKC + look) * 16 + group * 8, 8), :] = spread[
                        top : top + 8, look * LANES : (look + 1) * LANES
                    ]
        for k in range(share):
            found = choose(start + at * share + k, found)
    return found


def pair_kernel(pair_count, with_halo, step, *refs):
    if with_halo:
        (listed, counts, images, halo, looks, series, weights, raw, raw_halo, planes, sems) = refs
    else:
        (pairs, images, looks, series, listed, counts, raw, planes, sems, sums) = refs
    dates = images.shape[0]
    steps = dates // step
    me = lax.axis_index("dates")
    row_start = 8 * (me if with_halo else 1 - me)
    own_slot, halo_slot = GAP * me, dates * (1 - me)
    copies = [
        pltpu.make_async_copy(
            images.at[pl.ds(at * step, step), pl.ds(row_start, 8)],
            raw.at[pl.ds(at * step, step)],
            sems.at[at],
        )
        for at in range(steps)
    ]
    if with_halo:
        copies.append(pltpu.make_async_copy(halo, raw_halo, sems.at[steps]))
    for copy in copies:
        copy.start()

    total = series if with_halo else sums
    spare = dates + GAP
    total[...] = jnp.zeros_like(total)
    planes[pl.ds(spare * 128, 128), :] = jnp.zeros((128, LANES), jnp.float32)

    second_list = pair_count + UNROLL

    def choose(at, found):
        packed = pairs[at]
        listed[found[0]] = packed
        listed[second_list + found[1]] = packed
        return (found[0] + ((packed >> 20) & 1), found[1] + (packed >> 21))

    found = (jnp.int32(0), jnp.int32(0))
    share = 0 if with_halo else pair_count // dates
    for at in range(steps):
        copies[at].wait()
        found = spread_looks(
            raw, at * step, own_slot + at * step, step, looks, planes,
            choose, at * step * share, share, found,
        )
    if not with_halo:
        for at in range(dates * share, pair_count):
            found = choose(at, found)
        for part in range(2):
            counts[part] = found[part]
            for at in range(UNROLL):
                listed[part * second_list + found[part] + at] = jnp.int32(spare * 1025)
    if with_halo:
        copies[steps].wait()
        spread_looks(raw_halo, 0, halo_slot, GAP, looks, planes)

    def one_pair(packed, power):
        first = packed & 1023
        second = (packed >> 10) & 1023
        a_row = pl.multiple_of(first * 128, 128)
        b_row = pl.multiple_of(second * 128, 128)
        terms_re, terms_im = [], []
        for look in range(LOOKR * LOOKC):
            a_re = planes[pl.ds(a_row + look * 16, 8, stride=2), :]
            a_im = planes[pl.ds(a_row + look * 16 + 1, 8, stride=2), :]
            b_re = planes[pl.ds(b_row + look * 16, 8, stride=2), :]
            b_im = planes[pl.ds(b_row + look * 16 + 1, 8, stride=2), :]
            terms_re.append(a_re * b_re + a_im * b_im)
            terms_im.append(a_im * b_re - a_re * b_im)
        while len(terms_re) > 1:
            terms_re = [terms_re[k] + terms_re[k + 1] for k in range(0, len(terms_re), 2)]
            terms_im = [terms_im[k] + terms_im[k + 1] for k in range(0, len(terms_im), 2)]
        real = terms_re[0].astype(jnp.bfloat16).astype(jnp.float32)
        imag = terms_im[0].astype(jnp.bfloat16).astype(jnp.float32)
        a_at = pl.multiple_of(first * 16, 16)
        b_at = pl.multiple_of(second * 16, 16)
        total[pl.ds(a_at, 8), :] += real
        total[pl.ds(a_at + 8, 8), :] += imag
        total[pl.ds(b_at, 8), :] -= real
        total[pl.ds(b_at + 8, 8), :] -= imag
        return power + (real * real + imag * imag)

    power = jnp.zeros((8, LANES), jnp.float32)
    for part in range(2 if with_halo else 1):

        def some_pairs(at, power, part=part):
            for k in range(UNROLL):
                power = one_pair(listed[part * second_list + at * UNROLL + k], power)
            return power

        power = lax.fori_loop(0, (counts[part] + UNROLL - 1) // UNROLL, some_pairs, power)
    scale = 1.0 / float(LOOKR * LOOKC)
    if with_halo:
        weights[...] = power * (scale * scale / float(pair_count))
    else:
        def narrow(date, carry):
            value = sums[pl.ds(pl.multiple_of((own_slot + date) * 16, 16), 16), :] * scale + carry
            rounded = value.astype(jnp.bfloat16)
            series[pl.ds(pl.multiple_of(date * 16, 16), 16), :] = rounded
            return value - rounded.astype(jnp.float32)

        lax.fori_loop(0, dates, narrow, jnp.zeros((16, LANES), jnp.float32), unroll=4)
        high, low = split_bf16(power * (scale * scale / float(pair_count)))
        series[pl.ds(dates * 16, 16), :] = jnp.concatenate(
            [high.astype(jnp.float32), low.astype(jnp.float32)], axis=0
        ).astype(jnp.bfloat16)


def in_vmem():
    return pl.BlockSpec(memory_space=pltpu.VMEM)


def in_smem():
    return pl.BlockSpec(memory_space=pltpu.SMEM)


def in_hbm():
    return pl.BlockSpec(memory_space=pl.ANY)


def call_pairs(pairs, images, looks, given=None):
    dates = images.shape[0]
    pair_count = pairs.shape[0]
    step = max(k for k in range(1, MAX_STEP + 1) if dates % k == 0)
    slots = dates + GAP + 1
    scratch = [
        pltpu.VMEM((dates, 8, 16, LANES), jnp.bfloat16),
        pltpu.VMEM((slots * 128, LANES), jnp.float32),
        pltpu.SemaphoreType.DMA((dates // step + 1,)),
    ]
    sums = jax.ShapeDtypeStruct((slots * 16, LANES), jnp.float32)
    if given is not None:
        halo, listed, counts = given
        out_shape = (sums, jax.ShapeDtypeStruct((8, LANES), jnp.float32))
        scratch.insert(1, pltpu.VMEM((GAP, 8, 16, LANES), jnp.bfloat16))
        in_specs = [in_smem()] * 2 + [in_hbm(), in_hbm(), in_vmem()]
        out_specs = (in_vmem(), in_vmem())
        args = (listed, counts, images, halo, looks)
    else:
        out_shape = (
            jax.ShapeDtypeStruct(((dates + 1) * 16, LANES), jnp.bfloat16),
            jax.ShapeDtypeStruct((2 * (pair_count + UNROLL),), jnp.int32),
            jax.ShapeDtypeStruct((2,), jnp.int32),
        )
        scratch.append(pltpu.VMEM(sums.shape, sums.dtype))
        in_specs = [in_smem(), in_hbm(), in_vmem()]
        out_specs = (in_vmem(), in_smem(), in_smem())
        args = (pairs, images, looks)
    return pl.pallas_call(
        lambda *refs: pair_kernel(pair_count, given is not None, step, *refs),
        out_shape=out_shape,
        in_specs=in_specs,
        out_specs=out_specs,
        scratch_shapes=scratch,
        compiler_params=pltpu.CompilerParams(vmem_limit_bytes=VMEM_LIMIT),
        cost_estimate=pl.CostEstimate(
            flops=pair_count * 70 * 1024, bytes_accessed=pair_count * 48 * 1024, transcendentals=0
        ),
        name="pairs_other" if given is None else "pairs_own",
    )(*args)


def half_basis(row_start, col_start, row_total, col_total):
    sub = lax.broadcasted_iota(jnp.int32, (8, LANES), 0)
    lane = lax.broadcasted_iota(jnp.int32, (8, LANES), 1)
    width = LANES // SPLIT
    row = row_start + (sub // SPLIT) * SPLIT + lane // width
    col = col_start + (sub % SPLIT) * width + lane % width
    return centred(row, row_total), centred(col, col_total)


def centred(place, total):
    return (2.0 * place.astype(jnp.float32) + 1.0) / float(total) - 1.0


def combine_kernel(dates, row_total, col_total, *refs):
    (own, own_weights, other, high, low, moments, full, weighted_rows) = refs
    me = lax.axis_index("dates")
    count = dates * 2
    span = dates + GAP
    scale = 1.0 / float(LOOKR * LOOKC)

    def rows(start, size):
        return pl.ds(pl.multiple_of(start * 16, 16), size * 16)

    full[rows((dates - GAP) * me, span), :] = own[pl.ds(0, span * 16), :] * scale
    rest = dates - GAP
    full[rows(span * (1 - me), rest), :] = other[rows(GAP * (1 - me), rest), :].astype(jnp.float32)
    full[rows(dates - GAP * me, GAP), :] += other[rows(rest * me, GAP), :].astype(jnp.float32)
    y_plane, x_plane = half_basis(8 * me, LANES * lax.axis_index("cols"), row_total, col_total)
    basis = (jnp.ones((8, LANES), jnp.float32), y_plane, x_plane)
    padded = full.shape[0] // 16
    full[pl.ds(count * 16, (padded - count) * 16), :] = jnp.zeros(
        ((padded - count) * 16, LANES), jnp.float32
    )
    for at in range(3):
        full[pl.ds((count + at) * 16, 8), :] = basis[at]
    sent = other[pl.ds(dates * 16, 16), :].astype(jnp.float32)
    weights = own_weights[...] + (sent[:8] + sent[8:])
    weighted_rows[...] = jnp.zeros_like(weighted_rows)
    for at in range(3):
        plane = weights * basis[at]
        for part in range(2):
            for sub in range(8):
                weighted_rows[part * 3 + at : part * 3 + at + 1, pl.ds((part * 8 + sub) * LANES, LANES)] = (
                    plane[sub : sub + 1]
                )
    for at in range(16):
        value = full[pl.ds(at, padded, stride=16), :]
        upper, lower = split_bf16(value)
        high[:, at * LANES : (at + 1) * LANES] = upper
        low[:, at * LANES : (at + 1) * LANES] = lower
    upper, lower = split_bf16(weighted_rows[...])
    moments[...] = (
        dot32(upper, high[...], NT) + dot32(lower, high[...], NT) + dot32(upper, low[...], NT)
    )


def call_combine(own, own_weights, other, dates, row_total, col_total):
    padded = pad_dates(dates * 2)
    wide = jax.ShapeDtypeStruct((padded, 16 * LANES), jnp.bfloat16)
    return pl.pallas_call(
        lambda *refs: combine_kernel(dates, row_total, col_total, *refs),
        out_shape=(wide, wide, jax.ShapeDtypeStruct((8, padded), jnp.float32)),
        in_specs=[in_vmem()] * 3,
        out_specs=(in_vmem(),) * 3,
        scratch_shapes=[
            pltpu.VMEM((padded * 16, LANES), jnp.float32),
            pltpu.VMEM((8, 16 * LANES), jnp.float32),
        ],
        compiler_params=pltpu.CompilerParams(vmem_limit_bytes=VMEM_LIMIT),
        cost_estimate=pl.CostEstimate(flops=padded * 8 * 12288, bytes_accessed=16 << 20, transcendentals=0),
        name="combine",
    )(own, own_weights, other)


def pad_dates(count):
    return (count + 3 + 15) // 16 * 16


def inverse_kernel(pairs, high, low, state, residual, normal_high, normal_low):
    padded = high.shape[0]
    date = lax.broadcasted_iota(jnp.int32, (padded, pairs.shape[1]), 0)
    design = (
        jnp.where(date == pairs[0:1, :], 1.0, 0.0) - jnp.where(date == pairs[1:2, :], 1.0, 0.0)
    ).astype(jnp.bfloat16)
    eye = jnp.where(
        lax.broadcasted_iota(jnp.int32, (padded, padded), 0)
        == lax.broadcasted_iota(jnp.int32, (padded, padded), 1),
        1.0,
        0.0,
    )
    normal = dot32(design, design, NT) + RIDGE * eye
    normal_high[...], normal_low[...] = split_bf16(normal)
    largest = jnp.max(jnp.sum(jnp.abs(normal), axis=1))
    careful = largest > 128.0
    scale, error = centre((largest - RIDGE) / (largest + RIDGE))
    start = 2.0 / (largest + RIDGE)
    state[...] = (scale * start) * (2.0 * eye - start * normal)

    def step(scale):
        now, rest = split_bf16(state[...])
        residual[...] = eye - dot32(normal_high[...], now, NN) - dot32(normal_high[...], rest, NN)

        @pl.when(careful)
        def _():
            residual[...] -= dot32(normal_low[...], now, NN)

        upper, lower = split_bf16(residual[...])
        change = dot32(now, upper, NN)
        state[...] = scale * (state[...] + change)

        @pl.when(careful)
        def _():
            state[...] += scale * (dot32(now, lower, NN) + dot32(rest, upper, NN))

    def body(error):
        scale, left = centre(error)
        step(scale)
        return jnp.maximum(left, 0.05 * error)

    lax.while_loop(lambda error: error > 5e-4, body, error)
    step(jnp.float32(1.0))
    high[...], low[...] = split_bf16(state[...])


def centre(error):
    scale = 2.0 / (2.0 - error * error)
    return scale, scale - 1.0


def call_inverse(pair_rows, count):
    padded = pad_dates(count)
    square = jax.ShapeDtypeStruct((padded, padded), jnp.bfloat16)
    return pl.pallas_call(
        inverse_kernel,
        out_shape=(square, square),
        in_specs=[in_vmem()],
        out_specs=(in_vmem(),) * 2,
        scratch_shapes=[
            pltpu.VMEM((padded, padded), jnp.float32),
            pltpu.VMEM((padded, padded), jnp.float32),
            pltpu.VMEM((padded, padded), jnp.bfloat16),
            pltpu.VMEM((padded, padded), jnp.bfloat16),
        ],
        compiler_params=pltpu.CompilerParams(vmem_limit_bytes=VMEM_LIMIT),
        cost_estimate=pl.CostEstimate(flops=50 * padded**3, bytes_accessed=24 << 20, transcendentals=0),
        name="inverse",
    )(pair_rows)


def solve_kernel(inverse_high, inverse_low, high, low, series):
    padded = high.shape[0]
    lane = lax.broadcasted_iota(jnp.int32, (padded, LANES), 1)
    width = LANES // SPLIT
    for group in range(4):
        cols = pl.ds(group * SPLIT * LANES, SPLIT * LANES)
        solved = (
            dot32(inverse_high[...], high[:, cols], NN)
            + dot32(inverse_high[...], low[:, cols], NN)
            + dot32(inverse_low[...], high[:, cols], NN)
        )
        blocks = [solved[:, k * LANES : (k + 1) * LANES] for k in range(SPLIT)]
        for bit in (1, 2):
            shift = bit * width
            even = (lane // shift) % 2 == 0
            swapped = list(blocks)
            for k in range(SPLIT):
                if k & bit == 0:
                    first, second = blocks[k], blocks[k | bit]
                    swapped[k] = jnp.where(even, first, pltpu.roll(second, shift, 1))
                    swapped[k | bit] = jnp.where(even, pltpu.roll(first, LANES - shift, 1), second)
            blocks = swapped
        part, half = group // 2, group % 2
        for k in range(SPLIT):
            series[(half * SPLIT + k) * 2 + part] = blocks[k]


def call_solve(inverse, values):
    padded = values[0].shape[0]
    return pl.pallas_call(
        solve_kernel,
        out_shape=jax.ShapeDtypeStruct((16, padded, LANES), jnp.float32),
        in_specs=[in_vmem()] * 4,
        out_specs=in_vmem(),
        compiler_params=pltpu.CompilerParams(vmem_limit_bytes=VMEM_LIMIT),
        cost_estimate=pl.CostEstimate(
            flops=6 * padded * padded * 16 * LANES, bytes_accessed=20 << 20, transcendentals=0
        ),
        name="solve",
    )(*inverse, *values)


def refine_kernel(count, row_total, col_total, *refs):
    (series, moments, inverse_high, inverse_low, refined) = refs
    padded = series.shape[1]
    normal = [
        [moments[at : at + 1, count + k : count + k + 1] for k in range(3)] for at in range(3)
    ]

    def cyclic(row_at, col_at):
        a, b = (row_at + 1) % 3, (row_at + 2) % 3
        c, d = (col_at + 1) % 3, (col_at + 2) % 3
        return normal[a][c] * normal[b][d] - normal[a][d] * normal[b][c]

    cofacts = [[cyclic(row_at, col_at) for col_at in range(3)] for row_at in range(3)]
    determinant = sum(normal[0][k] * cofacts[0][k] for k in range(3))
    rows = []
    for part in range(2):
        for at in range(3):
            rows.append(
                sum(
                    (cofacts[k][at] / determinant) * moments[part * 3 + k : part * 3 + k + 1, :]
                    for k in range(3)
                )
            )
    rows.append(jnp.zeros((2, padded), jnp.float32))
    upper, lower = split_bf16(jnp.concatenate(rows, axis=0))
    ramps = (
        dot32(inverse_high[...], upper, NT)
        + dot32(inverse_high[...], lower, NT)
        + dot32(inverse_low[...], upper, NT)
    )[:count]
    lane = lax.broadcasted_iota(jnp.int32, (1, LANES), 1)
    x_row = centred(LANES * lax.axis_index("cols") + lane, col_total)
    row_start = 8 * lax.axis_index("dates")
    for part in range(2):
        level, along_y, along_x = (
            jnp.broadcast_to(ramps[:, part * 3 + at : part * 3 + at + 1], (count, LANES))
            for at in range(3)
        )
        level = level + along_x * x_row
        for row in range(8):
            y = centred(row_start + row, row_total)
            refined[pl.ds(row * 2 + part, count, stride=16), :] = series[row * 2 + part, :count] - (
                level + along_y * y
            )


def call_refine(series, moments, inverse, count, row_total, col_total):
    return pl.pallas_call(
        lambda *refs: refine_kernel(count, row_total, col_total, *refs),
        out_shape=jax.ShapeDtypeStruct((count * 16, LANES), jnp.float32),
        in_specs=[in_vmem()] * 4,
        out_specs=in_vmem(),
        compiler_params=pltpu.CompilerParams(vmem_limit_bytes=VMEM_LIMIT),
        cost_estimate=pl.CostEstimate(flops=count * 16 * LANES * 6, bytes_accessed=16 << 20, transcendentals=0),
        name="refine",
    )(series, moments, *inverse)


def sum_devices(value):
    cols = lax.axis_size("cols")
    if cols & (cols - 1):
        return lax.psum(value, ("dates", "cols"))
    bit = 1
    while bit < cols:
        value = value + lax.ppermute(value, "cols", [(at, at ^ bit) for at in range(cols)])
        bit *= 2
        if bit == 2:
            value = value + swap_dates(value)
    return value


def swap_dates(value):
    return lax.ppermute(value, "dates", [(0, 1), (1, 0)])


def two_halves(complex_images, pair_list):
    dates, rows, _, cols = complex_images.shape
    me = lax.axis_index("dates")
    half = rows // LOOKR // 2
    row_total, col_total = half * 2, cols // LOOKC * lax.axis_size("cols")
    images = complex_images.reshape(dates, rows, 2, SPLIT, cols // SPLIT)
    images = images.transpose(0, 1, 3, 2, 4).reshape(dates, rows // LOOKR, 16, LANES)
    first, second = pair_list[:, 0], pair_list[:, 1]
    low, base = dates * me, (dates - GAP) * me
    first_own = (first >= low) & (first < low + dates)
    second_own = (second >= low) & (second < low + dates)
    inside = (first_own & second_own).astype(jnp.int32)
    across = (first_own ^ second_own).astype(jnp.int32)
    packed = (first - base) | ((second - base) << 10)
    packed = jnp.where(first_own | second_own, packed | (inside << 20) | (across << 21), 0)

    edge = lax.dynamic_slice(
        images, ((dates - GAP) * (1 - me), half * (1 - me), 0, 0), (GAP, half, 16, LANES)
    )
    edge, pair_rows = lax.optimization_barrier((edge, pair_list.T))
    halo = swap_dates(edge)
    inverse = call_inverse(pair_rows, dates * 2)
    halo, inverse, packed = lax.optimization_barrier((halo, inverse, packed))
    looks = jnp.asarray(look_matrix(), jnp.bfloat16)
    other, listed, counts = call_pairs(packed, images, looks)
    other = swap_dates(other)
    own, own_weights = call_pairs(packed, images, looks, (halo, listed, counts))
    high, lowpart, moments = call_combine(own, own_weights, other, dates, row_total, col_total)
    moments = sum_devices(moments)
    series = call_solve(inverse, (high, lowpart))
    refined = call_refine(series, moments, inverse, dates * 2, row_total, col_total)
    return refined.reshape(dates * 2, half, 2, LANES)


highest = lax.Precision.HIGHEST


def pseudo_inverse(pair_list, count):
    date_ids = jnp.arange(count, dtype=jnp.int32)
    design = (pair_list[:, 0:1] == date_ids[None, :]).astype(jnp.float32) - (
        pair_list[:, 1:2] == date_ids[None, :]
    ).astype(jnp.float32)
    normal = jnp.dot(design.T, design, precision=highest) + RIDGE * jnp.eye(
        count, dtype=jnp.float32
    )
    factor = jnp.linalg.cholesky(normal)
    return jax.scipy.linalg.cho_solve((factor, True), design.T)


def pool_looks(plane):
    count, rows, cols = plane.shape
    rows_pooled = jnp.sum(plane.reshape(count, rows // LOOKR, LOOKR, cols), axis=2)
    return jnp.sum(rows_pooled.reshape(count, rows // LOOKR, cols // LOOKC, LOOKC), axis=3)


def multilook_pairs(tile_stack, pair_list, pair_block):
    real_planes = tile_stack[:, :, 0, :]
    imag_planes = tile_stack[:, :, 1, :]
    groups = pair_list.reshape(-1, pair_block, 2)
    scale = 1.0 / float(LOOKR * LOOKC)

    def one_group(group):
        first_real = jnp.take(real_planes, group[:, 0], axis=0).astype(jnp.float32)
        first_imag = jnp.take(imag_planes, group[:, 0], axis=0).astype(jnp.float32)
        second_real = jnp.take(real_planes, group[:, 1], axis=0).astype(jnp.float32)
        second_imag = jnp.take(imag_planes, group[:, 1], axis=0).astype(jnp.float32)
        real_part = pool_looks(first_real * second_real + first_imag * second_imag)
        imag_part = pool_looks(first_imag * second_real - first_real * second_imag)
        return (jnp.stack([real_part, imag_part], axis=2) * scale).astype(jnp.bfloat16)

    looked = lax.map(one_group, groups)
    return looked.reshape((pair_list.shape[0],) + looked.shape[2:])


def coordinates(start, count, total):
    return (2.0 * (start + jnp.arange(count, dtype=jnp.int32)).astype(jnp.float32) + 1.0) / float(
        total
    ) - 1.0


def basis_planes(row_coord, col_coord):
    constant = jnp.ones((row_coord.shape[0], col_coord.shape[0]), jnp.float32)
    return jnp.stack([constant, row_coord[:, None] * constant, col_coord[None, :] * constant])


def weighted(widened, planes, pair_count):
    weights = jnp.sum(widened * widened, axis=(0, 2)) / float(pair_count)
    weighted_planes = planes * weights[None]
    normal = jnp.einsum("jrc,krc->jk", weighted_planes, planes, precision=highest)
    return (weighted_planes, normal)


def inverse3(matrix):

    def cyclic(row_at, col_at):
        return (
            matrix[(row_at + 1) % 3, (col_at + 1) % 3] * matrix[(row_at + 2) % 3, (col_at + 2) % 3]
            - matrix[(row_at + 1) % 3, (col_at + 2) % 3]
            * matrix[(row_at + 2) % 3, (col_at + 1) % 3]
        )

    cofacts = jnp.stack(
        [jnp.stack([cyclic(row_at, col_at) for col_at in range(3)]) for row_at in range(3)]
    )
    determinant = jnp.sum(matrix[0] * cofacts[0])
    return cofacts.T / determinant


def refine(series, ramp_rhs, normal, planes):
    ramp_coef = jnp.einsum("jk,dkh->djh", inverse3(normal), ramp_rhs, precision=highest)
    return series - jnp.einsum("djh,jrc->drhc", ramp_coef, planes, precision=highest)


def any_dates(complex_images, pair_list):
    date_count = lax.axis_size("dates")
    date_index = lax.axis_index("dates")
    col_index = lax.axis_index("cols")
    pair_count = pair_list.shape[0]
    date_total = complex_images.shape[0] * date_count
    rounded_pseudo = pseudo_inverse(pair_list, date_total).astype(jnp.bfloat16)
    regrouped = lax.all_to_all(complex_images, "dates", split_axis=1, concat_axis=0, tiled=True)
    interferograms = multilook_pairs(regrouped, pair_list, PAIR_BLOCK * date_count)
    ml_rows = interferograms.shape[1]
    ml_cols = interferograms.shape[3]
    planes = basis_planes(
        coordinates(date_index * ml_rows, ml_rows, ml_rows * date_count),
        coordinates(col_index * ml_cols, ml_cols, ml_cols * lax.axis_size("cols")),
    )
    widened = interferograms.astype(jnp.float32)
    weighted_planes, normal_part = weighted(widened, planes, pair_count)
    flat_pairs = interferograms.reshape(pair_count, -1)
    series = jnp.dot(rounded_pseudo, flat_pairs, preferred_element_type=jnp.float32).reshape(
        (date_total,) + interferograms.shape[1:]
    )
    rhs_part = jnp.einsum("jrc,drhc->djh", weighted_planes, series, precision=highest)
    normal, ramp_rhs = lax.psum((normal_part, rhs_part), ("dates", "cols"))
    return refine(series, ramp_rhs, normal, planes)


def solution(mesh):
    def body(complex_images, pair_list):
        dates, rows, _, cols = complex_images.shape
        if mesh.shape["dates"] == 2 and cols == LANES * LOOKC and rows == 32 and dates >= GAP:
            return two_halves(complex_images, pair_list)
        return any_dates(complex_images, pair_list)

    return jax.shard_map(
        body,
        mesh=mesh,
        in_specs=(P("dates", None, None, "cols"), P()),
        out_specs=P(None, "dates", None, "cols"),
        check_vma=False,
    )
```

```python
import jax
import jax.numpy as jnp
import numpy as np
from jax import lax
from jax.experimental import pallas as pl
from jax.experimental.pallas import tpu as pltpu
from jax.sharding import PartitionSpec as P

LOOKR = 2
LOOKC = 4
PAIR_BLOCK = 37
GAP = 12
RIDGE = 0.5
MAX_STEP = 40
UNROLL = 8
LANES = 128
SPLIT = 4
PAIR_VMEM = 28 * 1024 * 1024
SMALL_VMEM = 12 * 1024 * 1024
NN = (((1,), (0,)), ((), ()))
NT = (((1,), (1,)), ((), ()))


def look_matrix():
    row = np.arange(SPLIT * LANES)
    lane, sub = row % LANES, row // LANES
    target = (lane % LOOKC) * LANES + sub * (LANES // SPLIT) + lane // LOOKC
    return (target[:, None] == row[None, :]).astype(np.float32)


def split_bf16(value):
    high = value.astype(jnp.bfloat16)
    return high, (value - high.astype(jnp.float32)).astype(jnp.bfloat16)


def dot32(first, second, dims):
    return lax.dot_general(first, second, dims, preferred_element_type=jnp.float32)


def spread_looks(source, date, slot, step, looks, planes, choose=None, start=0, share=0, found=None):
    raw = source[pl.ds(date, step)].reshape(step, 2, SPLIT, 16, LANES)
    left = jnp.concatenate(
        [raw[:, :, sub].reshape(step * 32, LANES) for sub in range(SPLIT)], axis=1
    )
    spread = dot32(left, looks[...], NN)
    for at in range(step):
        base = pl.multiple_of((slot + at) * 128, 128)
        for group in range(2):
            for rlook in range(LOOKR):
                top = (at * 2 + group) * 16 + rlook * 8
                for look in range(LOOKC):
                    planes[pl.ds(base + (rlook * LOOKC + look) * 16 + group * 8, 8), :] = spread[
                        top : top + 8, look * LANES : (look + 1) * LANES
                    ]
        for k in range(share):
            found = choose(start + at * share + k, found)
    return found


def pair_kernel(pair_count, with_halo, step, *refs):
    if with_halo:
        (listed, counts, images, halo, looks, series, weights, raw, raw_halo, planes, sems) = refs
    else:
        (pairs, images, looks, series, listed, counts, raw, planes, sems, sums) = refs
    dates = images.shape[0]
    steps = dates // step
    me = lax.axis_index("dates")
    row_start = 8 * (me if with_halo else 1 - me)
    own_slot, halo_slot = GAP * me, dates * (1 - me)
    copies = [
        pltpu.make_async_copy(
            images.at[pl.ds(at * step, step), pl.ds(row_start, 8)],
            raw.at[pl.ds(at * step, step)],
            sems.at[at],
        )
        for at in range(steps)
    ]
    if with_halo:
        copies.append(pltpu.make_async_copy(halo, raw_halo, sems.at[steps]))
    for copy in copies:
        copy.start()

    total = series if with_halo else sums
    spare = dates + GAP
    total[...] = jnp.zeros_like(total)
    planes[pl.ds(spare * 128, 128), :] = jnp.zeros((128, LANES), jnp.float32)

    second_list = pair_count + UNROLL

    def choose(at, found):
        packed = pairs[at]
        listed[found[0]] = packed
        listed[second_list + found[1]] = packed
        return (found[0] + ((packed >> 20) & 1), found[1] + (packed >> 21))

    found = (jnp.int32(0), jnp.int32(0))
    share = 0 if with_halo else pair_count // dates
    for at in range(steps):
        copies[at].wait()
        found = spread_looks(
            raw, at * step, own_slot + at * step, step, looks, planes,
            choose, at * step * share, share, found,
        )
    if not with_halo:
        for at in range(dates * share, pair_count):
            found = choose(at, found)
        for part in range(2):
            counts[part] = found[part]
            for at in range(UNROLL):
                listed[part * second_list + found[part] + at] = jnp.int32(spare * 1025)
    if with_halo:
        copies[steps].wait()
        spread_looks(raw_halo, 0, halo_slot, GAP, looks, planes)

    def one_pair(packed, power):
        first = packed & 1023
        second = (packed >> 10) & 1023
        a_row = pl.multiple_of(first * 128, 128)
        b_row = pl.multiple_of(second * 128, 128)
        terms_re, terms_im = [], []
        for look in range(LOOKR * LOOKC):
            a_re = planes[pl.ds(a_row + look * 16, 8, stride=2), :]
            a_im = planes[pl.ds(a_row + look * 16 + 1, 8, stride=2), :]
            b_re = planes[pl.ds(b_row + look * 16, 8, stride=2), :]
            b_im = planes[pl.ds(b_row + look * 16 + 1, 8, stride=2), :]
            terms_re.append(a_re * b_re + a_im * b_im)
            terms_im.append(a_im * b_re - a_re * b_im)
        while len(terms_re) > 1:
            terms_re = [terms_re[k] + terms_re[k + 1] for k in range(0, len(terms_re), 2)]
            terms_im = [terms_im[k] + terms_im[k + 1] for k in range(0, len(terms_im), 2)]
        real = terms_re[0].astype(jnp.bfloat16).astype(jnp.float32)
        imag = terms_im[0].astype(jnp.bfloat16).astype(jnp.float32)
        a_at = pl.multiple_of(first * 16, 16)
        b_at = pl.multiple_of(second * 16, 16)
        total[pl.ds(a_at, 8), :] += real
        total[pl.ds(a_at + 8, 8), :] += imag
        total[pl.ds(b_at, 8), :] -= real
        total[pl.ds(b_at + 8, 8), :] -= imag
        return power + (real * real + imag * imag)

    power = jnp.zeros((8, LANES), jnp.float32)
    for part in range(2 if with_halo else 1):

        def some_pairs(at, power, part=part):
            for k in range(UNROLL):
                power = one_pair(listed[part * second_list + at * UNROLL + k], power)
            return power

        power = lax.fori_loop(0, (counts[part] + UNROLL - 1) // UNROLL, some_pairs, power)
    scale = 1.0 / float(LOOKR * LOOKC)
    if with_halo:
        weights[...] = power * (scale * scale / float(pair_count))
    else:
        def narrow(date, carry):
            value = sums[pl.ds(pl.multiple_of((own_slot + date) * 16, 16), 16), :] * scale + carry
            rounded = value.astype(jnp.bfloat16)
            series[pl.ds(pl.multiple_of(date * 16, 16), 16), :] = rounded
            return value - rounded.astype(jnp.float32)

        lax.fori_loop(0, dates, narrow, jnp.zeros((16, LANES), jnp.float32), unroll=4)
        high, low = split_bf16(power * (scale * scale / float(pair_count)))
        series[pl.ds(dates * 16, 16), :] = jnp.concatenate(
            [high.astype(jnp.float32), low.astype(jnp.float32)], axis=0
        ).astype(jnp.bfloat16)


def in_vmem():
    return pl.BlockSpec(memory_space=pltpu.VMEM)


def in_smem():
    return pl.BlockSpec(memory_space=pltpu.SMEM)


def in_hbm():
    return pl.BlockSpec(memory_space=pl.ANY)


def call_pairs(pairs, images, looks, given=None):
    dates = images.shape[0]
    pair_count = pairs.shape[0]
    step = max(k for k in range(1, MAX_STEP + 1) if dates % k == 0)
    slots = dates + GAP + 1
    scratch = [
        pltpu.VMEM((dates, 8, 16, LANES), jnp.bfloat16),
        pltpu.VMEM((slots * 128, LANES), jnp.float32),
        pltpu.SemaphoreType.DMA((dates // step + 1,)),
    ]
    sums = jax.ShapeDtypeStruct((slots * 16, LANES), jnp.float32)
    if given is not None:
        halo, listed, counts = given
        out_shape = (sums, jax.ShapeDtypeStruct((8, LANES), jnp.float32))
        scratch.insert(1, pltpu.VMEM((GAP, 8, 16, LANES), jnp.bfloat16))
        in_specs = [in_smem()] * 2 + [in_hbm(), in_hbm(), in_vmem()]
        out_specs = (in_vmem(), in_vmem())
        args = (listed, counts, images, halo, looks)
    else:
        out_shape = (
            jax.ShapeDtypeStruct(((dates + 1) * 16, LANES), jnp.bfloat16),
            jax.ShapeDtypeStruct((2 * (pair_count + UNROLL),), jnp.int32),
            jax.ShapeDtypeStruct((2,), jnp.int32),
        )
        scratch.append(pltpu.VMEM(sums.shape, sums.dtype))
        in_specs = [in_smem(), in_hbm(), in_vmem()]
        out_specs = (in_vmem(), in_smem(), in_smem())
        args = (pairs, images, looks)
    return pl.pallas_call(
        lambda *refs: pair_kernel(pair_count, given is not None, step, *refs),
        out_shape=out_shape,
        in_specs=in_specs,
        out_specs=out_specs,
        scratch_shapes=scratch,
        compiler_params=pltpu.CompilerParams(vmem_limit_bytes=PAIR_VMEM),
        cost_estimate=pl.CostEstimate(
            flops=pair_count * 70 * 1024, bytes_accessed=pair_count * 48 * 1024, transcendentals=0
        ),
        name="pairs_other" if given is None else "pairs_own",
    )(*args)


def half_basis(row_start, col_start, row_total, col_total):
    sub = lax.broadcasted_iota(jnp.int32, (8, LANES), 0)
    lane = lax.broadcasted_iota(jnp.int32, (8, LANES), 1)
    width = LANES // SPLIT
    row = row_start + (sub // SPLIT) * SPLIT + lane // width
    col = col_start + (sub % SPLIT) * width + lane % width
    return centred(row, row_total), centred(col, col_total)


def centred(place, total):
    return (2.0 * place.astype(jnp.float32) + 1.0) / float(total) - 1.0


def combine_kernel(dates, row_total, col_total, *refs):
    (own, own_weights, other, high, low, moments, full, weighted_rows) = refs
    me = lax.axis_index("dates")
    count = dates * 2
    span = dates + GAP
    scale = 1.0 / float(LOOKR * LOOKC)

    def rows(start, size):
        return pl.ds(pl.multiple_of(start * 16, 16), size * 16)

    full[rows((dates - GAP) * me, span), :] = own[pl.ds(0, span * 16), :] * scale
    rest = dates - GAP
    full[rows(span * (1 - me), rest), :] = other[rows(GAP * (1 - me), rest), :].astype(jnp.float32)
    full[rows(dates - GAP * me, GAP), :] += other[rows(rest * me, GAP), :].astype(jnp.float32)
    y_plane, x_plane = half_basis(8 * me, LANES * lax.axis_index("cols"), row_total, col_total)
    basis = (jnp.ones((8, LANES), jnp.float32), y_plane, x_plane)
    padded = full.shape[0] // 16
    full[pl.ds(count * 16, (padded - count) * 16), :] = jnp.zeros(
        ((padded - count) * 16, LANES), jnp.float32
    )
    for at in range(3):
        full[pl.ds((count + at) * 16, 8), :] = basis[at]
    sent = other[pl.ds(dates * 16, 16), :].astype(jnp.float32)
    weights = own_weights[...] + (sent[:8] + sent[8:])
    weighted_rows[...] = jnp.zeros_like(weighted_rows)
    for at in range(3):
        plane = weights * basis[at]
        for part in range(2):
            for sub in range(8):
                weighted_rows[part * 3 + at : part * 3 + at + 1, pl.ds((part * 8 + sub) * LANES, LANES)] = (
                    plane[sub : sub + 1]
                )
    for at in range(16):
        value = full[pl.ds(at, padded, stride=16), :]
        upper, lower = split_bf16(value)
        high[:, at * LANES : (at + 1) * LANES] = upper
        low[:, at * LANES : (at + 1) * LANES] = lower
    upper, lower = split_bf16(weighted_rows[...])
    moments[...] = (
        dot32(upper, high[...], NT) + dot32(lower, high[...], NT) + dot32(upper, low[...], NT)
    )


def call_combine(own, own_weights, other, dates, row_total, col_total):
    padded = pad_dates(dates * 2)
    wide = jax.ShapeDtypeStruct((padded, 16 * LANES), jnp.bfloat16)
    return pl.pallas_call(
        lambda *refs: combine_kernel(dates, row_total, col_total, *refs),
        out_shape=(wide, wide, jax.ShapeDtypeStruct((8, padded), jnp.float32)),
        in_specs=[in_vmem()] * 3,
        out_specs=(in_vmem(),) * 3,
        scratch_shapes=[
            pltpu.VMEM((padded * 16, LANES), jnp.float32),
            pltpu.VMEM((8, 16 * LANES), jnp.float32),
        ],
        compiler_params=pltpu.CompilerParams(vmem_limit_bytes=SMALL_VMEM),
        cost_estimate=pl.CostEstimate(flops=padded * 8 * 12288, bytes_accessed=16 << 20, transcendentals=0),
        name="combine",
    )(own, own_weights, other)


def pad_dates(count):
    return (count + 3 + 15) // 16 * 16


def inverse_kernel(pairs, high, low, state, residual, normal_high, normal_low):
    padded = high.shape[0]
    date = lax.broadcasted_iota(jnp.int32, (padded, pairs.shape[1]), 0)
    design = (
        jnp.where(date == pairs[0:1, :], 1.0, 0.0) - jnp.where(date == pairs[1:2, :], 1.0, 0.0)
    ).astype(jnp.bfloat16)
    eye = jnp.where(
        lax.broadcasted_iota(jnp.int32, (padded, padded), 0)
        == lax.broadcasted_iota(jnp.int32, (padded, padded), 1),
        1.0,
        0.0,
    )
    normal = dot32(design, design, NT) + RIDGE * eye
    normal_high[...], normal_low[...] = split_bf16(normal)
    largest = jnp.max(jnp.sum(jnp.abs(normal), axis=1))
    careful = largest > 128.0
    scale, error = centre((largest - RIDGE) / (largest + RIDGE))
    start = 2.0 / (largest + RIDGE)
    state[...] = (scale * start) * (2.0 * eye - start * normal)

    def step(scale):
        now, rest = split_bf16(state[...])
        residual[...] = eye - dot32(normal_high[...], now, NN) - dot32(normal_high[...], rest, NN)

        @pl.when(careful)
        def _():
            residual[...] -= dot32(normal_low[...], now, NN)

        upper, lower = split_bf16(residual[...])
        change = dot32(now, upper, NN)
        state[...] = scale * (state[...] + change)

        @pl.when(careful)
        def _():
            state[...] += scale * (dot32(now, lower, NN) + dot32(rest, upper, NN))

    def body(error):
        scale, left = centre(error)
        step(scale)
        return jnp.maximum(left, 0.05 * error)

    lax.while_loop(lambda error: error > 5e-4, body, error)
    step(jnp.float32(1.0))
    high[...], low[...] = split_bf16(state[...])


def centre(error):
    scale = 2.0 / (2.0 - error * error)
    return scale, scale - 1.0


def call_inverse(pair_rows, count):
    padded = pad_dates(count)
    square = jax.ShapeDtypeStruct((padded, padded), jnp.bfloat16)
    return pl.pallas_call(
        inverse_kernel,
        out_shape=(square, square),
        in_specs=[in_vmem()],
        out_specs=(in_vmem(),) * 2,
        scratch_shapes=[
            pltpu.VMEM((padded, padded), jnp.float32),
            pltpu.VMEM((padded, padded), jnp.float32),
            pltpu.VMEM((padded, padded), jnp.bfloat16),
            pltpu.VMEM((padded, padded), jnp.bfloat16),
        ],
        compiler_params=pltpu.CompilerParams(vmem_limit_bytes=SMALL_VMEM),
        cost_estimate=pl.CostEstimate(flops=50 * padded**3, bytes_accessed=24 << 20, transcendentals=0),
        name="inverse",
    )(pair_rows)


def solve_kernel(inverse_high, inverse_low, high, low, series):
    padded = high.shape[0]
    lane = lax.broadcasted_iota(jnp.int32, (padded, LANES), 1)
    width = LANES // SPLIT
    for group in range(4):
        cols = pl.ds(group * SPLIT * LANES, SPLIT * LANES)
        solved = (
            dot32(inverse_high[...], high[:, cols], NN)
            + dot32(inverse_high[...], low[:, cols], NN)
            + dot32(inverse_low[...], high[:, cols], NN)
        )
        blocks = [solved[:, k * LANES : (k + 1) * LANES] for k in range(SPLIT)]
        for bit in (1, 2):
            shift = bit * width
            even = (lane // shift) % 2 == 0
            swapped = list(blocks)
            for k in range(SPLIT):
                if k & bit == 0:
                    first, second = blocks[k], blocks[k | bit]
                    swapped[k] = jnp.where(even, first, pltpu.roll(second, shift, 1))
                    swapped[k | bit] = jnp.where(even, pltpu.roll(first, LANES - shift, 1), second)
            blocks = swapped
        part, half = group // 2, group % 2
        for k in range(SPLIT):
            series[(half * SPLIT + k) * 2 + part] = blocks[k]


def call_solve(inverse, values):
    padded = values[0].shape[0]
    return pl.pallas_call(
        solve_kernel,
        out_shape=jax.ShapeDtypeStruct((16, padded, LANES), jnp.float32),
        in_specs=[in_vmem()] * 4,
        out_specs=in_vmem(),
        compiler_params=pltpu.CompilerParams(vmem_limit_bytes=SMALL_VMEM),
        cost_estimate=pl.CostEstimate(
            flops=6 * padded * padded * 16 * LANES, bytes_accessed=20 << 20, transcendentals=0
        ),
        name="solve",
    )(*inverse, *values)


def refine_kernel(count, row_total, col_total, *refs):
    (series, moments, inverse_high, inverse_low, refined) = refs
    padded = series.shape[1]
    normal = [
        [moments[at : at + 1, count + k : count + k + 1] for k in range(3)] for at in range(3)
    ]

    def cyclic(row_at, col_at):
        a, b = (row_at + 1) % 3, (row_at + 2) % 3
        c, d = (col_at + 1) % 3, (col_at + 2) % 3
        return normal[a][c] * normal[b][d] - normal[a][d] * normal[b][c]

    cofacts = [[cyclic(row_at, col_at) for col_at in range(3)] for row_at in range(3)]
    determinant = sum(normal[0][k] * cofacts[0][k] for k in range(3))
    rows = []
    for part in range(2):
        for at in range(3):
            rows.append(
                sum(
                    (cofacts[k][at] / determinant) * moments[part * 3 + k : part * 3 + k + 1, :]
                    for k in range(3)
                )
            )
    rows.append(jnp.zeros((2, padded), jnp.float32))
    upper, lower = split_bf16(jnp.concatenate(rows, axis=0))
    ramps = (
        dot32(inverse_high[...], upper, NT)
        + dot32(inverse_high[...], lower, NT)
        + dot32(inverse_low[...], upper, NT)
    )[:count]
    lane = lax.broadcasted_iota(jnp.int32, (1, LANES), 1)
    x_row = centred(LANES * lax.axis_index("cols") + lane, col_total)
    row_start = 8 * lax.axis_index("dates")
    for part in range(2):
        level, along_y, along_x = (
            jnp.broadcast_to(ramps[:, part * 3 + at : part * 3 + at + 1], (count, LANES))
            for at in range(3)
        )
        level = level + along_x * x_row
        for row in range(8):
            y = centred(row_start + row, row_total)
            refined[pl.ds(row * 2 + part, count, stride=16), :] = series[row * 2 + part, :count] - (
                level + along_y * y
            )


def call_refine(series, moments, inverse, count, row_total, col_total):
    return pl.pallas_call(
        lambda *refs: refine_kernel(count, row_total, col_total, *refs),
        out_shape=jax.ShapeDtypeStruct((count * 16, LANES), jnp.float32),
        in_specs=[in_vmem()] * 4,
        out_specs=in_vmem(),
        compiler_params=pltpu.CompilerParams(vmem_limit_bytes=SMALL_VMEM),
        cost_estimate=pl.CostEstimate(flops=count * 16 * LANES * 6, bytes_accessed=16 << 20, transcendentals=0),
        name="refine",
    )(series, moments, *inverse)


def sum_devices(value):
    cols = lax.axis_size("cols")
    if cols & (cols - 1):
        return lax.psum(value, ("dates", "cols"))
    bit = 1
    while bit < cols:
        value = value + lax.ppermute(value, "cols", [(at, at ^ bit) for at in range(cols)])
        bit *= 2
        if bit == 2:
            value = value + swap_dates(value)
    return value


def swap_dates(value):
    return lax.ppermute(value, "dates", [(0, 1), (1, 0)])


def two_halves(complex_images, pair_list):
    dates, rows, _, cols = complex_images.shape
    me = lax.axis_index("dates")
    half = rows // LOOKR // 2
    row_total, col_total = half * 2, cols // LOOKC * lax.axis_size("cols")
    images = complex_images.reshape(dates, rows, 2, SPLIT, cols // SPLIT)
    images = images.transpose(0, 1, 3, 2, 4).reshape(dates, rows // LOOKR, 16, LANES)
    first, second = pair_list[:, 0], pair_list[:, 1]
    low, base = dates * me, (dates - GAP) * me
    first_own = (first >= low) & (first < low + dates)
    second_own = (second >= low) & (second < low + dates)
    inside = (first_own & second_own).astype(jnp.int32)
    across = (first_own ^ second_own).astype(jnp.int32)
    packed = (first - base) | ((second - base) << 10)
    packed = jnp.where(first_own | second_own, packed | (inside << 20) | (across << 21), 0)

    edge = lax.dynamic_slice(
        images, ((dates - GAP) * (1 - me), half * (1 - me), 0, 0), (GAP, half, 16, LANES)
    )
    edge, pair_rows = lax.optimization_barrier((edge, pair_list.T))
    halo = swap_dates(edge)
    inverse = call_inverse(pair_rows, dates * 2)
    halo, inverse, packed = lax.optimization_barrier((halo, inverse, packed))
    looks = jnp.asarray(look_matrix(), jnp.bfloat16)
    other, listed, counts = call_pairs(packed, images, looks)
    other = swap_dates(other)
    own, own_weights = call_pairs(packed, images, looks, (halo, listed, counts))
    high, lowpart, moments = call_combine(own, own_weights, other, dates, row_total, col_total)
    moments = sum_devices(moments)
    series = call_solve(inverse, (high, lowpart))
    refined = call_refine(series, moments, inverse, dates * 2, row_total, col_total)
    return refined.reshape(dates * 2, half, 2, LANES)


highest = lax.Precision.HIGHEST


def pseudo_inverse(pair_list, count):
    date_ids = jnp.arange(count, dtype=jnp.int32)
    design = (pair_list[:, 0:1] == date_ids[None, :]).astype(jnp.float32) - (
        pair_list[:, 1:2] == date_ids[None, :]
    ).astype(jnp.float32)
    normal = jnp.dot(design.T, design, precision=highest) + RIDGE * jnp.eye(
        count, dtype=jnp.float32
    )
    factor = jnp.linalg.cholesky(normal)
    return jax.scipy.linalg.cho_solve((factor, True), design.T)


def pool_looks(plane):
    count, rows, cols = plane.shape
    rows_pooled = jnp.sum(plane.reshape(count, rows // LOOKR, LOOKR, cols), axis=2)
    return jnp.sum(rows_pooled.reshape(count, rows // LOOKR, cols // LOOKC, LOOKC), axis=3)


def multilook_pairs(tile_stack, pair_list, pair_block):
    real_planes = tile_stack[:, :, 0, :]
    imag_planes = tile_stack[:, :, 1, :]
    groups = pair_list.reshape(-1, pair_block, 2)
    scale = 1.0 / float(LOOKR * LOOKC)

    def one_group(group):
        first_real = jnp.take(real_planes, group[:, 0], axis=0).astype(jnp.float32)
        first_imag = jnp.take(imag_planes, group[:, 0], axis=0).astype(jnp.float32)
        second_real = jnp.take(real_planes, group[:, 1], axis=0).astype(jnp.float32)
        second_imag = jnp.take(imag_planes, group[:, 1], axis=0).astype(jnp.float32)
        real_part = pool_looks(first_real * second_real + first_imag * second_imag)
        imag_part = pool_looks(first_imag * second_real - first_real * second_imag)
        return (jnp.stack([real_part, imag_part], axis=2) * scale).astype(jnp.bfloat16)

    looked = lax.map(one_group, groups)
    return looked.reshape((pair_list.shape[0],) + looked.shape[2:])


def coordinates(start, count, total):
    return (2.0 * (start + jnp.arange(count, dtype=jnp.int32)).astype(jnp.float32) + 1.0) / float(
        total
    ) - 1.0


def basis_planes(row_coord, col_coord):
    constant = jnp.ones((row_coord.shape[0], col_coord.shape[0]), jnp.float32)
    return jnp.stack([constant, row_coord[:, None] * constant, col_coord[None, :] * constant])


def weighted(widened, planes, pair_count):
    weights = jnp.sum(widened * widened, axis=(0, 2)) / float(pair_count)
    weighted_planes = planes * weights[None]
    normal = jnp.einsum("jrc,krc->jk", weighted_planes, planes, precision=highest)
    return (weighted_planes, normal)


def inverse3(matrix):

    def cyclic(row_at, col_at):
        return (
            matrix[(row_at + 1) % 3, (col_at + 1) % 3] * matrix[(row_at + 2) % 3, (col_at + 2) % 3]
            - matrix[(row_at + 1) % 3, (col_at + 2) % 3]
            * matrix[(row_at + 2) % 3, (col_at + 1) % 3]
        )

    cofacts = jnp.stack(
        [jnp.stack([cyclic(row_at, col_at) for col_at in range(3)]) for row_at in range(3)]
    )
    determinant = jnp.sum(matrix[0] * cofacts[0])
    return cofacts.T / determinant


def refine(series, ramp_rhs, normal, planes):
    ramp_coef = jnp.einsum("jk,dkh->djh", inverse3(normal), ramp_rhs, precision=highest)
    return series - jnp.einsum("djh,jrc->drhc", ramp_coef, planes, precision=highest)


def any_dates(complex_images, pair_list):
    date_count = lax.axis_size("dates")
    date_index = lax.axis_index("dates")
    col_index = lax.axis_index("cols")
    pair_count = pair_list.shape[0]
    date_total = complex_images.shape[0] * date_count
    rounded_pseudo = pseudo_inverse(pair_list, date_total).astype(jnp.bfloat16)
    regrouped = lax.all_to_all(complex_images, "dates", split_axis=1, concat_axis=0, tiled=True)
    interferograms = multilook_pairs(regrouped, pair_list, PAIR_BLOCK * date_count)
    ml_rows = interferograms.shape[1]
    ml_cols = interferograms.shape[3]
    planes = basis_planes(
        coordinates(date_index * ml_rows, ml_rows, ml_rows * date_count),
        coordinates(col_index * ml_cols, ml_cols, ml_cols * lax.axis_size("cols")),
    )
    widened = interferograms.astype(jnp.float32)
    weighted_planes, normal_part = weighted(widened, planes, pair_count)
    flat_pairs = interferograms.reshape(pair_count, -1)
    series = jnp.dot(rounded_pseudo, flat_pairs, preferred_element_type=jnp.float32).reshape(
        (date_total,) + interferograms.shape[1:]
    )
    rhs_part = jnp.einsum("jrc,drhc->djh", weighted_planes, series, precision=highest)
    normal, ramp_rhs = lax.psum((normal_part, rhs_part), ("dates", "cols"))
    return refine(series, ramp_rhs, normal, planes)


def solution(mesh):
    def body(complex_images, pair_list):
        dates, rows, _, cols = complex_images.shape
        if mesh.shape["dates"] == 2 and cols == LANES * LOOKC and rows == 32 and dates >= GAP:
            return two_halves(complex_images, pair_list)
        return any_dates(complex_images, pair_list)

    return jax.shard_map(
        body,
        mesh=mesh,
        in_specs=(P("dates", None, None, "cols"), P()),
        out_specs=P(None, "dates", None, "cols"),
        check_vma=False,
    )
```

```python
import jax
import jax.numpy as jnp
import numpy as np
from jax import lax
from jax.experimental import pallas as pl
from jax.experimental.pallas import tpu as pltpu
from jax.sharding import PartitionSpec as P

LOOKR = 2
LOOKC = 4
PAIR_BLOCK = 37
GAP = 12
RIDGE = 0.5
MAX_STEP = 40
UNROLL = 8
LANES = 128
SPLIT = 4
SOME_STEPS = 3
PAIR_VMEM = 52 * 1024 * 1024
OWN_VMEM = 32 * 1024 * 1024
SMALL_VMEM = 12 * 1024 * 1024
NN = (((1,), (0,)), ((), ()))
NT = (((1,), (1,)), ((), ()))


def look_matrix():
    row = np.arange(SPLIT * LANES)
    lane, sub = row % LANES, row // LANES
    target = (lane % LOOKC) * LANES + sub * (LANES // SPLIT) + lane // LOOKC
    return (target[:, None] == row[None, :]).astype(np.float32)


def split_bf16(value):
    high = value.astype(jnp.bfloat16)
    return high, (value - high.astype(jnp.float32)).astype(jnp.bfloat16)


def dot32(first, second, dims):
    return lax.dot_general(first, second, dims, preferred_element_type=jnp.float32)


def spread_looks(source, row, date, slot, step, looks, planes, choose=None, start=0, share=0, found=None):
    raw = source[pl.ds(date, step), pl.ds(row, 8)].reshape(step, 2, SPLIT, 16, LANES)
    left = jnp.concatenate(
        [raw[:, :, sub].reshape(step * 32, LANES) for sub in range(SPLIT)], axis=1
    )
    spread = dot32(left, looks[...], NN)
    for at in range(step):
        base = pl.multiple_of((slot + at) * 128, 128)
        for group in range(2):
            for rlook in range(LOOKR):
                top = (at * 2 + group) * 16 + rlook * 8
                for look in range(LOOKC):
                    planes[pl.ds(base + (rlook * LOOKC + look) * 16 + group * 8, 8), :] = spread[
                        top : top + 8, look * LANES : (look + 1) * LANES
                    ]
        for k in range(share):
            found = choose(start + at * share + k, found)
    return found


def pair_kernel(pair_count, with_halo, step, *refs):
    if with_halo:
        (listed, counts, images, halo, looks, series, weights, planes) = refs
    else:
        (pairs, images, looks, series, listed, counts, raw, planes, sems, sums) = refs
    dates = images.shape[0]
    steps = dates // step
    me = lax.axis_index("dates")
    row_start = 8 * (me if with_halo else 1 - me)
    own_slot, halo_slot = GAP * me, dates * (1 - me)
    copies = []
    if not with_halo:
        for at in range(steps):
            part = pl.ds(at * step, step)
            copies.append(
                pltpu.make_async_copy(images.at[part, pl.ds(row_start, 8)], raw.at[part], sems.at[at])
            )
    for copy in copies:
        copy.start()

    total = series if with_halo else sums
    spare = dates + GAP
    total[...] = jnp.zeros_like(total)
    planes[pl.ds(spare * 128, 128), :] = jnp.zeros((128, LANES), jnp.float32)

    second_list = pair_count + UNROLL

    def choose(at, found):
        packed = pairs[at]
        listed[found[0]] = packed
        listed[second_list + found[1]] = packed
        return (found[0] + ((packed >> 20) & 1), found[1] + (packed >> 21))

    found = (jnp.int32(0), jnp.int32(0))
    share = 0 if with_halo else pair_count // dates
    for at in range(steps):
        if with_halo:
            source, row = images, row_start
        else:
            copies[at].wait()
            source, row = raw, 0
        found = spread_looks(
            source, row, at * step, own_slot + at * step, step, looks, planes,
            choose, at * step * share, share, found,
        )
    if not with_halo:
        for at in range(dates * share, pair_count):
            found = choose(at, found)
        for part in range(2):
            counts[part] = found[part]
            for at in range(UNROLL):
                listed[part * second_list + found[part] + at] = jnp.int32(spare * 1025)
    if with_halo:
        spread_looks(halo, 0, 0, halo_slot, GAP, looks, planes)

    def one_pair(packed, power):
        first = packed & 1023
        second = (packed >> 10) & 1023
        a_row = pl.multiple_of(first * 128, 128)
        b_row = pl.multiple_of(second * 128, 128)
        terms_re, terms_im = [], []
        for look in range(LOOKR * LOOKC):
            a_re = planes[pl.ds(a_row + look * 16, 8, stride=2), :]
            a_im = planes[pl.ds(a_row + look * 16 + 1, 8, stride=2), :]
            b_re = planes[pl.ds(b_row + look * 16, 8, stride=2), :]
            b_im = planes[pl.ds(b_row + look * 16 + 1, 8, stride=2), :]
            terms_re.append(a_re * b_re + a_im * b_im)
            terms_im.append(a_im * b_re - a_re * b_im)
        while len(terms_re) > 1:
            terms_re = [terms_re[k] + terms_re[k + 1] for k in range(0, len(terms_re), 2)]
            terms_im = [terms_im[k] + terms_im[k + 1] for k in range(0, len(terms_im), 2)]
        real = terms_re[0].astype(jnp.bfloat16).astype(jnp.float32)
        imag = terms_im[0].astype(jnp.bfloat16).astype(jnp.float32)
        a_at = pl.multiple_of(first * 16, 16)
        b_at = pl.multiple_of(second * 16, 16)
        total[pl.ds(a_at, 8), :] += real
        total[pl.ds(a_at + 8, 8), :] += imag
        total[pl.ds(b_at, 8), :] -= real
        total[pl.ds(b_at + 8, 8), :] -= imag
        return power + (real * real + imag * imag)

    power = jnp.zeros((8, LANES), jnp.float32)
    for part in range(2 if with_halo else 1):

        def some_pairs(at, power, part=part):
            for k in range(UNROLL):
                power = one_pair(listed[part * second_list + at * UNROLL + k], power)
            return power

        power = lax.fori_loop(0, (counts[part] + UNROLL - 1) // UNROLL, some_pairs, power)
    scale = 1.0 / float(LOOKR * LOOKC)
    if with_halo:
        weights[...] = power * (scale * scale / float(pair_count))
    else:
        def narrow(date, carry):
            value = sums[pl.ds(pl.multiple_of((own_slot + date) * 16, 16), 16), :] * scale + carry
            rounded = value.astype(jnp.bfloat16)
            series[pl.ds(pl.multiple_of(date * 16, 16), 16), :] = rounded
            return value - rounded.astype(jnp.float32)

        lax.fori_loop(0, dates, narrow, jnp.zeros((16, LANES), jnp.float32), unroll=4)
        high, low = split_bf16(power * (scale * scale / float(pair_count)))
        series[pl.ds(dates * 16, 16), :] = jnp.concatenate(
            [high.astype(jnp.float32), low.astype(jnp.float32)], axis=0
        ).astype(jnp.bfloat16)


def in_vmem():
    return pl.BlockSpec(memory_space=pltpu.VMEM)


def in_smem():
    return pl.BlockSpec(memory_space=pltpu.SMEM)


def in_hbm():
    return pl.BlockSpec(memory_space=pl.ANY)


def call_pairs(pairs, images, looks, given=None):
    dates = images.shape[0]
    pair_count = pairs.shape[0]
    step = max(k for k in range(1, MAX_STEP + 1) if dates % k == 0)
    slots = dates + GAP + 1
    scratch = [pltpu.VMEM((slots * 128, LANES), jnp.float32)]
    sums = jax.ShapeDtypeStruct((slots * 16, LANES), jnp.float32)
    if given is not None:
        halo, listed, counts = given
        out_shape = (sums, jax.ShapeDtypeStruct((8, LANES), jnp.float32))
        in_specs = [in_smem()] * 2 + [in_vmem()] * 3
        out_specs = (in_vmem(), in_vmem())
        args = (listed, counts, images, halo, looks)
    else:
        out_shape = (
            jax.ShapeDtypeStruct(((dates + 1) * 16, LANES), jnp.bfloat16),
            jax.ShapeDtypeStruct((2 * (pair_count + UNROLL),), jnp.int32),
            jax.ShapeDtypeStruct((2,), jnp.int32),
        )
        scratch = [pltpu.VMEM((dates, 8, 16, LANES), jnp.bfloat16)] + scratch
        scratch += [pltpu.SemaphoreType.DMA((dates // step,)), pltpu.VMEM(sums.shape, sums.dtype)]
        in_specs = [in_smem(), in_hbm(), in_vmem()]
        out_specs = (in_vmem(), in_smem(), in_smem())
        args = (pairs, images, looks)
    return pl.pallas_call(
        lambda *refs: pair_kernel(pair_count, given is not None, step, *refs),
        out_shape=out_shape,
        in_specs=in_specs,
        out_specs=out_specs,
        scratch_shapes=scratch,
        compiler_params=pltpu.CompilerParams(vmem_limit_bytes=PAIR_VMEM if given is None else OWN_VMEM),
        cost_estimate=pl.CostEstimate(
            flops=pair_count * 70 * 1024, bytes_accessed=pair_count * 48 * 1024, transcendentals=0
        ),
        name="pairs_other" if given is None else "pairs_own",
    )(*args)


def half_basis(row_start, col_start, row_total, col_total):
    sub = lax.broadcasted_iota(jnp.int32, (8, LANES), 0)
    lane = lax.broadcasted_iota(jnp.int32, (8, LANES), 1)
    width = LANES // SPLIT
    row = row_start + (sub // SPLIT) * SPLIT + lane // width
    col = col_start + (sub % SPLIT) * width + lane % width
    return centred(row, row_total), centred(col, col_total)


def centred(place, total):
    return (2.0 * place.astype(jnp.float32) + 1.0) / float(total) - 1.0


def combine_kernel(dates, row_total, col_total, *refs):
    (own, own_weights, other, high, low, moments, full, weighted_rows) = refs
    me = lax.axis_index("dates")
    count = dates * 2
    span = dates + GAP
    scale = 1.0 / float(LOOKR * LOOKC)

    def rows(start, size):
        return pl.ds(pl.multiple_of(start * 16, 16), size * 16)

    full[rows((dates - GAP) * me, span), :] = own[pl.ds(0, span * 16), :] * scale
    rest = dates - GAP
    full[rows(span * (1 - me), rest), :] = other[rows(GAP * (1 - me), rest), :].astype(jnp.float32)
    full[rows(dates - GAP * me, GAP), :] += other[rows(rest * me, GAP), :].astype(jnp.float32)
    y_plane, x_plane = half_basis(8 * me, LANES * lax.axis_index("cols"), row_total, col_total)
    basis = (jnp.ones((8, LANES), jnp.float32), y_plane, x_plane)
    padded = full.shape[0] // 16
    full[pl.ds(count * 16, (padded - count) * 16), :] = jnp.zeros(
        ((padded - count) * 16, LANES), jnp.float32
    )
    for at in range(3):
        full[pl.ds((count + at) * 16, 8), :] = basis[at]
    sent = other[pl.ds(dates * 16, 16), :].astype(jnp.float32)
    weights = own_weights[...] + (sent[:8] + sent[8:])
    weighted_rows[...] = jnp.zeros_like(weighted_rows)
    for at in range(3):
        plane = weights * basis[at]
        for part in range(2):
            for sub in range(8):
                weighted_rows[part * 3 + at : part * 3 + at + 1, pl.ds((part * 8 + sub) * LANES, LANES)] = (
                    plane[sub : sub + 1]
                )
    for at in range(16):
        value = full[pl.ds(at, padded, stride=16), :]
        upper, lower = split_bf16(value)
        high[:, at * LANES : (at + 1) * LANES] = upper
        low[:, at * LANES : (at + 1) * LANES] = lower
    upper, lower = split_bf16(weighted_rows[...])
    moments[...] = (
        dot32(upper, high[...], NT) + dot32(lower, high[...], NT) + dot32(upper, low[...], NT)
    )


def call_combine(own, own_weights, other, dates, row_total, col_total):
    padded = pad_dates(dates * 2)
    wide = jax.ShapeDtypeStruct((padded, 16 * LANES), jnp.bfloat16)
    return pl.pallas_call(
        lambda *refs: combine_kernel(dates, row_total, col_total, *refs),
        out_shape=(wide, wide, jax.ShapeDtypeStruct((8, padded), jnp.float32)),
        in_specs=[in_vmem()] * 3,
        out_specs=(in_vmem(),) * 3,
        scratch_shapes=[
            pltpu.VMEM((padded * 16, LANES), jnp.float32),
            pltpu.VMEM((8, 16 * LANES), jnp.float32),
        ],
        compiler_params=pltpu.CompilerParams(vmem_limit_bytes=SMALL_VMEM),
        cost_estimate=pl.CostEstimate(flops=padded * 8 * 12288, bytes_accessed=16 << 20, transcendentals=0),
        name="combine",
    )(own, own_weights, other)


def pad_dates(count):
    return (count + 3 + 15) // 16 * 16


def start_inverse_kernel(pairs, state, normal_high, normal_low, progress):
    padded = state.shape[0]
    date = lax.broadcasted_iota(jnp.int32, (padded, pairs.shape[1]), 0)
    design = (
        jnp.where(date == pairs[0:1, :], 1.0, 0.0) - jnp.where(date == pairs[1:2, :], 1.0, 0.0)
    ).astype(jnp.bfloat16)
    eye = unit(padded)
    normal = dot32(design, design, NT) + RIDGE * eye
    normal_high[...], normal_low[...] = split_bf16(normal)
    largest = jnp.max(jnp.sum(jnp.abs(normal), axis=1))
    scale, error = centre((largest - RIDGE) / (largest + RIDGE))
    first = 2.0 / (largest + RIDGE)
    state[...] = (scale * first) * (2.0 * eye - first * normal)
    progress[0] = error
    progress[1] = largest


def go_on_inverse_kernel(last, state, normal_high, normal_low, progress, *refs):
    residual, now_state = refs[-2:]
    eye = unit(state.shape[0])
    careful = progress[1] > 128.0
    now_state[...] = state[...]

    def step(scale):
        now, rest = split_bf16(now_state[...])
        residual[...] = eye - dot32(normal_high[...], now, NN) - dot32(normal_high[...], rest, NN)

        @pl.when(careful)
        def _():
            residual[...] -= dot32(normal_low[...], now, NN)

        upper, lower = split_bf16(residual[...])
        change = dot32(now, upper, NN)
        now_state[...] = scale * (now_state[...] + change)

        @pl.when(careful)
        def _():
            now_state[...] += scale * (dot32(now, lower, NN) + dot32(rest, upper, NN))

    def unfinished(carry):
        return (carry[0] > 5e-4) & (last | (carry[1] < SOME_STEPS))

    def body(carry):
        error, count = carry
        scale, left = centre(error)
        step(scale)
        return jnp.maximum(left, 0.05 * error), count + 1

    error, _ = lax.while_loop(unfinished, body, (progress[0], jnp.int32(0)))
    if last:
        step(jnp.float32(1.0))
        refs[0][...], refs[1][...] = split_bf16(now_state[...])
    else:
        refs[0][...] = now_state[...]
        refs[1][0] = error
        refs[1][1] = progress[1]


def unit(size):
    row = lax.broadcasted_iota(jnp.int32, (size, size), 0)
    return jnp.where(row == lax.broadcasted_iota(jnp.int32, (size, size), 1), 1.0, 0.0)


def centre(error):
    scale = 2.0 / (2.0 - error * error)
    return scale, scale - 1.0


def inverse_call(kernel, out_shape, out_specs, scratch, name, args):
    return pl.pallas_call(
        kernel,
        out_shape=out_shape,
        in_specs=[in_vmem()] * min(len(args), 3) + [in_smem()] * (len(args) - 3),
        out_specs=out_specs,
        scratch_shapes=scratch,
        compiler_params=pltpu.CompilerParams(vmem_limit_bytes=SMALL_VMEM),
        cost_estimate=pl.CostEstimate(flops=1 << 30, bytes_accessed=8 << 20, transcendentals=0),
        name=name,
    )(*args)


def start_inverse(pair_rows, count):
    padded = pad_dates(count)
    full = jax.ShapeDtypeStruct((padded, padded), jnp.float32)
    half = jax.ShapeDtypeStruct((padded, padded), jnp.bfloat16)
    progress = jax.ShapeDtypeStruct((2,), jnp.float32)
    return inverse_call(
        start_inverse_kernel,
        (full, half, half, progress),
        (in_vmem(), in_vmem(), in_vmem(), in_smem()),
        [],
        "start_inverse",
        (pair_rows,),
    )


def go_on_inverse(state, normal_high, normal_low, progress, last):
    out_shape = (normal_high, normal_high) if last else (state, progress)
    full = pltpu.VMEM(state.shape, jnp.float32)
    return inverse_call(
        lambda *refs: go_on_inverse_kernel(last, *refs),
        tuple(jax.ShapeDtypeStruct(like.shape, like.dtype) for like in out_shape),
        (in_vmem(), in_vmem() if last else in_smem()),
        [full, full],
        "end_inverse" if last else "go_on_inverse",
        (state, normal_high, normal_low, progress),
    )


def solve_kernel(inverse_high, inverse_low, high, low, series):
    padded = high.shape[0]
    lane = lax.broadcasted_iota(jnp.int32, (padded, LANES), 1)
    width = LANES // SPLIT
    for group in range(4):
        cols = pl.ds(group * SPLIT * LANES, SPLIT * LANES)
        solved = (
            dot32(inverse_high[...], high[:, cols], NN)
            + dot32(inverse_high[...], low[:, cols], NN)
            + dot32(inverse_low[...], high[:, cols], NN)
        )
        blocks = [solved[:, k * LANES : (k + 1) * LANES] for k in range(SPLIT)]
        for bit in (1, 2):
            shift = bit * width
            even = (lane // shift) % 2 == 0
            swapped = list(blocks)
            for k in range(SPLIT):
                if k & bit == 0:
                    first, second = blocks[k], blocks[k | bit]
                    swapped[k] = jnp.where(even, first, pltpu.roll(second, shift, 1))
                    swapped[k | bit] = jnp.where(even, pltpu.roll(first, LANES - shift, 1), second)
            blocks = swapped
        part, half = group // 2, group % 2
        for k in range(SPLIT):
            series[(half * SPLIT + k) * 2 + part] = blocks[k]


def call_solve(inverse, values):
    padded = values[0].shape[0]
    return pl.pallas_call(
        solve_kernel,
        out_shape=jax.ShapeDtypeStruct((16, padded, LANES), jnp.float32),
        in_specs=[in_vmem()] * 4,
        out_specs=in_vmem(),
        compiler_params=pltpu.CompilerParams(vmem_limit_bytes=SMALL_VMEM),
        cost_estimate=pl.CostEstimate(
            flops=6 * padded * padded * 16 * LANES, bytes_accessed=20 << 20, transcendentals=0
        ),
        name="solve",
    )(*inverse, *values)


def refine_kernel(count, row_total, col_total, *refs):
    (series, moments, inverse_high, inverse_low, refined) = refs
    padded = series.shape[1]
    normal = [
        [moments[at : at + 1, count + k : count + k + 1] for k in range(3)] for at in range(3)
    ]

    def cyclic(row_at, col_at):
        a, b = (row_at + 1) % 3, (row_at + 2) % 3
        c, d = (col_at + 1) % 3, (col_at + 2) % 3
        return normal[a][c] * normal[b][d] - normal[a][d] * normal[b][c]

    cofacts = [[cyclic(row_at, col_at) for col_at in range(3)] for row_at in range(3)]
    determinant = sum(normal[0][k] * cofacts[0][k] for k in range(3))
    rows = []
    for part in range(2):
        for at in range(3):
            rows.append(
                sum(
                    (cofacts[k][at] / determinant) * moments[part * 3 + k : part * 3 + k + 1, :]
                    for k in range(3)
                )
            )
    rows.append(jnp.zeros((2, padded), jnp.float32))
    upper, lower = split_bf16(jnp.concatenate(rows, axis=0))
    ramps = (
        dot32(inverse_high[...], upper, NT)
        + dot32(inverse_high[...], lower, NT)
        + dot32(inverse_low[...], upper, NT)
    )[:count]
    lane = lax.broadcasted_iota(jnp.int32, (1, LANES), 1)
    x_row = centred(LANES * lax.axis_index("cols") + lane, col_total)
    row_start = 8 * lax.axis_index("dates")
    for part in range(2):
        level, along_y, along_x = (
            jnp.broadcast_to(ramps[:, part * 3 + at : part * 3 + at + 1], (count, LANES))
            for at in range(3)
        )
        level = level + along_x * x_row
        for row in range(8):
            y = centred(row_start + row, row_total)
            refined[pl.ds(row * 2 + part, count, stride=16), :] = series[row * 2 + part, :count] - (
                level + along_y * y
            )


def call_refine(series, moments, inverse, count, row_total, col_total):
    return pl.pallas_call(
        lambda *refs: refine_kernel(count, row_total, col_total, *refs),
        out_shape=jax.ShapeDtypeStruct((count * 16, LANES), jnp.float32),
        in_specs=[in_vmem()] * 4,
        out_specs=in_vmem(),
        compiler_params=pltpu.CompilerParams(vmem_limit_bytes=SMALL_VMEM),
        cost_estimate=pl.CostEstimate(flops=count * 16 * LANES * 6, bytes_accessed=16 << 20, transcendentals=0),
        name="refine",
    )(series, moments, *inverse)


def sum_beside(value, work):
    cols = lax.axis_size("cols")
    pairings = [("dates", [(0, 1), (1, 0)])]
    bit = cols // 2
    while bit and not cols & (cols - 1):
        pairings.append(("cols", [(at, at ^ bit) for at in range(cols)]))
        bit //= 2
    state = ()
    for at in range(max(len(pairings), len(work))):
        value, state = lax.optimization_barrier((value, state))
        if at < len(pairings):
            other = lax.ppermute(value, *pairings[at])
        if at < len(work):
            state = work[at](state)
        if at < len(pairings):
            value = value + other
    if cols & (cols - 1):
        value = lax.psum(value, "cols")
    return value, state


def swap_dates(value):
    return lax.ppermute(value, "dates", [(0, 1), (1, 0)])


def two_halves(complex_images, pair_list):
    dates, rows, _, cols = complex_images.shape
    me = lax.axis_index("dates")
    half = rows // LOOKR // 2
    row_total, col_total = half * 2, cols // LOOKC * lax.axis_size("cols")
    images = complex_images.reshape(dates, rows, 2, SPLIT, cols // SPLIT)
    images = images.transpose(0, 1, 3, 2, 4).reshape(dates, rows // LOOKR, 16, LANES)
    first, second = pair_list[:, 0], pair_list[:, 1]
    low, base = dates * me, (dates - GAP) * me
    first_own = (first >= low) & (first < low + dates)
    second_own = (second >= low) & (second < low + dates)
    inside = (first_own & second_own).astype(jnp.int32)
    across = (first_own ^ second_own).astype(jnp.int32)
    packed = (first - base) | ((second - base) << 10)
    packed = jnp.where(first_own | second_own, packed | (inside << 20) | (across << 21), 0)

    edge = lax.dynamic_slice(
        images, ((dates - GAP) * (1 - me), half * (1 - me), 0, 0), (GAP, half, 16, LANES)
    )
    edge, packed = lax.optimization_barrier((edge, packed))
    halo = swap_dates(edge)
    looks = jnp.asarray(look_matrix(), jnp.bfloat16)
    other, listed, counts = call_pairs(packed, images, looks)
    other, halo = lax.optimization_barrier((other, halo))
    other = swap_dates(other)
    own, own_weights = call_pairs(packed, images, looks, (halo, listed, counts))
    high, lowpart, moments = call_combine(own, own_weights, other, dates, row_total, col_total)

    def first(state):
        return start_inverse(pair_list.T, dates * 2)

    def second(state):
        values, progress = go_on_inverse(*state, last=False)
        return (values,) + state[1:3] + (progress,)

    def third(state):
        return go_on_inverse(*state, last=True)

    def fourth(state):
        return state, call_solve(state, (high, lowpart))

    moments, (inverse, series) = sum_beside(moments, [first, second, third, fourth])
    refined = call_refine(series, moments, inverse, dates * 2, row_total, col_total)
    return refined.reshape(dates * 2, half, 2, LANES)


highest = lax.Precision.HIGHEST


def pseudo_inverse(pair_list, count):
    date_ids = jnp.arange(count, dtype=jnp.int32)
    design = (pair_list[:, 0:1] == date_ids[None, :]).astype(jnp.float32) - (
        pair_list[:, 1:2] == date_ids[None, :]
    ).astype(jnp.float32)
    normal = jnp.dot(design.T, design, precision=highest) + RIDGE * jnp.eye(
        count, dtype=jnp.float32
    )
    factor = jnp.linalg.cholesky(normal)
    return jax.scipy.linalg.cho_solve((factor, True), design.T)


def pool_looks(plane):
    count, rows, cols = plane.shape
    rows_pooled = jnp.sum(plane.reshape(count, rows // LOOKR, LOOKR, cols), axis=2)
    return jnp.sum(rows_pooled.reshape(count, rows // LOOKR, cols // LOOKC, LOOKC), axis=3)


def multilook_pairs(tile_stack, pair_list, pair_block):
    real_planes = tile_stack[:, :, 0, :]
    imag_planes = tile_stack[:, :, 1, :]
    groups = pair_list.reshape(-1, pair_block, 2)
    scale = 1.0 / float(LOOKR * LOOKC)

    def one_group(group):
        first_real = jnp.take(real_planes, group[:, 0], axis=0).astype(jnp.float32)
        first_imag = jnp.take(imag_planes, group[:, 0], axis=0).astype(jnp.float32)
        second_real = jnp.take(real_planes, group[:, 1], axis=0).astype(jnp.float32)
        second_imag = jnp.take(imag_planes, group[:, 1], axis=0).astype(jnp.float32)
        real_part = pool_looks(first_real * second_real + first_imag * second_imag)
        imag_part = pool_looks(first_imag * second_real - first_real * second_imag)
        return (jnp.stack([real_part, imag_part], axis=2) * scale).astype(jnp.bfloat16)

    looked = lax.map(one_group, groups)
    return looked.reshape((pair_list.shape[0],) + looked.shape[2:])


def coordinates(start, count, total):
    return (2.0 * (start + jnp.arange(count, dtype=jnp.int32)).astype(jnp.float32) + 1.0) / float(
        total
    ) - 1.0


def basis_planes(row_coord, col_coord):
    constant = jnp.ones((row_coord.shape[0], col_coord.shape[0]), jnp.float32)
    return jnp.stack([constant, row_coord[:, None] * constant, col_coord[None, :] * constant])


def weighted(widened, planes, pair_count):
    weights = jnp.sum(widened * widened, axis=(0, 2)) / float(pair_count)
    weighted_planes = planes * weights[None]
    normal = jnp.einsum("jrc,krc->jk", weighted_planes, planes, precision=highest)
    return (weighted_planes, normal)


def inverse3(matrix):

    def cyclic(row_at, col_at):
        return (
            matrix[(row_at + 1) % 3, (col_at + 1) % 3] * matrix[(row_at + 2) % 3, (col_at + 2) % 3]
            - matrix[(row_at + 1) % 3, (col_at + 2) % 3]
            * matrix[(row_at + 2) % 3, (col_at + 1) % 3]
        )

    cofacts = jnp.stack(
        [jnp.stack([cyclic(row_at, col_at) for col_at in range(3)]) for row_at in range(3)]
    )
    determinant = jnp.sum(matrix[0] * cofacts[0])
    return cofacts.T / determinant


def refine(series, ramp_rhs, normal, planes):
    ramp_coef = jnp.einsum("jk,dkh->djh", inverse3(normal), ramp_rhs, precision=highest)
    return series - jnp.einsum("djh,jrc->drhc", ramp_coef, planes, precision=highest)


def any_dates(complex_images, pair_list):
    date_count = lax.axis_size("dates")
    date_index = lax.axis_index("dates")
    col_index = lax.axis_index("cols")
    pair_count = pair_list.shape[0]
    date_total = complex_images.shape[0] * date_count
    rounded_pseudo = pseudo_inverse(pair_list, date_total).astype(jnp.bfloat16)
    regrouped = lax.all_to_all(complex_images, "dates", split_axis=1, concat_axis=0, tiled=True)
    interferograms = multilook_pairs(regrouped, pair_list, PAIR_BLOCK * date_count)
    ml_rows = interferograms.shape[1]
    ml_cols = interferograms.shape[3]
    planes = basis_planes(
        coordinates(date_index * ml_rows, ml_rows, ml_rows * date_count),
        coordinates(col_index * ml_cols, ml_cols, ml_cols * lax.axis_size("cols")),
    )
    widened = interferograms.astype(jnp.float32)
    weighted_planes, normal_part = weighted(widened, planes, pair_count)
    flat_pairs = interferograms.reshape(pair_count, -1)
    series = jnp.dot(rounded_pseudo, flat_pairs, preferred_element_type=jnp.float32).reshape(
        (date_total,) + interferograms.shape[1:]
    )
    rhs_part = jnp.einsum("jrc,drhc->djh", weighted_planes, series, precision=highest)
    normal, ramp_rhs = lax.psum((normal_part, rhs_part), ("dates", "cols"))
    return refine(series, ramp_rhs, normal, planes)


def solution(mesh):
    def body(complex_images, pair_list):
        dates, rows, _, cols = complex_images.shape
        if mesh.shape["dates"] == 2 and cols == LANES * LOOKC and rows == 32 and dates >= GAP:
            return two_halves(complex_images, pair_list)
        return any_dates(complex_images, pair_list)

    return jax.shard_map(
        body,
        mesh=mesh,
        in_specs=(P("dates", None, None, "cols"), P()),
        out_specs=P(None, "dates", None, "cols"),
        check_vma=False,
    )
```

```python
import jax
import jax.numpy as jnp
from jax import lax
from jax.experimental import pallas as pl
from jax.experimental.pallas import tpu as pltpu
from jax.sharding import PartitionSpec as P

LOOKR = 2
LOOKC = 4
PAIR_BLOCK = 37
GAP = 12
RIDGE = 0.5
MAX_STEP = 40
UNROLL = 16
LANES = 128
SPLIT = 4
SOME_STEPS = 2
PAIR_VMEM = 52 * 1024 * 1024
OWN_VMEM = 32 * 1024 * 1024
SMALL_VMEM = 12 * 1024 * 1024
NN = (((1,), (0,)), ((), ()))
NT = (((1,), (1,)), ((), ()))


def fill_looks(looks):
    row = lax.broadcasted_iota(jnp.int32, (looks.shape[0], 1), 0)
    lane, sub = row % LANES, row // LANES
    target = (lane % LOOKC) * LANES + sub * (LANES // SPLIT) + lane // LOOKC
    here = target == lax.broadcasted_iota(jnp.int32, looks.shape, 1)
    looks[...] = jnp.where(here, 1.0, 0.0).astype(jnp.bfloat16)


def split_bf16(value):
    high = value.astype(jnp.bfloat16)
    return high, (value - high.astype(jnp.float32)).astype(jnp.bfloat16)


def dot32(first, second, dims):
    return lax.dot_general(first, second, dims, preferred_element_type=jnp.float32)


def spread_looks(source, row, date, slot, step, looks, planes, choose=None, start=0, share=0, found=None):
    raw = source[pl.ds(date, step), pl.ds(row, 8)].reshape(step, 2, SPLIT, 16, LANES)
    left = jnp.concatenate(
        [raw[:, :, sub].reshape(step * 32, LANES) for sub in range(SPLIT)], axis=1
    )
    spread = dot32(left, looks[...], NN)
    for at in range(step):
        base = pl.multiple_of((slot + at) * 128, 128)
        for group in range(2):
            for rlook in range(LOOKR):
                top = (at * 2 + group) * 16 + rlook * 8
                for look in range(LOOKC):
                    planes[pl.ds(base + (rlook * LOOKC + look) * 16 + group * 8, 8), :] = spread[
                        top : top + 8, look * LANES : (look + 1) * LANES
                    ]
        for k in range(share):
            found = choose(start + at * share + k, found)
    return found


def pair_kernel(pair_count, with_halo, step, *refs):
    if with_halo:
        (listed, counts, images, halo, series, weights, planes, looks) = refs
    else:
        (pairs, images, series, listed, counts, raw, planes, looks, sems, sums) = refs
    dates = images.shape[0]
    steps = dates // step
    me = lax.axis_index("dates")
    row_start = 8 * (me if with_halo else 1 - me)
    own_slot, halo_slot = GAP * me, dates * (1 - me)
    copies = []
    if not with_halo:
        for at in range(steps):
            part = pl.ds(at * step, step)
            copies.append(
                pltpu.make_async_copy(images.at[part, pl.ds(row_start, 8)], raw.at[part], sems.at[at])
            )
    for copy in copies:
        copy.start()

    total = series if with_halo else sums
    spare = dates + GAP
    fill_looks(looks)
    total[...] = jnp.zeros_like(total)
    planes[pl.ds(spare * 128, 128), :] = jnp.zeros((128, LANES), jnp.float32)

    second_list = pair_count + UNROLL

    def choose(at, found):
        packed = pairs[at]
        listed[found[0]] = packed
        listed[second_list + found[1]] = packed
        return (found[0] + ((packed >> 20) & 1), found[1] + (packed >> 21))

    found = (jnp.int32(0), jnp.int32(0))
    share = 0 if with_halo else pair_count // dates
    for at in range(steps):
        if with_halo:
            source, row = images, row_start
        else:
            copies[at].wait()
            source, row = raw, 0
        found = spread_looks(
            source, row, at * step, own_slot + at * step, step, looks, planes,
            choose, at * step * share, share, found,
        )
    if not with_halo:
        for at in range(dates * share, pair_count):
            found = choose(at, found)
        for part in range(2):
            counts[part] = found[part]
            for at in range(UNROLL):
                listed[part * second_list + found[part] + at] = jnp.int32(spare * 1025)
    if with_halo:
        spread_looks(halo, 0, 0, halo_slot, GAP, looks, planes)

    def one_pair(packed, power):
        first = packed & 1023
        second = (packed >> 10) & 1023
        a_row = pl.multiple_of(first * 128, 128)
        b_row = pl.multiple_of(second * 128, 128)
        terms_re, terms_im = [], []
        for look in range(LOOKR * LOOKC):
            a_re = planes[pl.ds(a_row + look * 16, 8, stride=2), :]
            a_im = planes[pl.ds(a_row + look * 16 + 1, 8, stride=2), :]
            b_re = planes[pl.ds(b_row + look * 16, 8, stride=2), :]
            b_im = planes[pl.ds(b_row + look * 16 + 1, 8, stride=2), :]
            terms_re.append(a_re * b_re + a_im * b_im)
            terms_im.append(a_im * b_re - a_re * b_im)
        while len(terms_re) > 1:
            terms_re = [terms_re[k] + terms_re[k + 1] for k in range(0, len(terms_re), 2)]
            terms_im = [terms_im[k] + terms_im[k + 1] for k in range(0, len(terms_im), 2)]
        real = terms_re[0].astype(jnp.bfloat16).astype(jnp.float32)
        imag = terms_im[0].astype(jnp.bfloat16).astype(jnp.float32)
        a_at = pl.multiple_of(first * 16, 16)
        b_at = pl.multiple_of(second * 16, 16)
        total[pl.ds(a_at, 8), :] += real
        total[pl.ds(a_at + 8, 8), :] += imag
        total[pl.ds(b_at, 8), :] -= real
        total[pl.ds(b_at + 8, 8), :] -= imag
        return power + (real * real + imag * imag)

    power = jnp.zeros((8, LANES), jnp.float32)
    for part in range(2 if with_halo else 1):

        def some_pairs(at, power, part=part):
            for k in range(UNROLL):
                power = one_pair(listed[part * second_list + at * UNROLL + k], power)
            return power

        power = lax.fori_loop(0, (counts[part] + UNROLL - 1) // UNROLL, some_pairs, power)
    scale = 1.0 / float(LOOKR * LOOKC)
    if with_halo:
        weights[...] = power * (scale * scale / float(pair_count))
    else:
        def narrow(date, carry):
            value = sums[pl.ds(pl.multiple_of((own_slot + date) * 16, 16), 16), :] * scale + carry
            rounded = value.astype(jnp.bfloat16)
            series[pl.ds(pl.multiple_of(date * 16, 16), 16), :] = rounded
            return value - rounded.astype(jnp.float32)

        lax.fori_loop(0, dates, narrow, jnp.zeros((16, LANES), jnp.float32), unroll=4)
        high, low = split_bf16(power * (scale * scale / float(pair_count)))
        series[pl.ds(dates * 16, 16), :] = jnp.concatenate(
            [high.astype(jnp.float32), low.astype(jnp.float32)], axis=0
        ).astype(jnp.bfloat16)


def in_vmem():
    return pl.BlockSpec(memory_space=pltpu.VMEM)


def in_smem():
    return pl.BlockSpec(memory_space=pltpu.SMEM)


def in_hbm():
    return pl.BlockSpec(memory_space=pl.ANY)


def call_pairs(pairs, images, given=None):
    dates = images.shape[0]
    pair_count = pairs.shape[0]
    step = max(k for k in range(1, MAX_STEP + 1) if dates % k == 0)
    slots = dates + GAP + 1
    scratch = [
        pltpu.VMEM((slots * 128, LANES), jnp.float32),
        pltpu.VMEM((SPLIT * LANES, LOOKC * LANES), jnp.bfloat16),
    ]
    sums = jax.ShapeDtypeStruct((slots * 16, LANES), jnp.float32)
    if given is not None:
        halo, listed, counts = given
        out_shape = (sums, jax.ShapeDtypeStruct((8, LANES), jnp.float32))
        in_specs = [in_smem()] * 2 + [in_vmem()] * 2
        out_specs = (in_vmem(), in_vmem())
        args = (listed, counts, images, halo)
    else:
        out_shape = (
            jax.ShapeDtypeStruct(((dates + 1) * 16, LANES), jnp.bfloat16),
            jax.ShapeDtypeStruct((2 * (pair_count + UNROLL),), jnp.int32),
            jax.ShapeDtypeStruct((2,), jnp.int32),
        )
        scratch = [pltpu.VMEM((dates, 8, 16, LANES), jnp.bfloat16)] + scratch
        scratch += [pltpu.SemaphoreType.DMA((dates // step,)), pltpu.VMEM(sums.shape, sums.dtype)]
        in_specs = [in_smem(), in_hbm()]
        out_specs = (in_vmem(), in_smem(), in_smem())
        args = (pairs, images)
    return pl.pallas_call(
        lambda *refs: pair_kernel(pair_count, given is not None, step, *refs),
        out_shape=out_shape,
        in_specs=in_specs,
        out_specs=out_specs,
        scratch_shapes=scratch,
        compiler_params=pltpu.CompilerParams(vmem_limit_bytes=PAIR_VMEM if given is None else OWN_VMEM),
        cost_estimate=pl.CostEstimate(
            flops=pair_count * 70 * 1024, bytes_accessed=pair_count * 48 * 1024, transcendentals=0
        ),
        name="pairs_other" if given is None else "pairs_own",
    )(*args)


def half_basis(row_start, col_start, row_total, col_total):
    sub = lax.broadcasted_iota(jnp.int32, (8, LANES), 0)
    lane = lax.broadcasted_iota(jnp.int32, (8, LANES), 1)
    width = LANES // SPLIT
    row = row_start + (sub // SPLIT) * SPLIT + lane // width
    col = col_start + (sub % SPLIT) * width + lane % width
    return centred(row, row_total), centred(col, col_total)


def centred(place, total):
    return (2.0 * place.astype(jnp.float32) + 1.0) / float(total) - 1.0


def combine_kernel(dates, row_total, col_total, *refs):
    (own, own_weights, other, high, low, moments, full, weighted_rows) = refs
    me = lax.axis_index("dates")
    count = dates * 2
    span = dates + GAP
    scale = 1.0 / float(LOOKR * LOOKC)

    def rows(start, size):
        return pl.ds(pl.multiple_of(start * 16, 16), size * 16)

    full[rows((dates - GAP) * me, span), :] = own[pl.ds(0, span * 16), :] * scale
    rest = dates - GAP
    full[rows(span * (1 - me), rest), :] = other[rows(GAP * (1 - me), rest), :].astype(jnp.float32)
    full[rows(dates - GAP * me, GAP), :] += other[rows(rest * me, GAP), :].astype(jnp.float32)
    y_plane, x_plane = half_basis(8 * me, LANES * lax.axis_index("cols"), row_total, col_total)
    basis = (jnp.ones((8, LANES), jnp.float32), y_plane, x_plane)
    padded = full.shape[0] // 16
    full[pl.ds(count * 16, (padded - count) * 16), :] = jnp.zeros(
        ((padded - count) * 16, LANES), jnp.float32
    )
    for at in range(3):
        full[pl.ds((count + at) * 16, 8), :] = basis[at]
    sent = other[pl.ds(dates * 16, 16), :].astype(jnp.float32)
    weights = own_weights[...] + (sent[:8] + sent[8:])
    weighted_rows[...] = jnp.zeros_like(weighted_rows)
    for at in range(3):
        plane = weights * basis[at]
        for part in range(2):
            for sub in range(8):
                weighted_rows[part * 3 + at : part * 3 + at + 1, pl.ds((part * 8 + sub) * LANES, LANES)] = (
                    plane[sub : sub + 1]
                )
    for at in range(16):
        value = full[pl.ds(at, padded, stride=16), :]
        upper, lower = split_bf16(value)
        high[:, at * LANES : (at + 1) * LANES] = upper
        low[:, at * LANES : (at + 1) * LANES] = lower
    upper, lower = split_bf16(weighted_rows[...])
    moments[...] = (
        dot32(upper, high[...], NT) + dot32(lower, high[...], NT) + dot32(upper, low[...], NT)
    )


def call_combine(own, own_weights, other, dates, row_total, col_total):
    padded = pad_dates(dates * 2)
    wide = jax.ShapeDtypeStruct((padded, 16 * LANES), jnp.bfloat16)
    return pl.pallas_call(
        lambda *refs: combine_kernel(dates, row_total, col_total, *refs),
        out_shape=(wide, wide, jax.ShapeDtypeStruct((8, padded), jnp.float32)),
        in_specs=[in_vmem()] * 3,
        out_specs=(in_vmem(),) * 3,
        scratch_shapes=[
            pltpu.VMEM((padded * 16, LANES), jnp.float32),
            pltpu.VMEM((8, 16 * LANES), jnp.float32),
        ],
        compiler_params=pltpu.CompilerParams(vmem_limit_bytes=SMALL_VMEM),
        cost_estimate=pl.CostEstimate(flops=padded * 8 * 12288, bytes_accessed=16 << 20, transcendentals=0),
        name="combine",
    )(own, own_weights, other)


def pad_dates(count):
    return (count + 3 + 15) // 16 * 16


def start_inverse_kernel(pairs, state, normal_high, normal_low, progress):
    padded = state.shape[0]
    date = lax.broadcasted_iota(jnp.int32, (padded, pairs.shape[1]), 0)
    design = (
        jnp.where(date == pairs[0:1, :], 1.0, 0.0) - jnp.where(date == pairs[1:2, :], 1.0, 0.0)
    ).astype(jnp.bfloat16)
    eye = unit(padded)
    normal = dot32(design, design, NT) + RIDGE * eye
    normal_high[...], normal_low[...] = split_bf16(normal)
    largest = jnp.max(jnp.sum(jnp.abs(normal), axis=1))
    scale, error = centre((largest - RIDGE) / (largest + RIDGE))
    first = 2.0 / (largest + RIDGE)
    state[...] = (scale * first) * (2.0 * eye - first * normal)
    progress[0:1, :] = jnp.broadcast_to(error, (1, LANES))
    progress[1:2, :] = jnp.broadcast_to(largest, (1, LANES))


def go_on_inverse_kernel(last, state, normal_high, normal_low, progress, *refs):
    residual, now_state = refs[-2:]
    eye = unit(state.shape[0])
    largest = jnp.max(progress[1:2, :])
    careful = largest > 128.0
    now_state[...] = state[...]

    def step(scale):
        now, rest = split_bf16(now_state[...])
        residual[...] = eye - dot32(normal_high[...], now, NN) - dot32(normal_high[...], rest, NN)

        @pl.when(careful)
        def _():
            residual[...] -= dot32(normal_low[...], now, NN)

        upper, lower = split_bf16(residual[...])
        change = dot32(now, upper, NN)
        now_state[...] = scale * (now_state[...] + change)

        @pl.when(careful)
        def _():
            now_state[...] += scale * (dot32(now, lower, NN) + dot32(rest, upper, NN))

    def unfinished(carry):
        return (carry[0] > 2e-3) & (last | (carry[1] < SOME_STEPS))

    def body(carry):
        error, count = carry
        scale, left = centre(error)
        step(scale)
        return jnp.maximum(left, 0.05 * error), count + 1

    error, _ = lax.while_loop(unfinished, body, (jnp.max(progress[0:1, :]), jnp.int32(0)))
    if last:
        step(jnp.float32(1.0))
        refs[0][...], refs[1][...] = split_bf16(now_state[...])
    else:
        refs[0][...] = now_state[...]
        refs[1][0:1, :] = jnp.broadcast_to(error, (1, LANES))
        refs[1][1:2, :] = progress[1:2, :]


def unit(size):
    row = lax.broadcasted_iota(jnp.int32, (size, size), 0)
    return jnp.where(row == lax.broadcasted_iota(jnp.int32, (size, size), 1), 1.0, 0.0)


def centre(error):
    scale = 2.0 / (2.0 - error * error)
    return scale, scale - 1.0


def inverse_call(kernel, out_shape, out_specs, scratch, name, args):
    return pl.pallas_call(
        kernel,
        out_shape=out_shape,
        in_specs=[in_vmem()] * len(args),
        out_specs=out_specs,
        scratch_shapes=scratch,
        compiler_params=pltpu.CompilerParams(vmem_limit_bytes=SMALL_VMEM),
        cost_estimate=pl.CostEstimate(flops=1 << 30, bytes_accessed=8 << 20, transcendentals=0),
        name=name,
    )(*args)


def start_inverse(pair_rows, count):
    padded = pad_dates(count)
    full = jax.ShapeDtypeStruct((padded, padded), jnp.float32)
    half = jax.ShapeDtypeStruct((padded, padded), jnp.bfloat16)
    progress = jax.ShapeDtypeStruct((2, LANES), jnp.float32)
    return inverse_call(
        start_inverse_kernel,
        (full, half, half, progress),
        (in_vmem(),) * 4,
        [],
        "start_inverse",
        (pair_rows,),
    )


def go_on_inverse(state, normal_high, normal_low, progress, last):
    out_shape = (normal_high, normal_high) if last else (state, progress)
    full = pltpu.VMEM(state.shape, jnp.float32)
    return inverse_call(
        lambda *refs: go_on_inverse_kernel(last, *refs),
        tuple(jax.ShapeDtypeStruct(like.shape, like.dtype) for like in out_shape),
        (in_vmem(),) * 2,
        [full, full],
        "end_inverse" if last else "go_on_inverse",
        (state, normal_high, normal_low, progress),
    )


def solve_kernel(part, inverse_high, inverse_low, high, low, series):
    padded = high.shape[0]
    lane = lax.broadcasted_iota(jnp.int32, (padded, LANES), 1)
    width = LANES // SPLIT
    for half in range(2):
        cols = pl.ds((part * 2 + half) * SPLIT * LANES, SPLIT * LANES)
        solved = (
            dot32(inverse_high[...], high[:, cols], NN)
            + dot32(inverse_high[...], low[:, cols], NN)
            + dot32(inverse_low[...], high[:, cols], NN)
        )
        blocks = [solved[:, k * LANES : (k + 1) * LANES] for k in range(SPLIT)]
        for bit in (1, 2):
            shift = bit * width
            even = (lane // shift) % 2 == 0
            swapped = list(blocks)
            for k in range(SPLIT):
                if k & bit == 0:
                    first, second = blocks[k], blocks[k | bit]
                    swapped[k] = jnp.where(even, first, pltpu.roll(second, shift, 1))
                    swapped[k | bit] = jnp.where(even, pltpu.roll(first, LANES - shift, 1), second)
            blocks = swapped
        for k in range(SPLIT):
            series[half * SPLIT + k] = blocks[k]


def call_solve(part, inverse, values):
    padded = values[0].shape[0]
    return pl.pallas_call(
        lambda *refs: solve_kernel(part, *refs),
        out_shape=jax.ShapeDtypeStruct((8, padded, LANES), jnp.float32),
        in_specs=[in_vmem()] * 4,
        out_specs=in_vmem(),
        compiler_params=pltpu.CompilerParams(vmem_limit_bytes=SMALL_VMEM),
        cost_estimate=pl.CostEstimate(
            flops=6 * padded * padded * 16 * LANES, bytes_accessed=20 << 20, transcendentals=0
        ),
        name="solve",
    )(*inverse, *values)


def refine_kernel(count, row_total, col_total, *refs):
    (*series, moments, inverse_high, inverse_low, refined) = refs
    padded = moments.shape[1]
    normal = [
        [moments[at : at + 1, count + k : count + k + 1] for k in range(3)] for at in range(3)
    ]

    def cyclic(row_at, col_at):
        a, b = (row_at + 1) % 3, (row_at + 2) % 3
        c, d = (col_at + 1) % 3, (col_at + 2) % 3
        return normal[a][c] * normal[b][d] - normal[a][d] * normal[b][c]

    cofacts = [[cyclic(row_at, col_at) for col_at in range(3)] for row_at in range(3)]
    determinant = sum(normal[0][k] * cofacts[0][k] for k in range(3))
    rows = []
    for part in range(2):
        for at in range(3):
            rows.append(
                sum(
                    (cofacts[k][at] / determinant) * moments[part * 3 + k : part * 3 + k + 1, :]
                    for k in range(3)
                )
            )
    rows.append(jnp.zeros((2, padded), jnp.float32))
    upper, lower = split_bf16(jnp.concatenate(rows, axis=0))
    ramps = (
        dot32(inverse_high[...], upper, NT)
        + dot32(inverse_high[...], lower, NT)
        + dot32(inverse_low[...], upper, NT)
    )[:count]
    lane = lax.broadcasted_iota(jnp.int32, (1, LANES), 1)
    x_row = centred(LANES * lax.axis_index("cols") + lane, col_total)
    row_start = 8 * lax.axis_index("dates")
    for part in range(2):
        level, along_y, along_x = (
            jnp.broadcast_to(ramps[:, part * 3 + at : part * 3 + at + 1], (count, LANES))
            for at in range(3)
        )
        level = level + along_x * x_row
        for row in range(8):
            y = centred(row_start + row, row_total)
            refined[pl.ds(row * 2 + part, count, stride=16), :] = series[part][row, :count] - (
                level + along_y * y
            )


def call_refine(series, moments, inverse, count, row_total, col_total):
    return pl.pallas_call(
        lambda *refs: refine_kernel(count, row_total, col_total, *refs),
        out_shape=jax.ShapeDtypeStruct((count * 16, LANES), jnp.float32),
        in_specs=[in_vmem()] * 5,
        out_specs=in_vmem(),
        compiler_params=pltpu.CompilerParams(vmem_limit_bytes=SMALL_VMEM),
        cost_estimate=pl.CostEstimate(flops=count * 16 * LANES * 6, bytes_accessed=16 << 20, transcendentals=0),
        name="refine",
    )(*series, moments, *inverse)


def sum_beside(value, state, work):
    cols = lax.axis_size("cols")
    pairings = [("dates", [(0, 1), (1, 0)])]
    bit = cols // 2
    while bit and not cols & (cols - 1):
        pairings.append(("cols", [(at, at ^ bit) for at in range(cols)]))
        bit //= 2
    for at in range(max(len(pairings), len(work))):
        value, state = lax.optimization_barrier((value, state))
        if at < len(pairings):
            other = lax.ppermute(value, *pairings[at])
        if at < len(work):
            state = work[at](state)
        if at < len(pairings):
            value = value + other
    if cols & (cols - 1):
        value = lax.psum(value, "cols")
    return value, state


def swap_dates(value):
    return lax.ppermute(value, "dates", [(0, 1), (1, 0)])


def two_halves(complex_images, pair_list):
    dates, rows, _, cols = complex_images.shape
    me = lax.axis_index("dates")
    half = rows // LOOKR // 2
    row_total, col_total = half * 2, cols // LOOKC * lax.axis_size("cols")
    images = complex_images.reshape(dates, rows, 2, SPLIT, cols // SPLIT)
    images = images.transpose(0, 1, 3, 2, 4).reshape(dates, rows // LOOKR, 16, LANES)
    first, second = pair_list[:, 0], pair_list[:, 1]
    low, base = dates * me, (dates - GAP) * me
    first_own = (first >= low) & (first < low + dates)
    second_own = (second >= low) & (second < low + dates)
    inside = (first_own & second_own).astype(jnp.int32)
    across = (first_own ^ second_own).astype(jnp.int32)
    packed = (first - base) | ((second - base) << 10)
    packed = jnp.where(first_own | second_own, packed | (inside << 20) | (across << 21), 0)

    edge = lax.dynamic_slice(
        images, ((dates - GAP) * (1 - me), half * (1 - me), 0, 0), (GAP, half, 16, LANES)
    )
    edge, packed = lax.optimization_barrier((edge, packed))
    halo = swap_dates(edge)
    other, listed, counts = call_pairs(packed, images)
    other, halo = lax.optimization_barrier((other, halo))
    other = swap_dates(other)
    own, own_weights = call_pairs(packed, images, (halo, listed, counts))
    own, pair_rows = lax.optimization_barrier((own, pair_list.T))
    started = start_inverse(pair_rows, dates * 2)
    own, started = lax.optimization_barrier((own, started))
    high, lowpart, moments = call_combine(own, own_weights, other, dates, row_total, col_total)

    def go_on(state):
        values, progress = go_on_inverse(*state, last=False)
        return (values,) + state[1:3] + (progress,)

    def end(state):
        return go_on_inverse(*state, last=True), ()

    def solve(state):
        inverse, solved = state
        return inverse, solved + (call_solve(len(solved), inverse, (high, lowpart)),)

    moments, (inverse, series) = sum_beside(moments, started, [go_on, go_on, end, solve, solve])
    refined = call_refine(series, moments, inverse, dates * 2, row_total, col_total)
    return refined.reshape(dates * 2, half, 2, LANES)


highest = lax.Precision.HIGHEST


def pseudo_inverse(pair_list, count):
    date_ids = jnp.arange(count, dtype=jnp.int32)
    design = (pair_list[:, 0:1] == date_ids[None, :]).astype(jnp.float32) - (
        pair_list[:, 1:2] == date_ids[None, :]
    ).astype(jnp.float32)
    normal = jnp.dot(design.T, design, precision=highest) + RIDGE * jnp.eye(
        count, dtype=jnp.float32
    )
    factor = jnp.linalg.cholesky(normal)
    return jax.scipy.linalg.cho_solve((factor, True), design.T)


def pool_looks(plane):
    count, rows, cols = plane.shape
    rows_pooled = jnp.sum(plane.reshape(count, rows // LOOKR, LOOKR, cols), axis=2)
    return jnp.sum(rows_pooled.reshape(count, rows // LOOKR, cols // LOOKC, LOOKC), axis=3)


def multilook_pairs(tile_stack, pair_list, pair_block):
    real_planes = tile_stack[:, :, 0, :]
    imag_planes = tile_stack[:, :, 1, :]
    groups = pair_list.reshape(-1, pair_block, 2)
    scale = 1.0 / float(LOOKR * LOOKC)

    def one_group(group):
        first_real = jnp.take(real_planes, group[:, 0], axis=0).astype(jnp.float32)
        first_imag = jnp.take(imag_planes, group[:, 0], axis=0).astype(jnp.float32)
        second_real = jnp.take(real_planes, group[:, 1], axis=0).astype(jnp.float32)
        second_imag = jnp.take(imag_planes, group[:, 1], axis=0).astype(jnp.float32)
        real_part = pool_looks(first_real * second_real + first_imag * second_imag)
        imag_part = pool_looks(first_imag * second_real - first_real * second_imag)
        return (jnp.stack([real_part, imag_part], axis=2) * scale).astype(jnp.bfloat16)

    looked = lax.map(one_group, groups)
    return looked.reshape((pair_list.shape[0],) + looked.shape[2:])


def coordinates(start, count, total):
    return (2.0 * (start + jnp.arange(count, dtype=jnp.int32)).astype(jnp.float32) + 1.0) / float(
        total
    ) - 1.0


def basis_planes(row_coord, col_coord):
    constant = jnp.ones((row_coord.shape[0], col_coord.shape[0]), jnp.float32)
    return jnp.stack([constant, row_coord[:, None] * constant, col_coord[None, :] * constant])


def weighted(widened, planes, pair_count):
    weights = jnp.sum(widened * widened, axis=(0, 2)) / float(pair_count)
    weighted_planes = planes * weights[None]
    normal = jnp.einsum("jrc,krc->jk", weighted_planes, planes, precision=highest)
    return (weighted_planes, normal)


def inverse3(matrix):

    def cyclic(row_at, col_at):
        return (
            matrix[(row_at + 1) % 3, (col_at + 1) % 3] * matrix[(row_at + 2) % 3, (col_at + 2) % 3]
            - matrix[(row_at + 1) % 3, (col_at + 2) % 3]
            * matrix[(row_at + 2) % 3, (col_at + 1) % 3]
        )

    cofacts = jnp.stack(
        [jnp.stack([cyclic(row_at, col_at) for col_at in range(3)]) for row_at in range(3)]
    )
    determinant = jnp.sum(matrix[0] * cofacts[0])
    return cofacts.T / determinant


def refine(series, ramp_rhs, normal, planes):
    ramp_coef = jnp.einsum("jk,dkh->djh", inverse3(normal), ramp_rhs, precision=highest)
    return series - jnp.einsum("djh,jrc->drhc", ramp_coef, planes, precision=highest)


def any_dates(complex_images, pair_list):
    date_count = lax.axis_size("dates")
    date_index = lax.axis_index("dates")
    col_index = lax.axis_index("cols")
    pair_count = pair_list.shape[0]
    date_total = complex_images.shape[0] * date_count
    rounded_pseudo = pseudo_inverse(pair_list, date_total).astype(jnp.bfloat16)
    regrouped = lax.all_to_all(complex_images, "dates", split_axis=1, concat_axis=0, tiled=True)
    interferograms = multilook_pairs(regrouped, pair_list, PAIR_BLOCK * date_count)
    ml_rows = interferograms.shape[1]
    ml_cols = interferograms.shape[3]
    planes = basis_planes(
        coordinates(date_index * ml_rows, ml_rows, ml_rows * date_count),
        coordinates(col_index * ml_cols, ml_cols, ml_cols * lax.axis_size("cols")),
    )
    widened = interferograms.astype(jnp.float32)
    weighted_planes, normal_part = weighted(widened, planes, pair_count)
    flat_pairs = interferograms.reshape(pair_count, -1)
    series = jnp.dot(rounded_pseudo, flat_pairs, preferred_element_type=jnp.float32).reshape(
        (date_total,) + interferograms.shape[1:]
    )
    rhs_part = jnp.einsum("jrc,drhc->djh", weighted_planes, series, precision=highest)
    normal, ramp_rhs = lax.psum((normal_part, rhs_part), ("dates", "cols"))
    return refine(series, ramp_rhs, normal, planes)


def solution(mesh):
    def body(complex_images, pair_list):
        dates, rows, _, cols = complex_images.shape
        if mesh.shape["dates"] == 2 and cols == LANES * LOOKC and rows == 32 and dates >= GAP:
            return two_halves(complex_images, pair_list)
        return any_dates(complex_images, pair_list)

    return jax.shard_map(
        body,
        mesh=mesh,
        in_specs=(P("dates", None, None, "cols"), P()),
        out_specs=P(None, "dates", None, "cols"),
        check_vma=False,
    )
```

```python
import jax
import jax.numpy as jnp
from jax import lax
from jax.experimental import pallas as pl
from jax.experimental.pallas import tpu as pltpu
from jax.sharding import PartitionSpec as P

LOOKR = 2
LOOKC = 4
PAIR_BLOCK = 37
GAP = 12
RIDGE = 0.5
MAX_STEP = 40
UNROLL = 16
LANES = 128
SPLIT = 4
SOME_STEPS = 2
PAIR_VMEM = 52 * 1024 * 1024
OWN_VMEM = 32 * 1024 * 1024
SMALL_VMEM = 12 * 1024 * 1024
NN = (((1,), (0,)), ((), ()))
NT = (((1,), (1,)), ((), ()))


def fill_looks(looks):
    row = lax.broadcasted_iota(jnp.int32, (looks.shape[0], 1), 0)
    lane, sub = row % LANES, row // LANES
    target = (lane % LOOKC) * LANES + sub * (LANES // SPLIT) + lane // LOOKC
    here = target == lax.broadcasted_iota(jnp.int32, looks.shape, 1)
    looks[...] = jnp.where(here, 1.0, 0.0).astype(jnp.bfloat16)


def split_bf16(value):
    high = value.astype(jnp.bfloat16)
    return high, (value - high.astype(jnp.float32)).astype(jnp.bfloat16)


def dot32(first, second, dims):
    return lax.dot_general(first, second, dims, preferred_element_type=jnp.float32)


def spread_looks(source, row, date, slot, step, looks, planes, choose=None, start=0, share=0, found=None):
    raw = source[pl.ds(date, step), pl.ds(row, 8)].reshape(step, 2, SPLIT, 16, LANES)
    left = jnp.concatenate(
        [raw[:, :, sub].reshape(step * 32, LANES) for sub in range(SPLIT)], axis=1
    )
    spread = dot32(left, looks[...], NN)
    for at in range(step):
        base = pl.multiple_of((slot + at) * 128, 128)
        for group in range(2):
            for rlook in range(LOOKR):
                top = (at * 2 + group) * 16 + rlook * 8
                for look in range(LOOKC):
                    planes[pl.ds(base + (rlook * LOOKC + look) * 16 + group * 8, 8), :] = spread[
                        top : top + 8, look * LANES : (look + 1) * LANES
                    ]
        for k in range(share):
            found = choose(start + at * share + k, found)
    return found


def pair_kernel(pair_count, with_halo, step, *refs):
    if with_halo:
        (listed, counts, images, halo, series, weights, planes, looks) = refs
    else:
        (pairs, images, series, listed, counts, raw, planes, looks, sems, sums) = refs
    dates = images.shape[0]
    steps = dates // step
    me = lax.axis_index("dates")
    row_start = 8 * (me if with_halo else 1 - me)
    own_slot, halo_slot = GAP * me, dates * (1 - me)
    copies = []
    if not with_halo:
        for at in range(steps):
            part = pl.ds(at * step, step)
            copies.append(
                pltpu.make_async_copy(images.at[part, pl.ds(row_start, 8)], raw.at[part], sems.at[at])
            )
    for copy in copies:
        copy.start()

    total = series if with_halo else sums
    spare = dates + GAP
    fill_looks(looks)
    total[...] = jnp.zeros_like(total)
    planes[pl.ds(spare * 128, 128), :] = jnp.zeros((128, LANES), jnp.float32)

    second_list = pair_count + UNROLL

    def choose(at, found):
        packed = pairs[at]
        listed[found[0]] = packed
        listed[second_list + found[1]] = packed
        return (found[0] + ((packed >> 20) & 1), found[1] + (packed >> 21))

    found = (jnp.int32(0), jnp.int32(0))
    share = 0 if with_halo else pair_count // dates
    for at in range(steps):
        if with_halo:
            source, row = images, row_start
        else:
            copies[at].wait()
            source, row = raw, 0
        found = spread_looks(
            source, row, at * step, own_slot + at * step, step, looks, planes,
            choose, at * step * share, share, found,
        )
    if not with_halo:
        for at in range(dates * share, pair_count):
            found = choose(at, found)
        for part in range(2):
            counts[part] = found[part]
            for at in range(UNROLL):
                listed[part * second_list + found[part] + at] = jnp.int32(spare * 1025)
    if with_halo:
        spread_looks(halo, 0, 0, halo_slot, GAP, looks, planes)

    def one_pair(packed, power):
        first = packed & 1023
        second = (packed >> 10) & 1023
        a_row = pl.multiple_of(first * 128, 128)
        b_row = pl.multiple_of(second * 128, 128)
        terms_re, terms_im = [], []
        for look in range(LOOKR * LOOKC):
            a_re = planes[pl.ds(a_row + look * 16, 8, stride=2), :]
            a_im = planes[pl.ds(a_row + look * 16 + 1, 8, stride=2), :]
            b_re = planes[pl.ds(b_row + look * 16, 8, stride=2), :]
            b_im = planes[pl.ds(b_row + look * 16 + 1, 8, stride=2), :]
            terms_re.append(a_re * b_re + a_im * b_im)
            terms_im.append(a_im * b_re - a_re * b_im)
        while len(terms_re) > 1:
            terms_re = [terms_re[k] + terms_re[k + 1] for k in range(0, len(terms_re), 2)]
            terms_im = [terms_im[k] + terms_im[k + 1] for k in range(0, len(terms_im), 2)]
        real = terms_re[0].astype(jnp.bfloat16).astype(jnp.float32)
        imag = terms_im[0].astype(jnp.bfloat16).astype(jnp.float32)
        a_at = pl.multiple_of(first * 16, 16)
        b_at = pl.multiple_of(second * 16, 16)
        total[pl.ds(a_at, 8), :] += real
        total[pl.ds(a_at + 8, 8), :] += imag
        total[pl.ds(b_at, 8), :] -= real
        total[pl.ds(b_at + 8, 8), :] -= imag
        return power + (real * real + imag * imag)

    power = jnp.zeros((8, LANES), jnp.float32)
    for part in range(2 if with_halo else 1):

        def some_pairs(at, power, part=part):
            for k in range(UNROLL):
                power = one_pair(listed[part * second_list + at * UNROLL + k], power)
            return power

        power = lax.fori_loop(0, (counts[part] + UNROLL - 1) // UNROLL, some_pairs, power)
    scale = 1.0 / float(LOOKR * LOOKC)
    if with_halo:
        weights[...] = power * (scale * scale / float(pair_count))
    else:
        chains = 4 if dates % 4 == 0 else 1
        length = dates // chains

        def narrow(at, carries):
            left = []
            for chain, carry in enumerate(carries):
                date = chain * length + at
                value = sums[pl.ds(pl.multiple_of((own_slot + date) * 16, 16), 16), :] * scale + carry
                rounded = value.astype(jnp.bfloat16)
                series[pl.ds(pl.multiple_of(date * 16, 16), 16), :] = rounded
                left.append(value - rounded.astype(jnp.float32))
            return tuple(left)

        lax.fori_loop(0, length, narrow, (jnp.zeros((16, LANES), jnp.float32),) * chains)
        high, low = split_bf16(power * (scale * scale / float(pair_count)))
        series[pl.ds(dates * 16, 16), :] = jnp.concatenate(
            [high.astype(jnp.float32), low.astype(jnp.float32)], axis=0
        ).astype(jnp.bfloat16)


def in_vmem():
    return pl.BlockSpec(memory_space=pltpu.VMEM)


def in_smem():
    return pl.BlockSpec(memory_space=pltpu.SMEM)


def in_hbm():
    return pl.BlockSpec(memory_space=pl.ANY)


def call_pairs(pairs, images, given=None):
    dates = images.shape[0]
    pair_count = pairs.shape[0]
    step = max(k for k in range(1, MAX_STEP + 1) if dates % k == 0)
    slots = dates + GAP + 1
    scratch = [
        pltpu.VMEM((slots * 128, LANES), jnp.float32),
        pltpu.VMEM((SPLIT * LANES, LOOKC * LANES), jnp.bfloat16),
    ]
    sums = jax.ShapeDtypeStruct((slots * 16, LANES), jnp.float32)
    if given is not None:
        halo, listed, counts = given
        out_shape = (sums, jax.ShapeDtypeStruct((8, LANES), jnp.float32))
        in_specs = [in_smem()] * 2 + [in_vmem()] * 2
        out_specs = (in_vmem(), in_vmem())
        args = (listed, counts, images, halo)
    else:
        out_shape = (
            jax.ShapeDtypeStruct(((dates + 1) * 16, LANES), jnp.bfloat16),
            jax.ShapeDtypeStruct((2 * (pair_count + UNROLL),), jnp.int32),
            jax.ShapeDtypeStruct((2,), jnp.int32),
        )
        scratch = [pltpu.VMEM((dates, 8, 16, LANES), jnp.bfloat16)] + scratch
        scratch += [pltpu.SemaphoreType.DMA((dates // step,)), pltpu.VMEM(sums.shape, sums.dtype)]
        in_specs = [in_smem(), in_hbm()]
        out_specs = (in_vmem(), in_smem(), in_smem())
        args = (pairs, images)
    return pl.pallas_call(
        lambda *refs: pair_kernel(pair_count, given is not None, step, *refs),
        out_shape=out_shape,
        in_specs=in_specs,
        out_specs=out_specs,
        scratch_shapes=scratch,
        compiler_params=pltpu.CompilerParams(vmem_limit_bytes=PAIR_VMEM if given is None else OWN_VMEM),
        cost_estimate=pl.CostEstimate(
            flops=pair_count * 70 * 1024, bytes_accessed=pair_count * 48 * 1024, transcendentals=0
        ),
        name="pairs_other" if given is None else "pairs_own",
    )(*args)


def half_basis(row_start, col_start, row_total, col_total):
    sub = lax.broadcasted_iota(jnp.int32, (8, LANES), 0)
    lane = lax.broadcasted_iota(jnp.int32, (8, LANES), 1)
    width = LANES // SPLIT
    row = row_start + (sub // SPLIT) * SPLIT + lane // width
    col = col_start + (sub % SPLIT) * width + lane % width
    return centred(row, row_total), centred(col, col_total)


def centred(place, total):
    return (2.0 * place.astype(jnp.float32) + 1.0) / float(total) - 1.0


def combine_kernel(dates, row_total, col_total, *refs):
    (own, own_weights, other, high, low, moments, full, weighted_rows) = refs
    me = lax.axis_index("dates")
    count = dates * 2
    span = dates + GAP
    scale = 1.0 / float(LOOKR * LOOKC)

    def rows(start, size):
        return pl.ds(pl.multiple_of(start * 16, 16), size * 16)

    full[rows((dates - GAP) * me, span), :] = own[pl.ds(0, span * 16), :] * scale
    rest = dates - GAP
    full[rows(span * (1 - me), rest), :] = other[rows(GAP * (1 - me), rest), :].astype(jnp.float32)
    full[rows(dates - GAP * me, GAP), :] += other[rows(rest * me, GAP), :].astype(jnp.float32)
    y_plane, x_plane = half_basis(8 * me, LANES * lax.axis_index("cols"), row_total, col_total)
    basis = (jnp.ones((8, LANES), jnp.float32), y_plane, x_plane)
    padded = full.shape[0] // 16
    full[pl.ds(count * 16, (padded - count) * 16), :] = jnp.zeros(
        ((padded - count) * 16, LANES), jnp.float32
    )
    for at in range(3):
        full[pl.ds((count + at) * 16, 8), :] = basis[at]
    sent = other[pl.ds(dates * 16, 16), :].astype(jnp.float32)
    weights = own_weights[...] + (sent[:8] + sent[8:])
    weighted_rows[...] = jnp.zeros_like(weighted_rows)
    for at in range(3):
        plane = weights * basis[at]
        for part in range(2):
            for sub in range(8):
                weighted_rows[part * 3 + at : part * 3 + at + 1, pl.ds((part * 8 + sub) * LANES, LANES)] = (
                    plane[sub : sub + 1]
                )
    for at in range(16):
        value = full[pl.ds(at, padded, stride=16), :]
        upper, lower = split_bf16(value)
        high[:, at * LANES : (at + 1) * LANES] = upper
        low[:, at * LANES : (at + 1) * LANES] = lower
    upper, lower = split_bf16(weighted_rows[...])
    moments[...] = (
        dot32(upper, high[...], NT) + dot32(lower, high[...], NT) + dot32(upper, low[...], NT)
    )


def call_combine(own, own_weights, other, dates, row_total, col_total):
    padded = pad_dates(dates * 2)
    wide = jax.ShapeDtypeStruct((padded, 16 * LANES), jnp.bfloat16)
    return pl.pallas_call(
        lambda *refs: combine_kernel(dates, row_total, col_total, *refs),
        out_shape=(wide, wide, jax.ShapeDtypeStruct((8, padded), jnp.float32)),
        in_specs=[in_vmem()] * 3,
        out_specs=(in_vmem(),) * 3,
        scratch_shapes=[
            pltpu.VMEM((padded * 16, LANES), jnp.float32),
            pltpu.VMEM((8, 16 * LANES), jnp.float32),
        ],
        compiler_params=pltpu.CompilerParams(vmem_limit_bytes=SMALL_VMEM),
        cost_estimate=pl.CostEstimate(flops=padded * 8 * 12288, bytes_accessed=16 << 20, transcendentals=0),
        name="combine",
    )(own, own_weights, other)


def pad_dates(count):
    return (count + 3 + 15) // 16 * 16


def start_inverse_kernel(pairs, state, normal_high, normal_low, progress):
    padded = state.shape[0]
    date = lax.broadcasted_iota(jnp.int32, (padded, pairs.shape[1]), 0)
    design = (
        jnp.where(date == pairs[0:1, :], 1.0, 0.0) - jnp.where(date == pairs[1:2, :], 1.0, 0.0)
    ).astype(jnp.bfloat16)
    eye = unit(padded)
    normal = dot32(design, design, NT) + RIDGE * eye
    normal_high[...], normal_low[...] = split_bf16(normal)
    largest = jnp.max(jnp.sum(jnp.abs(normal), axis=1))
    scale, error = centre((largest - RIDGE) / (largest + RIDGE))
    first = 2.0 / (largest + RIDGE)
    state[...] = (scale * first) * (2.0 * eye - first * normal)
    progress[0:1, :] = jnp.broadcast_to(error, (1, LANES))
    progress[1:2, :] = jnp.broadcast_to(largest, (1, LANES))


def go_on_inverse_kernel(last, state, normal_high, normal_low, progress, *refs):
    residual, now_state = refs[-2:]
    eye = unit(state.shape[0])
    largest = jnp.max(progress[1:2, :])
    careful = largest > 128.0
    now_state[...] = state[...]

    def step(scale):
        now, rest = split_bf16(now_state[...])
        residual[...] = eye - dot32(normal_high[...], now, NN) - dot32(normal_high[...], rest, NN)

        @pl.when(careful)
        def _():
            residual[...] -= dot32(normal_low[...], now, NN)

        upper, lower = split_bf16(residual[...])
        change = dot32(now, upper, NN)
        now_state[...] = scale * (now_state[...] + change)

        @pl.when(careful)
        def _():
            now_state[...] += scale * (dot32(now, lower, NN) + dot32(rest, upper, NN))

    def unfinished(carry):
        return (carry[0] > 2e-3) & (last | (carry[1] < SOME_STEPS))

    def body(carry):
        error, count = carry
        scale, left = centre(error)
        step(scale)
        return jnp.maximum(left, 0.05 * error), count + 1

    error, _ = lax.while_loop(unfinished, body, (jnp.max(progress[0:1, :]), jnp.int32(0)))
    if last:
        step(jnp.float32(1.0))
        refs[0][...], refs[1][...] = split_bf16(now_state[...])
    else:
        refs[0][...] = now_state[...]
        refs[1][0:1, :] = jnp.broadcast_to(error, (1, LANES))
        refs[1][1:2, :] = progress[1:2, :]


def unit(size):
    row = lax.broadcasted_iota(jnp.int32, (size, size), 0)
    return jnp.where(row == lax.broadcasted_iota(jnp.int32, (size, size), 1), 1.0, 0.0)


def centre(error):
    scale = 2.0 / (2.0 - error * error)
    return scale, scale - 1.0


def inverse_call(kernel, out_shape, out_specs, scratch, name, args):
    return pl.pallas_call(
        kernel,
        out_shape=out_shape,
        in_specs=[in_vmem()] * len(args),
        out_specs=out_specs,
        scratch_shapes=scratch,
        compiler_params=pltpu.CompilerParams(vmem_limit_bytes=SMALL_VMEM),
        cost_estimate=pl.CostEstimate(flops=1 << 30, bytes_accessed=8 << 20, transcendentals=0),
        name=name,
    )(*args)


def start_inverse(pair_rows, count):
    padded = pad_dates(count)
    full = jax.ShapeDtypeStruct((padded, padded), jnp.float32)
    half = jax.ShapeDtypeStruct((padded, padded), jnp.bfloat16)
    progress = jax.ShapeDtypeStruct((2, LANES), jnp.float32)
    return inverse_call(
        start_inverse_kernel,
        (full, half, half, progress),
        (in_vmem(),) * 4,
        [],
        "start_inverse",
        (pair_rows,),
    )


def go_on_inverse(state, normal_high, normal_low, progress, last):
    out_shape = (normal_high, normal_high) if last else (state, progress)
    full = pltpu.VMEM(state.shape, jnp.float32)
    return inverse_call(
        lambda *refs: go_on_inverse_kernel(last, *refs),
        tuple(jax.ShapeDtypeStruct(like.shape, like.dtype) for like in out_shape),
        (in_vmem(),) * 2,
        [full, full],
        "end_inverse" if last else "go_on_inverse",
        (state, normal_high, normal_low, progress),
    )


def solve_kernel(part, inverse_high, inverse_low, high, low, series):
    padded = high.shape[0]
    lane = lax.broadcasted_iota(jnp.int32, (padded, LANES), 1)
    width = LANES // SPLIT
    for half in range(2):
        cols = pl.ds((part * 2 + half) * SPLIT * LANES, SPLIT * LANES)
        solved = (
            dot32(inverse_high[...], high[:, cols], NN)
            + dot32(inverse_high[...], low[:, cols], NN)
            + dot32(inverse_low[...], high[:, cols], NN)
        )
        blocks = [solved[:, k * LANES : (k + 1) * LANES] for k in range(SPLIT)]
        for bit in (1, 2):
            shift = bit * width
            even = (lane // shift) % 2 == 0
            swapped = list(blocks)
            for k in range(SPLIT):
                if k & bit == 0:
                    first, second = blocks[k], blocks[k | bit]
                    swapped[k] = jnp.where(even, first, pltpu.roll(second, shift, 1))
                    swapped[k | bit] = jnp.where(even, pltpu.roll(first, LANES - shift, 1), second)
            blocks = swapped
        for k in range(SPLIT):
            series[half * SPLIT + k] = blocks[k]


def call_solve(part, inverse, values):
    padded = values[0].shape[0]
    return pl.pallas_call(
        lambda *refs: solve_kernel(part, *refs),
        out_shape=jax.ShapeDtypeStruct((8, padded, LANES), jnp.float32),
        in_specs=[in_vmem()] * 4,
        out_specs=in_vmem(),
        compiler_params=pltpu.CompilerParams(vmem_limit_bytes=SMALL_VMEM),
        cost_estimate=pl.CostEstimate(
            flops=6 * padded * padded * 16 * LANES, bytes_accessed=20 << 20, transcendentals=0
        ),
        name="solve",
    )(*inverse, *values)


def refine_kernel(count, row_total, col_total, *refs):
    (*series, moments, inverse_high, inverse_low, refined, held, sems) = refs
    padded = moments.shape[1]
    normal = [
        [moments[at : at + 1, count + k : count + k + 1] for k in range(3)] for at in range(3)
    ]

    def cyclic(row_at, col_at):
        a, b = (row_at + 1) % 3, (row_at + 2) % 3
        c, d = (col_at + 1) % 3, (col_at + 2) % 3
        return normal[a][c] * normal[b][d] - normal[a][d] * normal[b][c]

    cofacts = [[cyclic(row_at, col_at) for col_at in range(3)] for row_at in range(3)]
    determinant = sum(normal[0][k] * cofacts[0][k] for k in range(3))
    rows = []
    for part in range(2):
        for at in range(3):
            rows.append(
                sum(
                    (cofacts[k][at] / determinant) * moments[part * 3 + k : part * 3 + k + 1, :]
                    for k in range(3)
                )
            )
    rows.append(jnp.zeros((2, padded), jnp.float32))
    upper, lower = split_bf16(jnp.concatenate(rows, axis=0))
    ramps = (
        dot32(inverse_high[...], upper, NT)
        + dot32(inverse_high[...], lower, NT)
        + dot32(inverse_low[...], upper, NT)
    )[:count]
    lane = lax.broadcasted_iota(jnp.int32, (1, LANES), 1)
    x_row = centred(LANES * lax.axis_index("cols") + lane, col_total)
    row_start = 8 * lax.axis_index("dates")
    middle = (count // 2 + 7) // 8 * 8
    copies = []
    for at, (start, size) in enumerate(((0, middle), (middle, count - middle))):
        for part in range(2):
            level, along_y, along_x = (
                jnp.broadcast_to(
                    ramps[start : start + size, part * 3 + k : part * 3 + k + 1], (size, LANES)
                )
                for k in range(3)
            )
            level = level + along_x * x_row
            for row in range(8):
                y = centred(row_start + row, row_total)
                held[pl.ds(start * 16 + row * 2 + part, size, stride=16), :] = series[part][
                    row, start : start + size
                ] - (level + along_y * y)
        rows = pl.ds(start * 16, size * 16)
        copies.append(pltpu.make_async_copy(held.at[rows], refined.at[rows], sems.at[at]))
        copies[-1].start()
    for copy in copies:
        copy.wait()


def call_refine(series, moments, inverse, count, row_total, col_total):
    return pl.pallas_call(
        lambda *refs: refine_kernel(count, row_total, col_total, *refs),
        out_shape=jax.ShapeDtypeStruct((count * 16, LANES), jnp.float32),
        in_specs=[in_vmem()] * 5,
        out_specs=in_hbm(),
        scratch_shapes=[pltpu.VMEM((count * 16, LANES), jnp.float32), pltpu.SemaphoreType.DMA((2,))],
        compiler_params=pltpu.CompilerParams(vmem_limit_bytes=SMALL_VMEM),
        cost_estimate=pl.CostEstimate(flops=count * 16 * LANES * 6, bytes_accessed=16 << 20, transcendentals=0),
        name="refine",
    )(*series, moments, *inverse)


def sum_beside(value, state, work):
    cols = lax.axis_size("cols")
    pairings = [("dates", [(0, 1), (1, 0)])]
    bit = cols // 2
    while bit and not cols & (cols - 1):
        pairings.append(("cols", [(at, at ^ bit) for at in range(cols)]))
        bit //= 2
    for at in range(max(len(pairings), len(work))):
        value, state = lax.optimization_barrier((value, state))
        if at < len(pairings):
            other = lax.ppermute(value, *pairings[at])
        if at < len(work):
            state = work[at](state)
        if at < len(pairings):
            value = value + other
    if cols & (cols - 1):
        value = lax.psum(value, "cols")
    return value, state


def swap_dates(value):
    return lax.ppermute(value, "dates", [(0, 1), (1, 0)])


def two_halves(complex_images, pair_list):
    dates, rows, _, cols = complex_images.shape
    me = lax.axis_index("dates")
    half = rows // LOOKR // 2
    row_total, col_total = half * 2, cols // LOOKC * lax.axis_size("cols")
    images = complex_images.reshape(dates, rows, 2, SPLIT, cols // SPLIT)
    images = images.transpose(0, 1, 3, 2, 4).reshape(dates, rows // LOOKR, 16, LANES)
    first, second = pair_list[:, 0], pair_list[:, 1]
    low, base = dates * me, (dates - GAP) * me
    first_own = (first >= low) & (first < low + dates)
    second_own = (second >= low) & (second < low + dates)
    inside = (first_own & second_own).astype(jnp.int32)
    across = (first_own ^ second_own).astype(jnp.int32)
    packed = (first - base) | ((second - base) << 10)
    packed = jnp.where(first_own | second_own, packed | (inside << 20) | (across << 21), 0)

    edge = lax.dynamic_slice(
        images, ((dates - GAP) * (1 - me), half * (1 - me), 0, 0), (GAP, half, 16, LANES)
    )
    edge, packed = lax.optimization_barrier((edge, packed))
    halo = swap_dates(edge)
    other, listed, counts = call_pairs(packed, images)
    other, halo = lax.optimization_barrier((other, halo))
    other = swap_dates(other)
    own, own_weights = call_pairs(packed, images, (halo, listed, counts))
    own, pair_rows = lax.optimization_barrier((own, pair_list.T))
    started = start_inverse(pair_rows, dates * 2)
    own, started = lax.optimization_barrier((own, started))
    high, lowpart, moments = call_combine(own, own_weights, other, dates, row_total, col_total)

    def go_on(state):
        values, progress = go_on_inverse(*state, last=False)
        return (values,) + state[1:3] + (progress,)

    def end(state):
        return go_on_inverse(*state, last=True), ()

    def solve(state):
        inverse, solved = state
        return inverse, solved + (call_solve(len(solved), inverse, (high, lowpart)),)

    moments, (inverse, series) = sum_beside(moments, started, [go_on, go_on, end, solve, solve])
    refined = call_refine(series, moments, inverse, dates * 2, row_total, col_total)
    return refined.reshape(dates * 2, half, 2, LANES)


highest = lax.Precision.HIGHEST


def pseudo_inverse(pair_list, count):
    date_ids = jnp.arange(count, dtype=jnp.int32)
    design = (pair_list[:, 0:1] == date_ids[None, :]).astype(jnp.float32) - (
        pair_list[:, 1:2] == date_ids[None, :]
    ).astype(jnp.float32)
    normal = jnp.dot(design.T, design, precision=highest) + RIDGE * jnp.eye(
        count, dtype=jnp.float32
    )
    factor = jnp.linalg.cholesky(normal)
    return jax.scipy.linalg.cho_solve((factor, True), design.T)


def pool_looks(plane):
    count, rows, cols = plane.shape
    rows_pooled = jnp.sum(plane.reshape(count, rows // LOOKR, LOOKR, cols), axis=2)
    return jnp.sum(rows_pooled.reshape(count, rows // LOOKR, cols // LOOKC, LOOKC), axis=3)


def multilook_pairs(tile_stack, pair_list, pair_block):
    real_planes = tile_stack[:, :, 0, :]
    imag_planes = tile_stack[:, :, 1, :]
    groups = pair_list.reshape(-1, pair_block, 2)
    scale = 1.0 / float(LOOKR * LOOKC)

    def one_group(group):
        first_real = jnp.take(real_planes, group[:, 0], axis=0).astype(jnp.float32)
        first_imag = jnp.take(imag_planes, group[:, 0], axis=0).astype(jnp.float32)
        second_real = jnp.take(real_planes, group[:, 1], axis=0).astype(jnp.float32)
        second_imag = jnp.take(imag_planes, group[:, 1], axis=0).astype(jnp.float32)
        real_part = pool_looks(first_real * second_real + first_imag * second_imag)
        imag_part = pool_looks(first_imag * second_real - first_real * second_imag)
        return (jnp.stack([real_part, imag_part], axis=2) * scale).astype(jnp.bfloat16)

    looked = lax.map(one_group, groups)
    return looked.reshape((pair_list.shape[0],) + looked.shape[2:])


def coordinates(start, count, total):
    return (2.0 * (start + jnp.arange(count, dtype=jnp.int32)).astype(jnp.float32) + 1.0) / float(
        total
    ) - 1.0


def basis_planes(row_coord, col_coord):
    constant = jnp.ones((row_coord.shape[0], col_coord.shape[0]), jnp.float32)
    return jnp.stack([constant, row_coord[:, None] * constant, col_coord[None, :] * constant])


def weighted(widened, planes, pair_count):
    weights = jnp.sum(widened * widened, axis=(0, 2)) / float(pair_count)
    weighted_planes = planes * weights[None]
    normal = jnp.einsum("jrc,krc->jk", weighted_planes, planes, precision=highest)
    return (weighted_planes, normal)


def inverse3(matrix):

    def cyclic(row_at, col_at):
        return (
            matrix[(row_at + 1) % 3, (col_at + 1) % 3] * matrix[(row_at + 2) % 3, (col_at + 2) % 3]
            - matrix[(row_at + 1) % 3, (col_at + 2) % 3]
            * matrix[(row_at + 2) % 3, (col_at + 1) % 3]
        )

    cofacts = jnp.stack(
        [jnp.stack([cyclic(row_at, col_at) for col_at in range(3)]) for row_at in range(3)]
    )
    determinant = jnp.sum(matrix[0] * cofacts[0])
    return cofacts.T / determinant


def refine(series, ramp_rhs, normal, planes):
    ramp_coef = jnp.einsum("jk,dkh->djh", inverse3(normal), ramp_rhs, precision=highest)
    return series - jnp.einsum("djh,jrc->drhc", ramp_coef, planes, precision=highest)


def any_dates(complex_images, pair_list):
    date_count = lax.axis_size("dates")
    date_index = lax.axis_index("dates")
    col_index = lax.axis_index("cols")
    pair_count = pair_list.shape[0]
    date_total = complex_images.shape[0] * date_count
    rounded_pseudo = pseudo_inverse(pair_list, date_total).astype(jnp.bfloat16)
    regrouped = lax.all_to_all(complex_images, "dates", split_axis=1, concat_axis=0, tiled=True)
    interferograms = multilook_pairs(regrouped, pair_list, PAIR_BLOCK * date_count)
    ml_rows = interferograms.shape[1]
    ml_cols = interferograms.shape[3]
    planes = basis_planes(
        coordinates(date_index * ml_rows, ml_rows, ml_rows * date_count),
        coordinates(col_index * ml_cols, ml_cols, ml_cols * lax.axis_size("cols")),
    )
    widened = interferograms.astype(jnp.float32)
    weighted_planes, normal_part = weighted(widened, planes, pair_count)
    flat_pairs = interferograms.reshape(pair_count, -1)
    series = jnp.dot(rounded_pseudo, flat_pairs, preferred_element_type=jnp.float32).reshape(
        (date_total,) + interferograms.shape[1:]
    )
    rhs_part = jnp.einsum("jrc,drhc->djh", weighted_planes, series, precision=highest)
    normal, ramp_rhs = lax.psum((normal_part, rhs_part), ("dates", "cols"))
    return refine(series, ramp_rhs, normal, planes)


def solution(mesh):
    def body(complex_images, pair_list):
        dates, rows, _, cols = complex_images.shape
        if mesh.shape["dates"] == 2 and cols == LANES * LOOKC and rows == 32 and dates >= GAP:
            return two_halves(complex_images, pair_list)
        return any_dates(complex_images, pair_list)

    return jax.shard_map(
        body,
        mesh=mesh,
        in_specs=(P("dates", None, None, "cols"), P()),
        out_specs=P(None, "dates", None, "cols"),
        check_vma=False,
    )
```

```python
import jax
import jax.numpy as jnp
from jax import lax
from jax.experimental import pallas as pl
from jax.experimental.pallas import tpu as pltpu
from jax.sharding import PartitionSpec as P

LOOKR = 2
LOOKC = 4
PAIR_BLOCK = 37
GAP = 12
RIDGE = 0.5
MAX_STEP = 40
UNROLL = 16
LANES = 128
SPLIT = 4
SOME_STEPS = 2
PAIR_VMEM = 52 * 1024 * 1024
OWN_VMEM = 32 * 1024 * 1024
SMALL_VMEM = 12 * 1024 * 1024
NN = (((1,), (0,)), ((), ()))
NT = (((1,), (1,)), ((), ()))


def fill_looks(looks):
    row = lax.broadcasted_iota(jnp.int32, (looks.shape[0], 1), 0)
    lane, sub = row % LANES, row // LANES
    target = (lane % LOOKC) * LANES + sub * (LANES // SPLIT) + lane // LOOKC
    here = target == lax.broadcasted_iota(jnp.int32, looks.shape, 1)
    looks[...] = jnp.where(here, 1.0, 0.0).astype(jnp.bfloat16)


def split_bf16(value):
    high = value.astype(jnp.bfloat16)
    return high, (value - high.astype(jnp.float32)).astype(jnp.bfloat16)


def dot32(first, second, dims):
    return lax.dot_general(first, second, dims, preferred_element_type=jnp.float32)


def spread_looks(source, row, date, slot, step, looks, planes, choose=None, pairs=None, start=0, share=0, found=None):
    raw = source[pl.ds(date, step), pl.ds(row, 8)].reshape(step, 2, SPLIT, 16, LANES)
    left = jnp.concatenate(
        [raw[:, :, sub].reshape(step * 32, LANES) for sub in range(SPLIT)], axis=1
    )
    spread = dot32(left, looks[...], NN)
    for at in range(step):
        base = pl.multiple_of((slot + at) * 128, 128)
        for group in range(2):
            for rlook in range(LOOKR):
                top = (at * 2 + group) * 16 + rlook * 8
                for look in range(LOOKC):
                    planes[pl.ds(base + (rlook * LOOKC + look) * 16 + group * 8, 8), :] = spread[
                        top : top + 8, look * LANES : (look + 1) * LANES
                    ]
        for packed in [pairs[start + at * share + k] for k in range(share)]:
            found = choose(packed, found)
    return found


def pair_kernel(pair_count, with_halo, step, *refs):
    if with_halo:
        (listed, counts, images, halo, series, weights, planes, looks) = refs
    else:
        (pairs, images, series, listed, counts, raw, planes, looks, sems, sums) = refs
    dates = images.shape[0]
    steps = dates // step
    me = lax.axis_index("dates")
    row_start = 8 * (me if with_halo else 1 - me)
    own_slot, halo_slot = GAP * me, dates * (1 - me)
    copies = []
    if not with_halo:
        for at in range(steps):
            part = pl.ds(at * step, step)
            copies.append(
                pltpu.make_async_copy(images.at[part, pl.ds(row_start, 8)], raw.at[part], sems.at[at])
            )
    for copy in copies[:2]:
        copy.start()

    total = series if with_halo else sums
    spare = dates + GAP
    fill_looks(looks)
    total[...] = jnp.zeros_like(total)
    planes[pl.ds(spare * 128, 128), :] = jnp.zeros((128, LANES), jnp.float32)

    second_list = pair_count + UNROLL

    def choose(packed, found):
        listed[found[0]] = packed
        listed[second_list + found[1]] = packed
        return (found[0] + ((packed >> 20) & 1), found[1] + (packed >> 21))

    found = (jnp.int32(0), jnp.int32(0))
    share = 0 if with_halo else pair_count // dates
    for at in range(steps):
        if with_halo:
            source, row = images, row_start
        else:
            copies[at].wait()
            if at + 2 < steps:
                copies[at + 2].start()
            source, row = raw, 0
        found = spread_looks(
            source, row, at * step, own_slot + at * step, step, looks, planes,
            choose, None if with_halo else pairs, at * step * share, share, found,
        )
    if not with_halo:
        for at in range(dates * share, pair_count):
            found = choose(pairs[at], found)
        for part in range(2):
            counts[part] = found[part]
            for at in range(UNROLL):
                listed[part * second_list + found[part] + at] = jnp.int32(spare * 1025)
    if with_halo:
        spread_looks(halo, 0, 0, halo_slot, GAP, looks, planes)

    def one_pair(packed, power):
        first = packed & 1023
        second = (packed >> 10) & 1023
        a_row = pl.multiple_of(first * 128, 128)
        b_row = pl.multiple_of(second * 128, 128)
        terms_re, terms_im = [], []
        for look in range(LOOKR * LOOKC):
            a_re = planes[pl.ds(a_row + look * 16, 8, stride=2), :]
            a_im = planes[pl.ds(a_row + look * 16 + 1, 8, stride=2), :]
            b_re = planes[pl.ds(b_row + look * 16, 8, stride=2), :]
            b_im = planes[pl.ds(b_row + look * 16 + 1, 8, stride=2), :]
            terms_re.append(a_re * b_re + a_im * b_im)
            terms_im.append(a_im * b_re - a_re * b_im)
        while len(terms_re) > 1:
            terms_re = [terms_re[k] + terms_re[k + 1] for k in range(0, len(terms_re), 2)]
            terms_im = [terms_im[k] + terms_im[k + 1] for k in range(0, len(terms_im), 2)]
        real = terms_re[0].astype(jnp.bfloat16).astype(jnp.float32)
        imag = terms_im[0].astype(jnp.bfloat16).astype(jnp.float32)
        a_at = pl.multiple_of(first * 16, 16)
        b_at = pl.multiple_of(second * 16, 16)
        total[pl.ds(a_at, 8), :] += real
        total[pl.ds(a_at + 8, 8), :] += imag
        total[pl.ds(b_at, 8), :] -= real
        total[pl.ds(b_at + 8, 8), :] -= imag
        return power + (real * real + imag * imag)

    power = jnp.zeros((8, LANES), jnp.float32)
    for part in range(2 if with_halo else 1):

        def some_pairs(at, power, part=part):
            for k in range(UNROLL):
                power = one_pair(listed[part * second_list + at * UNROLL + k], power)
            return power

        power = lax.fori_loop(0, (counts[part] + UNROLL - 1) // UNROLL, some_pairs, power)
    scale = 1.0 / float(LOOKR * LOOKC)
    if with_halo:
        weights[...] = power * (scale * scale / float(pair_count))
    else:
        chains = 4 if dates % 4 == 0 else 1
        length = dates // chains

        def narrow(at, carries):
            left = []
            for chain, carry in enumerate(carries):
                date = chain * length + at
                value = sums[pl.ds(pl.multiple_of((own_slot + date) * 16, 16), 16), :] * scale + carry
                rounded = value.astype(jnp.bfloat16)
                series[pl.ds(pl.multiple_of(date * 16, 16), 16), :] = rounded
                left.append(value - rounded.astype(jnp.float32))
            return tuple(left)

        lax.fori_loop(0, length, narrow, (jnp.zeros((16, LANES), jnp.float32),) * chains)
        high, low = split_bf16(power * (scale * scale / float(pair_count)))
        series[pl.ds(dates * 16, 16), :] = jnp.concatenate(
            [high.astype(jnp.float32), low.astype(jnp.float32)], axis=0
        ).astype(jnp.bfloat16)


def in_vmem():
    return pl.BlockSpec(memory_space=pltpu.VMEM)


def in_smem():
    return pl.BlockSpec(memory_space=pltpu.SMEM)


def in_hbm():
    return pl.BlockSpec(memory_space=pl.ANY)


def call_pairs(pairs, images, given=None):
    dates = images.shape[0]
    pair_count = pairs.shape[0]
    step = max(k for k in range(1, MAX_STEP + 1) if dates % k == 0)
    slots = dates + GAP + 1
    scratch = [
        pltpu.VMEM((slots * 128, LANES), jnp.float32),
        pltpu.VMEM((SPLIT * LANES, LOOKC * LANES), jnp.bfloat16),
    ]
    sums = jax.ShapeDtypeStruct((slots * 16, LANES), jnp.float32)
    if given is not None:
        halo, listed, counts = given
        out_shape = (sums, jax.ShapeDtypeStruct((8, LANES), jnp.float32))
        in_specs = [in_smem()] * 2 + [in_vmem()] * 2
        out_specs = (in_vmem(), in_vmem())
        args = (listed, counts, images, halo)
    else:
        out_shape = (
            jax.ShapeDtypeStruct(((dates + 1) * 16, LANES), jnp.bfloat16),
            jax.ShapeDtypeStruct((2 * (pair_count + UNROLL),), jnp.int32),
            jax.ShapeDtypeStruct((2,), jnp.int32),
        )
        scratch = [pltpu.VMEM((dates, 8, 16, LANES), jnp.bfloat16)] + scratch
        scratch += [pltpu.SemaphoreType.DMA((dates // step,)), pltpu.VMEM(sums.shape, sums.dtype)]
        in_specs = [in_smem(), in_hbm()]
        out_specs = (in_vmem(), in_smem(), in_smem())
        args = (pairs, images)
    return pl.pallas_call(
        lambda *refs: pair_kernel(pair_count, given is not None, step, *refs),
        out_shape=out_shape,
        in_specs=in_specs,
        out_specs=out_specs,
        scratch_shapes=scratch,
        compiler_params=pltpu.CompilerParams(vmem_limit_bytes=PAIR_VMEM if given is None else OWN_VMEM),
        cost_estimate=pl.CostEstimate(
            flops=pair_count * 70 * 1024, bytes_accessed=pair_count * 48 * 1024, transcendentals=0
        ),
        name="pairs_other" if given is None else "pairs_own",
    )(*args)


def half_basis(row_start, col_start, row_total, col_total):
    sub = lax.broadcasted_iota(jnp.int32, (8, LANES), 0)
    lane = lax.broadcasted_iota(jnp.int32, (8, LANES), 1)
    width = LANES // SPLIT
    row = row_start + (sub // SPLIT) * SPLIT + lane // width
    col = col_start + (sub % SPLIT) * width + lane % width
    return centred(row, row_total), centred(col, col_total)


def centred(place, total):
    return (2.0 * place.astype(jnp.float32) + 1.0) / float(total) - 1.0


def combine_kernel(dates, row_total, col_total, *refs):
    (own, own_weights, other, high, low, moments, full, weighted_rows) = refs
    me = lax.axis_index("dates")
    count = dates * 2
    span = dates + GAP
    scale = 1.0 / float(LOOKR * LOOKC)

    def rows(start, size):
        return pl.ds(pl.multiple_of(start * 16, 16), size * 16)

    full[rows((dates - GAP) * me, span), :] = own[pl.ds(0, span * 16), :] * scale
    rest = dates - GAP
    full[rows(span * (1 - me), rest), :] = other[rows(GAP * (1 - me), rest), :].astype(jnp.float32)
    full[rows(dates - GAP * me, GAP), :] += other[rows(rest * me, GAP), :].astype(jnp.float32)
    y_plane, x_plane = half_basis(8 * me, LANES * lax.axis_index("cols"), row_total, col_total)
    basis = (jnp.ones((8, LANES), jnp.float32), y_plane, x_plane)
    padded = full.shape[0] // 16
    full[pl.ds(count * 16, (padded - count) * 16), :] = jnp.zeros(
        ((padded - count) * 16, LANES), jnp.float32
    )
    for at in range(3):
        full[pl.ds((count + at) * 16, 8), :] = basis[at]
    sent = other[pl.ds(dates * 16, 16), :].astype(jnp.float32)
    weights = own_weights[...] + (sent[:8] + sent[8:])
    weighted_rows[...] = jnp.zeros_like(weighted_rows)
    for at in range(3):
        plane = weights * basis[at]
        for part in range(2):
            for sub in range(8):
                weighted_rows[part * 3 + at : part * 3 + at + 1, pl.ds((part * 8 + sub) * LANES, LANES)] = (
                    plane[sub : sub + 1]
                )
    for at in range(16):
        value = full[pl.ds(at, padded, stride=16), :]
        upper, lower = split_bf16(value)
        high[:, at * LANES : (at + 1) * LANES] = upper
        low[:, at * LANES : (at + 1) * LANES] = lower
    upper, lower = split_bf16(weighted_rows[...])
    moments[...] = (
        dot32(upper, high[...], NT) + dot32(lower, high[...], NT) + dot32(upper, low[...], NT)
    )


def call_combine(own, own_weights, other, dates, row_total, col_total):
    padded = pad_dates(dates * 2)
    wide = jax.ShapeDtypeStruct((padded, 16 * LANES), jnp.bfloat16)
    return pl.pallas_call(
        lambda *refs: combine_kernel(dates, row_total, col_total, *refs),
        out_shape=(wide, wide, jax.ShapeDtypeStruct((8, padded), jnp.float32)),
        in_specs=[in_vmem()] * 3,
        out_specs=(in_vmem(),) * 3,
        scratch_shapes=[
            pltpu.VMEM((padded * 16, LANES), jnp.float32),
            pltpu.VMEM((8, 16 * LANES), jnp.float32),
        ],
        compiler_params=pltpu.CompilerParams(vmem_limit_bytes=SMALL_VMEM),
        cost_estimate=pl.CostEstimate(flops=padded * 8 * 12288, bytes_accessed=16 << 20, transcendentals=0),
        name="combine",
    )(own, own_weights, other)


def pad_dates(count):
    return (count + 3 + 15) // 16 * 16


def start_inverse_kernel(pairs, state, normal_high, normal_low, progress):
    padded = state.shape[0]
    date = lax.broadcasted_iota(jnp.int32, (padded, pairs.shape[1]), 0)
    design = (
        jnp.where(date == pairs[0:1, :], 1.0, 0.0) - jnp.where(date == pairs[1:2, :], 1.0, 0.0)
    ).astype(jnp.bfloat16)
    eye = unit(padded)
    normal = dot32(design, design, NT) + RIDGE * eye
    normal_high[...], normal_low[...] = split_bf16(normal)
    largest = jnp.max(jnp.sum(jnp.abs(normal), axis=1))
    scale, error = centre((largest - RIDGE) / (largest + RIDGE))
    first = 2.0 / (largest + RIDGE)
    state[...] = (scale * first) * (2.0 * eye - first * normal)
    progress[0:1, :] = jnp.broadcast_to(error, (1, LANES))
    progress[1:2, :] = jnp.broadcast_to(largest, (1, LANES))


def go_on_inverse_kernel(last, state, normal_high, normal_low, progress, *refs):
    residual, now_state = refs[-2:]
    eye = unit(state.shape[0])
    largest = jnp.max(progress[1:2, :])
    careful = largest > 128.0
    now_state[...] = state[...]

    def step(scale):
        now, rest = split_bf16(now_state[...])
        residual[...] = eye - dot32(normal_high[...], now, NN) - dot32(normal_high[...], rest, NN)

        @pl.when(careful)
        def _():
            residual[...] -= dot32(normal_low[...], now, NN)

        upper, lower = split_bf16(residual[...])
        change = dot32(now, upper, NN)
        now_state[...] = scale * (now_state[...] + change)

        @pl.when(careful)
        def _():
            now_state[...] += scale * (dot32(now, lower, NN) + dot32(rest, upper, NN))

    def unfinished(carry):
        return (carry[0] > 2e-3) & (last | (carry[1] < SOME_STEPS))

    def body(carry):
        error, count = carry
        scale, left = centre(error)
        step(scale)
        return jnp.maximum(left, 0.05 * error), count + 1

    error, _ = lax.while_loop(unfinished, body, (jnp.max(progress[0:1, :]), jnp.int32(0)))
    if last:
        step(jnp.float32(1.0))
        refs[0][...], refs[1][...] = split_bf16(now_state[...])
    else:
        refs[0][...] = now_state[...]
        refs[1][0:1, :] = jnp.broadcast_to(error, (1, LANES))
        refs[1][1:2, :] = progress[1:2, :]


def unit(size):
    row = lax.broadcasted_iota(jnp.int32, (size, size), 0)
    return jnp.where(row == lax.broadcasted_iota(jnp.int32, (size, size), 1), 1.0, 0.0)


def centre(error):
    scale = 2.0 / (2.0 - error * error)
    return scale, scale - 1.0


def inverse_call(kernel, out_shape, out_specs, scratch, name, args):
    return pl.pallas_call(
        kernel,
        out_shape=out_shape,
        in_specs=[in_vmem()] * len(args),
        out_specs=out_specs,
        scratch_shapes=scratch,
        compiler_params=pltpu.CompilerParams(vmem_limit_bytes=SMALL_VMEM),
        cost_estimate=pl.CostEstimate(flops=1 << 30, bytes_accessed=8 << 20, transcendentals=0),
        name=name,
    )(*args)


def start_inverse(pair_rows, count):
    padded = pad_dates(count)
    full = jax.ShapeDtypeStruct((padded, padded), jnp.float32)
    half = jax.ShapeDtypeStruct((padded, padded), jnp.bfloat16)
    progress = jax.ShapeDtypeStruct((2, LANES), jnp.float32)
    return inverse_call(
        start_inverse_kernel,
        (full, half, half, progress),
        (in_vmem(),) * 4,
        [],
        "start_inverse",
        (pair_rows,),
    )


def go_on_inverse(state, normal_high, normal_low, progress, last):
    out_shape = (normal_high, normal_high) if last else (state, progress)
    full = pltpu.VMEM(state.shape, jnp.float32)
    return inverse_call(
        lambda *refs: go_on_inverse_kernel(last, *refs),
        tuple(jax.ShapeDtypeStruct(like.shape, like.dtype) for like in out_shape),
        (in_vmem(),) * 2,
        [full, full],
        "end_inverse" if last else "go_on_inverse",
        (state, normal_high, normal_low, progress),
    )


def solve_kernel(part, inverse_high, inverse_low, high, low, series):
    padded = high.shape[0]
    lane = lax.broadcasted_iota(jnp.int32, (padded, LANES), 1)
    width = LANES // SPLIT
    for half in range(2):
        cols = pl.ds((part * 2 + half) * SPLIT * LANES, SPLIT * LANES)
        solved = (
            dot32(inverse_high[...], high[:, cols], NN)
            + dot32(inverse_high[...], low[:, cols], NN)
            + dot32(inverse_low[...], high[:, cols], NN)
        )
        blocks = [solved[:, k * LANES : (k + 1) * LANES] for k in range(SPLIT)]
        for bit in (1, 2):
            shift = bit * width
            even = (lane // shift) % 2 == 0
            swapped = list(blocks)
            for k in range(SPLIT):
                if k & bit == 0:
                    first, second = blocks[k], blocks[k | bit]
                    swapped[k] = jnp.where(even, first, pltpu.roll(second, shift, 1))
                    swapped[k | bit] = jnp.where(even, pltpu.roll(first, LANES - shift, 1), second)
            blocks = swapped
        for k in range(SPLIT):
            series[half * SPLIT + k] = blocks[k]


def call_solve(part, inverse, values):
    padded = values[0].shape[0]
    return pl.pallas_call(
        lambda *refs: solve_kernel(part, *refs),
        out_shape=jax.ShapeDtypeStruct((8, padded, LANES), jnp.float32),
        in_specs=[in_vmem()] * 4,
        out_specs=in_vmem(),
        compiler_params=pltpu.CompilerParams(vmem_limit_bytes=SMALL_VMEM),
        cost_estimate=pl.CostEstimate(
            flops=6 * padded * padded * 16 * LANES, bytes_accessed=20 << 20, transcendentals=0
        ),
        name="solve",
    )(*inverse, *values)


def refine_kernel(count, row_total, col_total, *refs):
    (*series, moments, inverse_high, inverse_low, refined, held, sems) = refs
    padded = moments.shape[1]
    normal = [
        [moments[at : at + 1, count + k : count + k + 1] for k in range(3)] for at in range(3)
    ]

    def cyclic(row_at, col_at):
        a, b = (row_at + 1) % 3, (row_at + 2) % 3
        c, d = (col_at + 1) % 3, (col_at + 2) % 3
        return normal[a][c] * normal[b][d] - normal[a][d] * normal[b][c]

    cofacts = [[cyclic(row_at, col_at) for col_at in range(3)] for row_at in range(3)]
    determinant = sum(normal[0][k] * cofacts[0][k] for k in range(3))
    rows = []
    for part in range(2):
        for at in range(3):
            rows.append(
                sum(
                    (cofacts[k][at] / determinant) * moments[part * 3 + k : part * 3 + k + 1, :]
                    for k in range(3)
                )
            )
    rows.append(jnp.zeros((2, padded), jnp.float32))
    upper, lower = split_bf16(jnp.concatenate(rows, axis=0))
    ramps = (
        dot32(inverse_high[...], upper, NT)
        + dot32(inverse_high[...], lower, NT)
        + dot32(inverse_low[...], upper, NT)
    )[:count]
    lane = lax.broadcasted_iota(jnp.int32, (1, LANES), 1)
    x_row = centred(LANES * lax.axis_index("cols") + lane, col_total)
    row_start = 8 * lax.axis_index("dates")
    middle = (count // 2 + 7) // 8 * 8
    copies = []
    for at, (start, size) in enumerate(((0, middle), (middle, count - middle))):
        for part in range(2):
            level, along_y, along_x = (
                jnp.broadcast_to(
                    ramps[start : start + size, part * 3 + k : part * 3 + k + 1], (size, LANES)
                )
                for k in range(3)
            )
            level = level + along_x * x_row
            for row in range(8):
                y = centred(row_start + row, row_total)
                held[pl.ds(start * 16 + row * 2 + part, size, stride=16), :] = series[part][
                    row, start : start + size
                ] - (level + along_y * y)
        rows = pl.ds(start * 16, size * 16)
        copies.append(pltpu.make_async_copy(held.at[rows], refined.at[rows], sems.at[at]))
        copies[-1].start()
    for copy in copies:
        copy.wait()


def call_refine(series, moments, inverse, count, row_total, col_total):
    return pl.pallas_call(
        lambda *refs: refine_kernel(count, row_total, col_total, *refs),
        out_shape=jax.ShapeDtypeStruct((count * 16, LANES), jnp.float32),
        in_specs=[in_vmem()] * 5,
        out_specs=in_hbm(),
        scratch_shapes=[pltpu.VMEM((count * 16, LANES), jnp.float32), pltpu.SemaphoreType.DMA((2,))],
        compiler_params=pltpu.CompilerParams(vmem_limit_bytes=SMALL_VMEM),
        cost_estimate=pl.CostEstimate(flops=count * 16 * LANES * 6, bytes_accessed=16 << 20, transcendentals=0),
        name="refine",
    )(*series, moments, *inverse)


def sum_beside(value, state, work):
    cols = lax.axis_size("cols")
    pairings = [("dates", [(0, 1), (1, 0)])]
    bit = cols // 2
    while bit and not cols & (cols - 1):
        pairings.append(("cols", [(at, at ^ bit) for at in range(cols)]))
        bit //= 2
    for at in range(max(len(pairings), len(work))):
        value, state = lax.optimization_barrier((value, state))
        if at < len(pairings):
            other = lax.ppermute(value, *pairings[at])
        if at < len(work):
            state = work[at](state)
        if at < len(pairings):
            value = value + other
    if cols & (cols - 1):
        value = lax.psum(value, "cols")
    return value, state


def swap_dates(value):
    return lax.ppermute(value, "dates", [(0, 1), (1, 0)])


def two_halves(complex_images, pair_list):
    dates, rows, _, cols = complex_images.shape
    me = lax.axis_index("dates")
    half = rows // LOOKR // 2
    row_total, col_total = half * 2, cols // LOOKC * lax.axis_size("cols")
    images = complex_images.reshape(dates, rows, 2, SPLIT, cols // SPLIT)
    images = images.transpose(0, 1, 3, 2, 4).reshape(dates, rows // LOOKR, 16, LANES)
    first, second = pair_list[:, 0], pair_list[:, 1]
    low, base = dates * me, (dates - GAP) * me
    first_own = (first >= low) & (first < low + dates)
    second_own = (second >= low) & (second < low + dates)
    inside = (first_own & second_own).astype(jnp.int32)
    across = (first_own ^ second_own).astype(jnp.int32)
    packed = (first - base) | ((second - base) << 10)
    packed = jnp.where(first_own | second_own, packed | (inside << 20) | (across << 21), 0)

    edge = lax.dynamic_slice(
        images, ((dates - GAP) * (1 - me), half * (1 - me), 0, 0), (GAP, half, 16, LANES)
    )
    edge, packed = lax.optimization_barrier((edge, packed))
    halo = swap_dates(edge)
    other, listed, counts = call_pairs(packed, images)
    other, halo = lax.optimization_barrier((other, halo))
    other = swap_dates(other)
    own, own_weights = call_pairs(packed, images, (halo, listed, counts))
    own, pair_rows = lax.optimization_barrier((own, pair_list.T))
    started = start_inverse(pair_rows, dates * 2)
    own, started = lax.optimization_barrier((own, started))
    high, lowpart, moments = call_combine(own, own_weights, other, dates, row_total, col_total)

    def go_on(state):
        values, progress = go_on_inverse(*state, last=False)
        return (values,) + state[1:3] + (progress,)

    def end(state):
        return go_on_inverse(*state, last=True), ()

    def solve(state):
        inverse, solved = state
        return inverse, solved + (call_solve(len(solved), inverse, (high, lowpart)),)

    moments, (inverse, series) = sum_beside(moments, started, [go_on, go_on, end, solve, solve])
    refined = call_refine(series, moments, inverse, dates * 2, row_total, col_total)
    return refined.reshape(dates * 2, half, 2, LANES)


highest = lax.Precision.HIGHEST


def pseudo_inverse(pair_list, count):
    date_ids = jnp.arange(count, dtype=jnp.int32)
    design = (pair_list[:, 0:1] == date_ids[None, :]).astype(jnp.float32) - (
        pair_list[:, 1:2] == date_ids[None, :]
    ).astype(jnp.float32)
    normal = jnp.dot(design.T, design, precision=highest) + RIDGE * jnp.eye(
        count, dtype=jnp.float32
    )
    factor = jnp.linalg.cholesky(normal)
    return jax.scipy.linalg.cho_solve((factor, True), design.T)


def pool_looks(plane):
    count, rows, cols = plane.shape
    rows_pooled = jnp.sum(plane.reshape(count, rows // LOOKR, LOOKR, cols), axis=2)
    return jnp.sum(rows_pooled.reshape(count, rows // LOOKR, cols // LOOKC, LOOKC), axis=3)


def multilook_pairs(tile_stack, pair_list, pair_block):
    real_planes = tile_stack[:, :, 0, :]
    imag_planes = tile_stack[:, :, 1, :]
    groups = pair_list.reshape(-1, pair_block, 2)
    scale = 1.0 / float(LOOKR * LOOKC)

    def one_group(group):
        first_real = jnp.take(real_planes, group[:, 0], axis=0).astype(jnp.float32)
        first_imag = jnp.take(imag_planes, group[:, 0], axis=0).astype(jnp.float32)
        second_real = jnp.take(real_planes, group[:, 1], axis=0).astype(jnp.float32)
        second_imag = jnp.take(imag_planes, group[:, 1], axis=0).astype(jnp.float32)
        real_part = pool_looks(first_real * second_real + first_imag * second_imag)
        imag_part = pool_looks(first_imag * second_real - first_real * second_imag)
        return (jnp.stack([real_part, imag_part], axis=2) * scale).astype(jnp.bfloat16)

    looked = lax.map(one_group, groups)
    return looked.reshape((pair_list.shape[0],) + looked.shape[2:])


def coordinates(start, count, total):
    return (2.0 * (start + jnp.arange(count, dtype=jnp.int32)).astype(jnp.float32) + 1.0) / float(
        total
    ) - 1.0


def basis_planes(row_coord, col_coord):
    constant = jnp.ones((row_coord.shape[0], col_coord.shape[0]), jnp.float32)
    return jnp.stack([constant, row_coord[:, None] * constant, col_coord[None, :] * constant])


def weighted(widened, planes, pair_count):
    weights = jnp.sum(widened * widened, axis=(0, 2)) / float(pair_count)
    weighted_planes = planes * weights[None]
    normal = jnp.einsum("jrc,krc->jk", weighted_planes, planes, precision=highest)
    return (weighted_planes, normal)


def inverse3(matrix):

    def cyclic(row_at, col_at):
        return (
            matrix[(row_at + 1) % 3, (col_at + 1) % 3] * matrix[(row_at + 2) % 3, (col_at + 2) % 3]
            - matrix[(row_at + 1) % 3, (col_at + 2) % 3]
            * matrix[(row_at + 2) % 3, (col_at + 1) % 3]
        )

    cofacts = jnp.stack(
        [jnp.stack([cyclic(row_at, col_at) for col_at in range(3)]) for row_at in range(3)]
    )
    determinant = jnp.sum(matrix[0] * cofacts[0])
    return cofacts.T / determinant


def refine(series, ramp_rhs, normal, planes):
    ramp_coef = jnp.einsum("jk,dkh->djh", inverse3(normal), ramp_rhs, precision=highest)
    return series - jnp.einsum("djh,jrc->drhc", ramp_coef, planes, precision=highest)


def any_dates(complex_images, pair_list):
    date_count = lax.axis_size("dates")
    date_index = lax.axis_index("dates")
    col_index = lax.axis_index("cols")
    pair_count = pair_list.shape[0]
    date_total = complex_images.shape[0] * date_count
    rounded_pseudo = pseudo_inverse(pair_list, date_total).astype(jnp.bfloat16)
    regrouped = lax.all_to_all(complex_images, "dates", split_axis=1, concat_axis=0, tiled=True)
    interferograms = multilook_pairs(regrouped, pair_list, PAIR_BLOCK * date_count)
    ml_rows = interferograms.shape[1]
    ml_cols = interferograms.shape[3]
    planes = basis_planes(
        coordinates(date_index * ml_rows, ml_rows, ml_rows * date_count),
        coordinates(col_index * ml_cols, ml_cols, ml_cols * lax.axis_size("cols")),
    )
    widened = interferograms.astype(jnp.float32)
    weighted_planes, normal_part = weighted(widened, planes, pair_count)
    flat_pairs = interferograms.reshape(pair_count, -1)
    series = jnp.dot(rounded_pseudo, flat_pairs, preferred_element_type=jnp.float32).reshape(
        (date_total,) + interferograms.shape[1:]
    )
    rhs_part = jnp.einsum("jrc,drhc->djh", weighted_planes, series, precision=highest)
    normal, ramp_rhs = lax.psum((normal_part, rhs_part), ("dates", "cols"))
    return refine(series, ramp_rhs, normal, planes)


def solution(mesh):
    def body(complex_images, pair_list):
        dates, rows, _, cols = complex_images.shape
        if mesh.shape["dates"] == 2 and cols == LANES * LOOKC and rows == 32 and dates >= GAP:
            return two_halves(complex_images, pair_list)
        return any_dates(complex_images, pair_list)

    return jax.shard_map(
        body,
        mesh=mesh,
        in_specs=(P("dates", None, None, "cols"), P()),
        out_specs=P(None, "dates", None, "cols"),
        check_vma=False,
    )
```

```python
import jax
import jax.numpy as jnp
from jax import lax
from jax.experimental import pallas as pl
from jax.experimental.pallas import tpu as pltpu
from jax.sharding import PartitionSpec as P

LOOKR = 2
LOOKC = 4
PAIR_BLOCK = 37
GAP = 12
RIDGE = 0.5
MAX_STEP = 40
UNROLL = 16
LANES = 128
SPLIT = 4
SOME_STEPS = 2
PAIR_VMEM = 52 * 1024 * 1024
OWN_VMEM = 32 * 1024 * 1024
SMALL_VMEM = 12 * 1024 * 1024
NN = (((1,), (0,)), ((), ()))
NT = (((1,), (1,)), ((), ()))


def fill_looks(looks):
    row = lax.broadcasted_iota(jnp.int32, (looks.shape[0], 1), 0)
    lane, sub = row % LANES, row // LANES
    target = (lane % LOOKC) * LANES + sub * (LANES // SPLIT) + lane // LOOKC
    here = target == lax.broadcasted_iota(jnp.int32, looks.shape, 1)
    looks[...] = jnp.where(here, 1.0, 0.0).astype(jnp.bfloat16)


def split_bf16(value):
    high = value.astype(jnp.bfloat16)
    return high, (value - high.astype(jnp.float32)).astype(jnp.bfloat16)


def dot32(first, second, dims):
    return lax.dot_general(first, second, dims, preferred_element_type=jnp.float32)


def spread_looks(source, row, date, slot, step, looks, planes, choose=None, start=0, share=0, found=None):
    raw = source[pl.ds(date, step), pl.ds(row, 8)].reshape(step, 2, SPLIT, 16, LANES)
    left = jnp.concatenate(
        [raw[:, :, sub].reshape(step * 32, LANES) for sub in range(SPLIT)], axis=1
    )
    spread = dot32(left, looks[...], NN)
    for at in range(step):
        base = pl.multiple_of((slot + at) * 128, 128)
        for group in range(2):
            for rlook in range(LOOKR):
                top = (at * 2 + group) * 16 + rlook * 8
                for look in range(LOOKC):
                    planes[pl.ds(base + (rlook * LOOKC + look) * 16 + group * 8, 8), :] = spread[
                        top : top + 8, look * LANES : (look + 1) * LANES
                    ]
        for k in range(share):
            found = choose(start + at * share + k, found)
    return found


def pair_kernel(pair_count, with_halo, step, *refs):
    if with_halo:
        (listed, counts, images, halo, series, weights, planes, looks) = refs
    else:
        (pairs, images, series, listed, counts, raw, planes, looks, sems, sums) = refs
    dates = images.shape[0]
    steps = dates // step
    me = lax.axis_index("dates")
    row_start = 8 * (me if with_halo else 1 - me)
    own_slot, halo_slot = GAP * me, dates * (1 - me)
    copies = []
    if not with_halo:
        for at in range(steps):
            part = pl.ds(at * step, step)
            copies.append(
                pltpu.make_async_copy(images.at[part, pl.ds(row_start, 8)], raw.at[part], sems.at[at])
            )
    for copy in copies:
        copy.start()

    total = series if with_halo else sums
    spare = dates + GAP
    fill_looks(looks)
    total[...] = jnp.zeros_like(total)
    planes[pl.ds(spare * 128, 128), :] = jnp.zeros((128, LANES), jnp.float32)

    second_list = pair_count + UNROLL

    def choose(at, found):
        packed = pairs[at]
        listed[found[0]] = packed
        listed[second_list + found[1]] = packed
        return (found[0] + ((packed >> 20) & 1), found[1] + (packed >> 21))

    found = (jnp.int32(0), jnp.int32(0))
    early = min(2 * dates, pair_count)
    share = 0 if with_halo else (pair_count - early) // dates
    if not with_halo:
        found = lax.fori_loop(0, early, choose, found, unroll=8)
    for at in range(steps):
        if with_halo:
            source, row = images, row_start
        else:
            copies[at].wait()
            source, row = raw, 0
        found = spread_looks(
            source, row, at * step, own_slot + at * step, step, looks, planes,
            choose, early + at * step * share, share, found,
        )
    if not with_halo:
        for at in range(early + dates * share, pair_count):
            found = choose(at, found)
        for part in range(2):
            counts[part] = found[part]
            for at in range(UNROLL):
                listed[part * second_list + found[part] + at] = jnp.int32(spare * 1025)
    if with_halo:
        spread_looks(halo, 0, 0, halo_slot, GAP, looks, planes)

    def one_pair(packed, power):
        first = packed & 1023
        second = (packed >> 10) & 1023
        a_row = pl.multiple_of(first * 128, 128)
        b_row = pl.multiple_of(second * 128, 128)
        terms_re, terms_im = [], []
        for look in range(LOOKR * LOOKC):
            a_re = planes[pl.ds(a_row + look * 16, 8, stride=2), :]
            a_im = planes[pl.ds(a_row + look * 16 + 1, 8, stride=2), :]
            b_re = planes[pl.ds(b_row + look * 16, 8, stride=2), :]
            b_im = planes[pl.ds(b_row + look * 16 + 1, 8, stride=2), :]
            terms_re.append(a_re * b_re + a_im * b_im)
            terms_im.append(a_im * b_re - a_re * b_im)
        while len(terms_re) > 1:
            terms_re = [terms_re[k] + terms_re[k + 1] for k in range(0, len(terms_re), 2)]
            terms_im = [terms_im[k] + terms_im[k + 1] for k in range(0, len(terms_im), 2)]
        real = terms_re[0].astype(jnp.bfloat16).astype(jnp.float32)
        imag = terms_im[0].astype(jnp.bfloat16).astype(jnp.float32)
        a_at = pl.multiple_of(first * 16, 16)
        b_at = pl.multiple_of(second * 16, 16)
        total[pl.ds(a_at, 8), :] += real
        total[pl.ds(a_at + 8, 8), :] += imag
        total[pl.ds(b_at, 8), :] -= real
        total[pl.ds(b_at + 8, 8), :] -= imag
        return power + (real * real + imag * imag)

    power = jnp.zeros((8, LANES), jnp.float32)
    for part in range(2 if with_halo else 1):

        def some_pairs(at, power, part=part):
            for k in range(UNROLL):
                power = one_pair(listed[part * second_list + at * UNROLL + k], power)
            return power

        power = lax.fori_loop(0, (counts[part] + UNROLL - 1) // UNROLL, some_pairs, power)
    scale = 1.0 / float(LOOKR * LOOKC)
    if with_halo:
        weights[...] = power * (scale * scale / float(pair_count))
    else:
        chains = 4 if dates % 4 == 0 else 1
        length = dates // chains

        def narrow(at, carries):
            left = []
            for chain, carry in enumerate(carries):
                date = chain * length + at
                value = sums[pl.ds(pl.multiple_of((own_slot + date) * 16, 16), 16), :] * scale + carry
                rounded = value.astype(jnp.bfloat16)
                series[pl.ds(pl.multiple_of(date * 16, 16), 16), :] = rounded
                left.append(value - rounded.astype(jnp.float32))
            return tuple(left)

        lax.fori_loop(0, length, narrow, (jnp.zeros((16, LANES), jnp.float32),) * chains)
        high, low = split_bf16(power * (scale * scale / float(pair_count)))
        series[pl.ds(dates * 16, 16), :] = jnp.concatenate(
            [high.astype(jnp.float32), low.astype(jnp.float32)], axis=0
        ).astype(jnp.bfloat16)


def in_vmem():
    return pl.BlockSpec(memory_space=pltpu.VMEM)


def in_smem():
    return pl.BlockSpec(memory_space=pltpu.SMEM)


def in_hbm():
    return pl.BlockSpec(memory_space=pl.ANY)


def call_pairs(pairs, images, given=None):
    dates = images.shape[0]
    pair_count = pairs.shape[0]
    step = max(k for k in range(1, MAX_STEP + 1) if dates % k == 0)
    slots = dates + GAP + 1
    scratch = [
        pltpu.VMEM((slots * 128, LANES), jnp.float32),
        pltpu.VMEM((SPLIT * LANES, LOOKC * LANES), jnp.bfloat16),
    ]
    sums = jax.ShapeDtypeStruct((slots * 16, LANES), jnp.float32)
    if given is not None:
        halo, listed, counts = given
        out_shape = (sums, jax.ShapeDtypeStruct((8, LANES), jnp.float32))
        in_specs = [in_smem()] * 2 + [in_vmem()] * 2
        out_specs = (in_vmem(), in_vmem())
        args = (listed, counts, images, halo)
    else:
        out_shape = (
            jax.ShapeDtypeStruct(((dates + 1) * 16, LANES), jnp.bfloat16),
            jax.ShapeDtypeStruct((2 * (pair_count + UNROLL),), jnp.int32),
            jax.ShapeDtypeStruct((2,), jnp.int32),
        )
        scratch = [pltpu.VMEM((dates, 8, 16, LANES), jnp.bfloat16)] + scratch
        scratch += [pltpu.SemaphoreType.DMA((dates // step,)), pltpu.VMEM(sums.shape, sums.dtype)]
        in_specs = [in_smem(), in_hbm()]
        out_specs = (in_vmem(), in_smem(), in_smem())
        args = (pairs, images)
    return pl.pallas_call(
        lambda *refs: pair_kernel(pair_count, given is not None, step, *refs),
        out_shape=out_shape,
        in_specs=in_specs,
        out_specs=out_specs,
        scratch_shapes=scratch,
        compiler_params=pltpu.CompilerParams(vmem_limit_bytes=PAIR_VMEM if given is None else OWN_VMEM),
        cost_estimate=pl.CostEstimate(
            flops=pair_count * 70 * 1024, bytes_accessed=pair_count * 48 * 1024, transcendentals=0
        ),
        name="pairs_other" if given is None else "pairs_own",
    )(*args)


def half_basis(row_start, col_start, row_total, col_total):
    sub = lax.broadcasted_iota(jnp.int32, (8, LANES), 0)
    lane = lax.broadcasted_iota(jnp.int32, (8, LANES), 1)
    width = LANES // SPLIT
    row = row_start + (sub // SPLIT) * SPLIT + lane // width
    col = col_start + (sub % SPLIT) * width + lane % width
    return centred(row, row_total), centred(col, col_total)


def centred(place, total):
    return (2.0 * place.astype(jnp.float32) + 1.0) / float(total) - 1.0


def combine_kernel(dates, row_total, col_total, *refs):
    (own, own_weights, other, high, low, moments, full, weighted_rows) = refs
    me = lax.axis_index("dates")
    count = dates * 2
    span = dates + GAP
    scale = 1.0 / float(LOOKR * LOOKC)

    def rows(start, size):
        return pl.ds(pl.multiple_of(start * 16, 16), size * 16)

    full[rows((dates - GAP) * me, span), :] = own[pl.ds(0, span * 16), :] * scale
    rest = dates - GAP
    full[rows(span * (1 - me), rest), :] = other[rows(GAP * (1 - me), rest), :].astype(jnp.float32)
    full[rows(dates - GAP * me, GAP), :] += other[rows(rest * me, GAP), :].astype(jnp.float32)
    y_plane, x_plane = half_basis(8 * me, LANES * lax.axis_index("cols"), row_total, col_total)
    basis = (jnp.ones((8, LANES), jnp.float32), y_plane, x_plane)
    padded = full.shape[0] // 16
    full[pl.ds(count * 16, (padded - count) * 16), :] = jnp.zeros(
        ((padded - count) * 16, LANES), jnp.float32
    )
    for at in range(3):
        full[pl.ds((count + at) * 16, 8), :] = basis[at]
    sent = other[pl.ds(dates * 16, 16), :].astype(jnp.float32)
    weights = own_weights[...] + (sent[:8] + sent[8:])
    weighted_rows[...] = jnp.zeros_like(weighted_rows)
    for at in range(3):
        plane = weights * basis[at]
        for part in range(2):
            for sub in range(8):
                weighted_rows[part * 3 + at : part * 3 + at + 1, pl.ds((part * 8 + sub) * LANES, LANES)] = (
                    plane[sub : sub + 1]
                )
    for at in range(16):
        value = full[pl.ds(at, padded, stride=16), :]
        upper, lower = split_bf16(value)
        high[:, at * LANES : (at + 1) * LANES] = upper
        low[:, at * LANES : (at + 1) * LANES] = lower
    upper, lower = split_bf16(weighted_rows[...])
    moments[...] = (
        dot32(upper, high[...], NT) + dot32(lower, high[...], NT) + dot32(upper, low[...], NT)
    )


def call_combine(own, own_weights, other, dates, row_total, col_total):
    padded = pad_dates(dates * 2)
    wide = jax.ShapeDtypeStruct((padded, 16 * LANES), jnp.bfloat16)
    return pl.pallas_call(
        lambda *refs: combine_kernel(dates, row_total, col_total, *refs),
        out_shape=(wide, wide, jax.ShapeDtypeStruct((8, padded), jnp.float32)),
        in_specs=[in_vmem()] * 3,
        out_specs=(in_vmem(),) * 3,
        scratch_shapes=[
            pltpu.VMEM((padded * 16, LANES), jnp.float32),
            pltpu.VMEM((8, 16 * LANES), jnp.float32),
        ],
        compiler_params=pltpu.CompilerParams(vmem_limit_bytes=SMALL_VMEM),
        cost_estimate=pl.CostEstimate(flops=padded * 8 * 12288, bytes_accessed=16 << 20, transcendentals=0),
        name="combine",
    )(own, own_weights, other)


def pad_dates(count):
    return (count + 3 + 15) // 16 * 16


def start_inverse_kernel(pairs, state, normal_high, normal_low, progress):
    padded = state.shape[0]
    date = lax.broadcasted_iota(jnp.int32, (padded, pairs.shape[1]), 0)
    design = (
        jnp.where(date == pairs[0:1, :], 1.0, 0.0) - jnp.where(date == pairs[1:2, :], 1.0, 0.0)
    ).astype(jnp.bfloat16)
    eye = unit(padded)
    normal = dot32(design, design, NT) + RIDGE * eye
    normal_high[...], normal_low[...] = split_bf16(normal)
    largest = jnp.max(jnp.sum(jnp.abs(normal), axis=1))
    scale, error = centre((largest - RIDGE) / (largest + RIDGE))
    first = 2.0 / (largest + RIDGE)
    state[...] = (scale * first) * (2.0 * eye - first * normal)
    progress[0:1, :] = jnp.broadcast_to(error, (1, LANES))
    progress[1:2, :] = jnp.broadcast_to(largest, (1, LANES))


def go_on_inverse_kernel(last, state, normal_high, normal_low, progress, *refs):
    residual, now_state = refs[-2:]
    eye = unit(state.shape[0])
    largest = jnp.max(progress[1:2, :])
    careful = largest > 128.0
    now_state[...] = state[...]

    def step(scale):
        now, rest = split_bf16(now_state[...])
        residual[...] = eye - dot32(normal_high[...], now, NN) - dot32(normal_high[...], rest, NN)

        @pl.when(careful)
        def _():
            residual[...] -= dot32(normal_low[...], now, NN)

        upper, lower = split_bf16(residual[...])
        change = dot32(now, upper, NN)
        now_state[...] = scale * (now_state[...] + change)

        @pl.when(careful)
        def _():
            now_state[...] += scale * (dot32(now, lower, NN) + dot32(rest, upper, NN))

    def unfinished(carry):
        return (carry[0] > 2e-3) & (last | (carry[1] < SOME_STEPS))

    def body(carry):
        error, count = carry
        scale, left = centre(error)
        step(scale)
        return jnp.maximum(left, 0.05 * error), count + 1

    error, _ = lax.while_loop(unfinished, body, (jnp.max(progress[0:1, :]), jnp.int32(0)))
    if last:
        step(jnp.float32(1.0))
        refs[0][...], refs[1][...] = split_bf16(now_state[...])
    else:
        refs[0][...] = now_state[...]
        refs[1][0:1, :] = jnp.broadcast_to(error, (1, LANES))
        refs[1][1:2, :] = progress[1:2, :]


def unit(size):
    row = lax.broadcasted_iota(jnp.int32, (size, size), 0)
    return jnp.where(row == lax.broadcasted_iota(jnp.int32, (size, size), 1), 1.0, 0.0)


def centre(error):
    scale = 2.0 / (2.0 - error * error)
    return scale, scale - 1.0


def inverse_call(kernel, out_shape, out_specs, scratch, name, args):
    return pl.pallas_call(
        kernel,
        out_shape=out_shape,
        in_specs=[in_vmem()] * len(args),
        out_specs=out_specs,
        scratch_shapes=scratch,
        compiler_params=pltpu.CompilerParams(vmem_limit_bytes=SMALL_VMEM),
        cost_estimate=pl.CostEstimate(flops=1 << 30, bytes_accessed=8 << 20, transcendentals=0),
        name=name,
    )(*args)


def start_inverse(pair_rows, count):
    padded = pad_dates(count)
    full = jax.ShapeDtypeStruct((padded, padded), jnp.float32)
    half = jax.ShapeDtypeStruct((padded, padded), jnp.bfloat16)
    progress = jax.ShapeDtypeStruct((2, LANES), jnp.float32)
    return inverse_call(
        start_inverse_kernel,
        (full, half, half, progress),
        (in_vmem(),) * 4,
        [],
        "start_inverse",
        (pair_rows,),
    )


def go_on_inverse(state, normal_high, normal_low, progress, last):
    out_shape = (normal_high, normal_high) if last else (state, progress)
    full = pltpu.VMEM(state.shape, jnp.float32)
    return inverse_call(
        lambda *refs: go_on_inverse_kernel(last, *refs),
        tuple(jax.ShapeDtypeStruct(like.shape, like.dtype) for like in out_shape),
        (in_vmem(),) * 2,
        [full, full],
        "end_inverse" if last else "go_on_inverse",
        (state, normal_high, normal_low, progress),
    )


def solve_kernel(part, inverse_high, inverse_low, high, low, series):
    padded = high.shape[0]
    lane = lax.broadcasted_iota(jnp.int32, (padded, LANES), 1)
    width = LANES // SPLIT
    for half in range(2):
        cols = pl.ds((part * 2 + half) * SPLIT * LANES, SPLIT * LANES)
        solved = (
            dot32(inverse_high[...], high[:, cols], NN)
            + dot32(inverse_high[...], low[:, cols], NN)
            + dot32(inverse_low[...], high[:, cols], NN)
        )
        blocks = [solved[:, k * LANES : (k + 1) * LANES] for k in range(SPLIT)]
        for bit in (1, 2):
            shift = bit * width
            even = (lane // shift) % 2 == 0
            swapped = list(blocks)
            for k in range(SPLIT):
                if k & bit == 0:
                    first, second = blocks[k], blocks[k | bit]
                    swapped[k] = jnp.where(even, first, pltpu.roll(second, shift, 1))
                    swapped[k | bit] = jnp.where(even, pltpu.roll(first, LANES - shift, 1), second)
            blocks = swapped
        for k in range(SPLIT):
            series[half * SPLIT + k] = blocks[k]


def call_solve(part, inverse, values):
    padded = values[0].shape[0]
    return pl.pallas_call(
        lambda *refs: solve_kernel(part, *refs),
        out_shape=jax.ShapeDtypeStruct((8, padded, LANES), jnp.float32),
        in_specs=[in_vmem()] * 4,
        out_specs=in_vmem(),
        compiler_params=pltpu.CompilerParams(vmem_limit_bytes=SMALL_VMEM),
        cost_estimate=pl.CostEstimate(
            flops=6 * padded * padded * 16 * LANES, bytes_accessed=20 << 20, transcendentals=0
        ),
        name="solve",
    )(*inverse, *values)


def refine_kernel(count, row_total, col_total, *refs):
    (*series, moments, inverse_high, inverse_low, refined, held, sems) = refs
    padded = moments.shape[1]
    normal = [
        [moments[at : at + 1, count + k : count + k + 1] for k in range(3)] for at in range(3)
    ]

    def cyclic(row_at, col_at):
        a, b = (row_at + 1) % 3, (row_at + 2) % 3
        c, d = (col_at + 1) % 3, (col_at + 2) % 3
        return normal[a][c] * normal[b][d] - normal[a][d] * normal[b][c]

    cofacts = [[cyclic(row_at, col_at) for col_at in range(3)] for row_at in range(3)]
    determinant = sum(normal[0][k] * cofacts[0][k] for k in range(3))
    rows = []
    for part in range(2):
        for at in range(3):
            rows.append(
                sum(
                    (cofacts[k][at] / determinant) * moments[part * 3 + k : part * 3 + k + 1, :]
                    for k in range(3)
                )
            )
    rows.append(jnp.zeros((2, padded), jnp.float32))
    upper, lower = split_bf16(jnp.concatenate(rows, axis=0))
    ramps = (
        dot32(inverse_high[...], upper, NT)
        + dot32(inverse_high[...], lower, NT)
        + dot32(inverse_low[...], upper, NT)
    )[:count]
    lane = lax.broadcasted_iota(jnp.int32, (1, LANES), 1)
    x_row = centred(LANES * lax.axis_index("cols") + lane, col_total)
    row_start = 8 * lax.axis_index("dates")
    middle = (count // 2 + 7) // 8 * 8
    copies = []
    for at, (start, size) in enumerate(((0, middle), (middle, count - middle))):
        for part in range(2):
            level, along_y, along_x = (
                jnp.broadcast_to(
                    ramps[start : start + size, part * 3 + k : part * 3 + k + 1], (size, LANES)
                )
                for k in range(3)
            )
            level = level + along_x * x_row
            for row in range(8):
                y = centred(row_start + row, row_total)
                held[pl.ds(start * 16 + row * 2 + part, size, stride=16), :] = series[part][
                    row, start : start + size
                ] - (level + along_y * y)
        rows = pl.ds(start * 16, size * 16)
        copies.append(pltpu.make_async_copy(held.at[rows], refined.at[rows], sems.at[at]))
        copies[-1].start()
    for copy in copies:
        copy.wait()


def call_refine(series, moments, inverse, count, row_total, col_total):
    return pl.pallas_call(
        lambda *refs: refine_kernel(count, row_total, col_total, *refs),
        out_shape=jax.ShapeDtypeStruct((count * 16, LANES), jnp.float32),
        in_specs=[in_vmem()] * 5,
        out_specs=in_hbm(),
        scratch_shapes=[pltpu.VMEM((count * 16, LANES), jnp.float32), pltpu.SemaphoreType.DMA((2,))],
        compiler_params=pltpu.CompilerParams(vmem_limit_bytes=SMALL_VMEM),
        cost_estimate=pl.CostEstimate(flops=count * 16 * LANES * 6, bytes_accessed=16 << 20, transcendentals=0),
        name="refine",
    )(*series, moments, *inverse)


def sum_beside(value, state, work):
    cols = lax.axis_size("cols")
    pairings = [("dates", [(0, 1), (1, 0)])]
    bit = cols // 2
    while bit and not cols & (cols - 1):
        pairings.append(("cols", [(at, at ^ bit) for at in range(cols)]))
        bit //= 2
    for at in range(max(len(pairings), len(work))):
        value, state = lax.optimization_barrier((value, state))
        if at < len(pairings):
            other = lax.ppermute(value, *pairings[at])
        if at < len(work):
            state = work[at](state)
        if at < len(pairings):
            value = value + other
    if cols & (cols - 1):
        value = lax.psum(value, "cols")
    return value, state


def swap_dates(value):
    return lax.ppermute(value, "dates", [(0, 1), (1, 0)])


def two_halves(complex_images, pair_list):
    dates, rows, _, cols = complex_images.shape
    me = lax.axis_index("dates")
    half = rows // LOOKR // 2
    row_total, col_total = half * 2, cols // LOOKC * lax.axis_size("cols")
    images = complex_images.reshape(dates, rows, 2, SPLIT, cols // SPLIT)
    images = images.transpose(0, 1, 3, 2, 4).reshape(dates, rows // LOOKR, 16, LANES)
    first, second = pair_list[:, 0], pair_list[:, 1]
    low, base = dates * me, (dates - GAP) * me
    first_own = (first >= low) & (first < low + dates)
    second_own = (second >= low) & (second < low + dates)
    inside = (first_own & second_own).astype(jnp.int32)
    across = (first_own ^ second_own).astype(jnp.int32)
    packed = (first - base) | ((second - base) << 10)
    packed = jnp.where(first_own | second_own, packed | (inside << 20) | (across << 21), 0)

    edge = lax.dynamic_slice(
        images, ((dates - GAP) * (1 - me), half * (1 - me), 0, 0), (GAP, half, 16, LANES)
    )
    edge, packed = lax.optimization_barrier((edge, packed))
    halo = swap_dates(edge)
    other, listed, counts = call_pairs(packed, images)
    other, halo = lax.optimization_barrier((other, halo))
    other = swap_dates(other)
    own, own_weights = call_pairs(packed, images, (halo, listed, counts))
    own, pair_rows = lax.optimization_barrier((own, pair_list.T))
    started = start_inverse(pair_rows, dates * 2)
    own, started = lax.optimization_barrier((own, started))
    high, lowpart, moments = call_combine(own, own_weights, other, dates, row_total, col_total)

    def go_on(state):
        values, progress = go_on_inverse(*state, last=False)
        return (values,) + state[1:3] + (progress,)

    def end(state):
        return go_on_inverse(*state, last=True), ()

    def solve(state):
        inverse, solved = state
        return inverse, solved + (call_solve(len(solved), inverse, (high, lowpart)),)

    moments, (inverse, series) = sum_beside(moments, started, [go_on, go_on, end, solve, solve])
    refined = call_refine(series, moments, inverse, dates * 2, row_total, col_total)
    return refined.reshape(dates * 2, half, 2, LANES)


highest = lax.Precision.HIGHEST


def pseudo_inverse(pair_list, count):
    date_ids = jnp.arange(count, dtype=jnp.int32)
    design = (pair_list[:, 0:1] == date_ids[None, :]).astype(jnp.float32) - (
        pair_list[:, 1:2] == date_ids[None, :]
    ).astype(jnp.float32)
    normal = jnp.dot(design.T, design, precision=highest) + RIDGE * jnp.eye(
        count, dtype=jnp.float32
    )
    factor = jnp.linalg.cholesky(normal)
    return jax.scipy.linalg.cho_solve((factor, True), design.T)


def pool_looks(plane):
    count, rows, cols = plane.shape
    rows_pooled = jnp.sum(plane.reshape(count, rows // LOOKR, LOOKR, cols), axis=2)
    return jnp.sum(rows_pooled.reshape(count, rows // LOOKR, cols // LOOKC, LOOKC), axis=3)


def multilook_pairs(tile_stack, pair_list, pair_block):
    real_planes = tile_stack[:, :, 0, :]
    imag_planes = tile_stack[:, :, 1, :]
    groups = pair_list.reshape(-1, pair_block, 2)
    scale = 1.0 / float(LOOKR * LOOKC)

    def one_group(group):
        first_real = jnp.take(real_planes, group[:, 0], axis=0).astype(jnp.float32)
        first_imag = jnp.take(imag_planes, group[:, 0], axis=0).astype(jnp.float32)
        second_real = jnp.take(real_planes, group[:, 1], axis=0).astype(jnp.float32)
        second_imag = jnp.take(imag_planes, group[:, 1], axis=0).astype(jnp.float32)
        real_part = pool_looks(first_real * second_real + first_imag * second_imag)
        imag_part = pool_looks(first_imag * second_real - first_real * second_imag)
        return (jnp.stack([real_part, imag_part], axis=2) * scale).astype(jnp.bfloat16)

    looked = lax.map(one_group, groups)
    return looked.reshape((pair_list.shape[0],) + looked.shape[2:])


def coordinates(start, count, total):
    return (2.0 * (start + jnp.arange(count, dtype=jnp.int32)).astype(jnp.float32) + 1.0) / float(
        total
    ) - 1.0


def basis_planes(row_coord, col_coord):
    constant = jnp.ones((row_coord.shape[0], col_coord.shape[0]), jnp.float32)
    return jnp.stack([constant, row_coord[:, None] * constant, col_coord[None, :] * constant])


def weighted(widened, planes, pair_count):
    weights = jnp.sum(widened * widened, axis=(0, 2)) / float(pair_count)
    weighted_planes = planes * weights[None]
    normal = jnp.einsum("jrc,krc->jk", weighted_planes, planes, precision=highest)
    return (weighted_planes, normal)


def inverse3(matrix):

    def cyclic(row_at, col_at):
        return (
            matrix[(row_at + 1) % 3, (col_at + 1) % 3] * matrix[(row_at + 2) % 3, (col_at + 2) % 3]
            - matrix[(row_at + 1) % 3, (col_at + 2) % 3]
            * matrix[(row_at + 2) % 3, (col_at + 1) % 3]
        )

    cofacts = jnp.stack(
        [jnp.stack([cyclic(row_at, col_at) for col_at in range(3)]) for row_at in range(3)]
    )
    determinant = jnp.sum(matrix[0] * cofacts[0])
    return cofacts.T / determinant


def refine(series, ramp_rhs, normal, planes):
    ramp_coef = jnp.einsum("jk,dkh->djh", inverse3(normal), ramp_rhs, precision=highest)
    return series - jnp.einsum("djh,jrc->drhc", ramp_coef, planes, precision=highest)


def any_dates(complex_images, pair_list):
    date_count = lax.axis_size("dates")
    date_index = lax.axis_index("dates")
    col_index = lax.axis_index("cols")
    pair_count = pair_list.shape[0]
    date_total = complex_images.shape[0] * date_count
    rounded_pseudo = pseudo_inverse(pair_list, date_total).astype(jnp.bfloat16)
    regrouped = lax.all_to_all(complex_images, "dates", split_axis=1, concat_axis=0, tiled=True)
    interferograms = multilook_pairs(regrouped, pair_list, PAIR_BLOCK * date_count)
    ml_rows = interferograms.shape[1]
    ml_cols = interferograms.shape[3]
    planes = basis_planes(
        coordinates(date_index * ml_rows, ml_rows, ml_rows * date_count),
        coordinates(col_index * ml_cols, ml_cols, ml_cols * lax.axis_size("cols")),
    )
    widened = interferograms.astype(jnp.float32)
    weighted_planes, normal_part = weighted(widened, planes, pair_count)
    flat_pairs = interferograms.reshape(pair_count, -1)
    series = jnp.dot(rounded_pseudo, flat_pairs, preferred_element_type=jnp.float32).reshape(
        (date_total,) + interferograms.shape[1:]
    )
    rhs_part = jnp.einsum("jrc,drhc->djh", weighted_planes, series, precision=highest)
    normal, ramp_rhs = lax.psum((normal_part, rhs_part), ("dates", "cols"))
    return refine(series, ramp_rhs, normal, planes)


def solution(mesh):
    def body(complex_images, pair_list):
        dates, rows, _, cols = complex_images.shape
        if mesh.shape["dates"] == 2 and cols == LANES * LOOKC and rows == 32 and dates >= GAP:
            return two_halves(complex_images, pair_list)
        return any_dates(complex_images, pair_list)

    return jax.shard_map(
        body,
        mesh=mesh,
        in_specs=(P("dates", None, None, "cols"), P()),
        out_specs=P(None, "dates", None, "cols"),
        check_vma=False,
    )
```
